32 devices in a mesh: dp: 4 (over z), fsdp: 2 (over y), tensor: 4 (over x, core).
Axes of the slice: x: 2, y: 2, z: 4, core: 2. Of those that a mesh axis runs over, the one named last changes fastest.
Arguments:
- activations: bfloat16 [9216, 1024], P(('dp', 'fsdp')), may hold values from -6 to 6
- cotangent: bfloat16 [9216, 1024], P(('dp', 'fsdp', 'tensor')), may hold values from -6 to 6
- lengths: int32 [40], P(('dp', 'fsdp')), may hold values from 32 to 512, as said below
- w_qkv: bfloat16 [2, 3, 1024, 1024], P(None, None, 'fsdp', 'tensor'), may hold values from -0.1875 to 0.1875
- w_out: bfloat16 [2, 1024, 1024], P(None, 'tensor', 'fsdp'), may hold values from -1.5 to 1.5
- w_up: bfloat16 [2, 1024, 4096], P(None, 'fsdp', 'tensor'), may hold values from -0.1875 to 0.1875
- w_down: bfloat16 [2, 4096, 1024], P(None, 'tensor', 'fsdp'), may hold values from -0.09375 to 0.09375
- b_qv: bfloat16 [2, 2, 16, 64], P(None, None, 'tensor', 'fsdp'), may hold values from -3 to 3
- b_up: bfloat16 [2, 32, 128], P(None, 'tensor', 'fsdp'), may hold values from -3 to 3
- norm_gains: bfloat16 [2, 2, 1024], P(None, None, 'fsdp'), may hold values from 0.099609375 to 1.8984375
- layer_biases: bfloat16 [2, 4, 1024], P(None, None, 'fsdp'), may hold values from -2 to 2
Outputs:
- layer_out: bfloat16 [9216, 1024], P(('dp', 'fsdp', 'tensor'))
- input_grad: float32 [9216, 1024], P(('dp', 'fsdp', 'tensor'))
- grad_qkv: float32 [2, 3, 1024, 1024], P(None, None, 'fsdp', 'tensor')
- grad_out: float32 [2, 1024, 1024], P(None, 'tensor', 'fsdp')
- grad_up: float32 [2, 1024, 4096], P(None, 'fsdp', 'tensor')
- grad_down: float32 [2, 4096, 1024], P(None, 'tensor', 'fsdp')
- grad_bias_qv: float32 [2, 2, 16, 64], P(None, None, 'tensor', 'fsdp')
- grad_bias_up: float32 [2, 32, 128], P(None, 'tensor', 'fsdp')
- grad_gains: float32 [2, 2, 1024], P(None, None, 'fsdp')
- grad_biases: float32 [2, 4, 1024], P(None, None, 'fsdp')
The draws below stay inside these ranges and needn't reach their ends.
Inputs may be any that keep to these rules, and one draw needn't show every extreme that they name: `lengths`: page i of a data group's 5 pages has 512 slots if i < 1, 256 if i < 2, else 128; it holds between a quarter of its slots and all of them; in each of the three buckets some page is full, and some page of the third bucket holds exactly a quarter of its slots.
All inputs are finite; a program needn't handle non-finite values.
Results may differ from the reference program's by a relative error of at most 0.028.
Values may be sent and summed in bfloat16 or wider, within the bound.
No kernel may reach another device: no remote copies, remote signals or barrier semaphores. Data moves between devices by JAX's collectives and lax.ppermute only.
A program may use at most 192 MiB of HBM per device.

```python
import jax
import jax.numpy as jnp
from jax import lax

D = 1024
HEADS = 16
HEAD = 64
FF = 4096
LAYERS = 2
LEN_A = 512
LEN_B = 256
LEN_C = 128
PAGES_A = 1
PAGES_B = 1
PAGES_C = 3
PAGES = 5
TOK_DEV = 1152
GROUPS = 8
TOKENS = 9216
FF_ROWS = 32


def draw_lengths(key, part):
    key = jax.random.fold_in(key, 11)
    total_pages = GROUPS * PAGES
    position = jnp.arange(total_pages, dtype=jnp.int32) % PAGES
    bucket_len = jnp.where(position < PAGES_A, LEN_A, jnp.where(position < PAGES_A + PAGES_B, LEN_B, LEN_C)).astype(jnp.int32)
    random_bits = jax.random.randint(jax.random.fold_in(key, 1), (total_pages,), 0, 1 << 20, dtype=jnp.int32)
    drawn = bucket_len // 4 + random_bits % (bucket_len - bucket_len // 4 + 1)
    chosen = jax.random.randint(jax.random.fold_in(key, 2), (3,), 0, GROUPS, dtype=jnp.int32)
    firsts = chosen * PAGES + jnp.array([0, PAGES_A, PAGES_A + PAGES_B], dtype=jnp.int32)
    page_ids = jnp.arange(total_pages, dtype=jnp.int32)
    forced_full = jnp.any(page_ids[:, None] == firsts[None, :], axis=1)
    short_page = (chosen[2] + 1) % GROUPS * PAGES + PAGES_A + PAGES_B
    forced_short = page_ids == short_page
    result = jnp.where(forced_full, bucket_len, drawn)
    result = jnp.where(forced_short, LEN_C // 4, result)
    return result.astype(jnp.int32)


def levels(key, dims, split, low, top_value):
    level, own = 1.0, jax.random.fold_in(key, 6)
    for axis_at, parts in split:
        draws = jnp.exp(jax.random.uniform(jax.random.fold_in(own, axis_at), (parts,), jnp.float32, low / len(split), top_value / len(split)))
        level = level * jnp.repeat(draws, dims[axis_at] // parts).reshape([-1 if axis == axis_at else 1 for axis in range(len(dims))])
    return level


def noise(own_key, dims, spread, bound, shards=(), held_as=jnp.bfloat16):
    gain = levels(own_key, dims, shards, -0.22, 0.18) if shards else 1.0
    values = jax.random.normal(own_key, dims, jnp.float32) * spread * gain
    return jnp.minimum(jnp.maximum(values, -bound), bound).astype(held_as)


def setup_inputs(seed: int = 0) -> dict:
    key_of = jax.random.split(jax.random.key(seed), 12)
    activations = noise(key_of[0], (TOKENS, D), 1.0, 6.0, ((0, 8),))
    cotangent = noise(key_of[1], (TOKENS, D), 1.0, 6.0, ((0, 32),))
    lengths = draw_lengths(jax.random.fold_in(key_of[11], 71), 0)
    w_qkv = noise(key_of[3], (LAYERS, 3, D, D), D ** -0.5, 0.1875, ((2, 2), (3, 4)))
    w_out = noise(key_of[4], (LAYERS, D, D), (D // 64) ** -0.5, 1.5, ((1, 4), (2, 2)))
    w_up = noise(key_of[5], (LAYERS, D, FF), D ** -0.5, 0.1875, ((1, 2), (2, 4)))
    w_down = noise(key_of[6], (LAYERS, FF, D), FF ** -0.5, 0.09375, ((1, 4), (2, 2)))
    b_qv = noise(key_of[7], (LAYERS, 2, HEADS, HEAD), 0.5, 3.0, ((2, 4), (3, 2)))
    b_up = noise(key_of[8], (LAYERS, FF_ROWS, 128), 0.5, 3.0, ((1, 4), (2, 2)))
    norm_gains = jnp.clip(1.0 + 0.18 * jax.random.normal(key_of[9], (LAYERS, 2, D), jnp.float32), 0.099609375, 1.8984375).astype(jnp.bfloat16)
    layer_biases = noise(key_of[10], (LAYERS, 4, D), 0.3, 2.0, ((2, 2),))
    return {"activations": activations, "cotangent": cotangent, "lengths": lengths, "w_qkv": w_qkv, "w_out": w_out, "w_up": w_up, "w_down": w_down, "b_qv": b_qv, "b_up": b_up, "norm_gains": norm_gains, "layer_biases": layer_biases}


@jax.custom_vjp
def low(v):
    return lax.optimization_barrier(v.astype(jnp.bfloat16)).astype(jnp.float32)

@jax.custom_vjp
def low_back(v):
    return v

def low_keep(v):
    return (low(v), None)

def low_pass(kept, grad):
    return (grad,)

def back_keep(v):
    return (v, None)

def back_low(kept, grad):
    return (low(grad),)
low.defvjp(low_keep, low_pass)
low_back.defvjp(back_keep, back_low)

def both_round(value):
    return low(low_back(value))

def matmul(left, right):
    return jnp.dot(left, right, precision=lax.Precision.HIGHEST, preferred_element_type=jnp.float32)

def layer_norm(hidden, gain_row, bias_row):
    center = hidden - lax.optimization_barrier(jnp.mean(hidden, -1, keepdims=True))
    variance = lax.optimization_barrier(jnp.mean(center * center, -1, keepdims=True))
    return center * lax.rsqrt(variance + 1e-05) * gain_row + bias_row

def attend(queries, keys_f, values_f, page_lengths, amount, length):
    head_shape = (amount, length, HEADS, HEAD)
    query_heads = queries.reshape(head_shape)
    key_heads = keys_f.reshape(head_shape)
    value_heads = values_f.reshape(head_shape)
    scores = jnp.einsum('plhe,pmhe->phlm', query_heads, key_heads, precision=lax.Precision.HIGHEST) * HEAD ** (-0.5)
    valid_keys = jnp.arange(length, dtype=jnp.int32)[None, None, None, :] < page_lengths[:, None, None, None]
    scores = low_back(jnp.where(valid_keys, scores, -1000000000.0))
    attn_probs = low(jax.nn.softmax(scores, axis=-1))
    context = jnp.einsum('phlm,pmhe->plhe', attn_probs, value_heads, precision=lax.Precision.HIGHEST)
    return context.reshape(amount * length, HEADS * HEAD)

def layer_forward(hidden_in, page_lengths, w_proj, w_mix, w_grow, w_shrink, bias_heads, bias_grow, gain_pair, bias_set):
    inputs_low = low(hidden_in)
    queries = both_round(matmul(inputs_low, w_proj[0]) + bias_heads[0].reshape(D))
    keys_f = both_round(matmul(inputs_low, w_proj[1]))
    values_f = both_round(matmul(inputs_low, w_proj[2]) + bias_heads[1].reshape(D))
    pieces = []
    row_at = 0
    page_at = 0
    for amount, length in ((PAGES_A, LEN_A), (PAGES_B, LEN_B), (PAGES_C, LEN_C)):
        span_rows = amount * length
        pieces.append(attend(queries[row_at:row_at + span_rows], keys_f[row_at:row_at + span_rows], values_f[row_at:row_at + span_rows], page_lengths[page_at:page_at + amount], amount, length))
        row_at += span_rows
        page_at += amount
    context = both_round(jnp.concatenate(pieces, 0))
    attn_sum = low_back(matmul(context, w_mix)) + bias_set[0]
    y_one = layer_norm(hidden_in + attn_sum, gain_pair[0], bias_set[2])
    upward = low_back(matmul(low(y_one), w_grow) + bias_grow.reshape(FF))
    activated = low(jax.nn.gelu(upward, approximate=False))
    down_sum = low_back(matmul(activated, w_shrink)) + bias_set[1]
    return layer_norm(y_one + down_sum, gain_pair[1], bias_set[3])

def group_forward(weights, hidden, page_lengths):
    for layer_index in range(LAYERS):
        hidden = layer_forward(hidden, page_lengths, *[w_all[layer_index] for w_all in weights])
    return hidden

def reference(activations, cotangent, lengths, w_qkv, w_out, w_up, w_down, b_qv, b_up, norm_gains, layer_biases):
    weights = tuple((w_all.astype(jnp.float32) for w_all in (w_qkv, w_out, w_up, w_down, b_qv, b_up, norm_gains, layer_biases)))
    inputs_f = activations.astype(jnp.float32).reshape(GROUPS, TOK_DEV, D)
    group_lengths = lengths.reshape(GROUPS, PAGES)
    group_step = jax.checkpoint(group_forward)

    def forward(inputs_all, weight_set):
        return lax.map(lambda pair: group_step(weight_set, pair[0], pair[1]), (inputs_all, group_lengths))
    outputs_f, pullback = jax.vjp(forward, inputs_f, weights)
    grad_inputs, grad_weights = pullback(cotangent.astype(jnp.float32).reshape(GROUPS, TOK_DEV, D))
    return (outputs_f.reshape(TOKENS, D).astype(jnp.bfloat16), grad_inputs.reshape(TOKENS, D), grad_weights[0], grad_weights[1], grad_weights[2], grad_weights[3], grad_weights[4], grad_weights[5], grad_weights[6], grad_weights[7])
```

```python
import jax
import jax.numpy as jnp
from jax import lax
from jax.sharding import PartitionSpec as P

HEAD = 64
LAYERS = 2
LEN_A = 512
LEN_B = 256
LEN_C = 128
PAGES_A = 1
PAGES_B = 1
PAGES_C = 3
BF = jnp.bfloat16
F32 = jnp.float32
CORE_SWAP = [(0, 1), (1, 0), (2, 3), (3, 2)]
CHIP_SWAP = [(0, 2), (2, 0), (1, 3), (3, 1)]


def to_core(value):
    return lax.ppermute(value, "tensor", CORE_SWAP)


def to_chip(value):
    return lax.ppermute(value, "tensor", CHIP_SWAP)


def from_fsdp(value, step):
    size = lax.axis_size("fsdp")
    return lax.ppermute(value, "fsdp", [((i + step) % size, i) for i in range(size)])


def to_fsdp(value, step):
    size = lax.axis_size("fsdp")
    return lax.ppermute(value, "fsdp", [(i, (i + step) % size) for i in range(size)])


def gather_own_first(shard, axis):
    size = lax.axis_size("fsdp")
    return jnp.concatenate([shard] + [from_fsdp(shard, step) for step in range(1, size)], axis)


def own_first(whole, axis):
    size = lax.axis_size("fsdp")
    here = lax.axis_index("fsdp")
    width = whole.shape[axis] // size
    return jnp.concatenate(
        [lax.dynamic_slice_in_dim(whole, (here + k) % size * width, width, axis) for k in range(size)], axis
    )


def natural(relative, axis):
    size = lax.axis_size("fsdp")
    here = lax.axis_index("fsdp")
    width = relative.shape[axis] // size
    return jnp.concatenate(
        [
            lax.dynamic_slice_in_dim(relative, (k - here + size) % size * width, width, axis)
            for k in range(size)
        ],
        axis,
    )


def swap_slots(rows):
    here = lax.axis_index("tensor")
    share = rows.shape[0] // 4
    return jnp.concatenate(
        [lax.dynamic_slice_in_dim(rows, (here ^ k) * share, share, 0) for k in range(4)], 0
    )


def layer_norm(hidden, gain_row, bias_row):
    center = hidden - jnp.mean(hidden, -1, keepdims=True)
    inverse = lax.rsqrt(jnp.mean(center * center, -1, keepdims=True) + 1e-05)
    normed = center * inverse
    return (normed * gain_row + bias_row, normed, inverse)


def norm_back(grad_result, normed, inverse, gain_row):
    grad_norm = grad_result * gain_row
    mean_one = jnp.mean(grad_norm, -1, keepdims=True)
    mean_two = jnp.mean(grad_norm * normed, -1, keepdims=True)
    grad_in = inverse * (grad_norm - mean_one - normed * mean_two)
    return (grad_in, jnp.sum(grad_result * normed, 0), jnp.sum(grad_result, 0))


def gelu_parts(upward):
    cdf_val = 0.5 * (1.0 + lax.erf(upward * 0.7071067811865476))
    density = jnp.exp(-0.5 * upward * upward) * 0.3989422804014327
    return (upward * cdf_val, cdf_val + upward * density)


def dot(left, right):
    return jnp.dot(left, right, preferred_element_type=F32)


def dot_t(left, right):
    return lax.dot_general(left, right, (((1,), (1,)), ((), ())), preferred_element_type=F32)


def dot_rows(left, right):
    return lax.dot_general(left, right, (((0,), (0,)), ((), ())), preferred_element_type=F32)


def gather_rows(share):
    across = to_chip(share)
    return (
        jnp.concatenate([share, to_core(share)], 0),
        jnp.concatenate([across, to_core(across)], 0),
    )


def reduce_rows(part_here, part_there):
    there = part_there()
    share = there.shape[0] // 2
    from_core = to_core(there[share:].astype(BF))
    from_chip = to_chip((there[:share] + from_core.astype(F32)).astype(BF))
    here = part_here()
    own = to_core(here[share:].astype(BF))
    return here[:share] + own.astype(F32) + from_chip.astype(F32)


def bucket_scores(query_heads, key_heads, page_lengths, length):
    scores = jnp.einsum(
        "plhe,pmhe->phlm", query_heads, key_heads, preferred_element_type=jnp.float32
    ) * HEAD ** (-0.5)
    valid_keys = (
        jnp.arange(length, dtype=jnp.int32)[None, None, None, :] < page_lengths[:, None, None, None]
    )
    return jnp.where(valid_keys, scores, -1000000000.0)


def attention_forward(queries, keys_b, values_b, page_lengths):
    heads_here = queries.shape[1] // HEAD
    outputs = []
    log_totals = []
    row_at = 0
    page_at = 0
    for amount, length in ((PAGES_A, LEN_A), (PAGES_B, LEN_B), (PAGES_C, LEN_C)):
        span_rows = amount * length
        head_shape = (amount, length, heads_here, HEAD)
        query_heads = queries[row_at : row_at + span_rows].reshape(head_shape)
        key_heads = keys_b[row_at : row_at + span_rows].reshape(head_shape)
        value_heads = values_b[row_at : row_at + span_rows].reshape(head_shape)
        scores = bucket_scores(
            query_heads, key_heads, page_lengths[page_at : page_at + amount], length
        )
        row_peak = jnp.max(scores, -1, keepdims=True)
        exponent = jnp.exp(scores - row_peak)
        row_total = jnp.sum(exponent, -1, keepdims=True)
        attn_low = (exponent / row_total).astype(jnp.bfloat16)
        context = jnp.einsum(
            "phlm,pmhe->plhe", attn_low, value_heads, preferred_element_type=jnp.float32
        )
        outputs.append(context.reshape(span_rows, heads_here * HEAD))
        log_totals.append(row_peak + jnp.log(row_total))
        row_at += span_rows
        page_at += amount
    return (jnp.concatenate(outputs, 0).astype(jnp.bfloat16), log_totals)


def attention_backward(queries, keys_b, values_b, page_lengths, log_totals, grad_context):
    heads_here = queries.shape[1] // HEAD
    grad_q_list = []
    grad_k_list = []
    grad_v_list = []
    row_at = 0
    page_at = 0
    bucket_index = 0
    for amount, length in ((PAGES_A, LEN_A), (PAGES_B, LEN_B), (PAGES_C, LEN_C)):
        span_rows = amount * length
        head_shape = (amount, length, heads_here, HEAD)
        query_heads = queries[row_at : row_at + span_rows].reshape(head_shape)
        key_heads = keys_b[row_at : row_at + span_rows].reshape(head_shape)
        value_heads = values_b[row_at : row_at + span_rows].reshape(head_shape)
        grad_heads = grad_context[row_at : row_at + span_rows].reshape(head_shape)
        scores = bucket_scores(
            query_heads, key_heads, page_lengths[page_at : page_at + amount], length
        )
        attn_probs = jnp.exp(scores - log_totals[bucket_index])
        attn_low = attn_probs.astype(jnp.bfloat16)
        grad_values = jnp.einsum(
            "phlm,plhe->pmhe", attn_low, grad_heads, preferred_element_type=jnp.float32
        )
        grad_probs = jnp.einsum(
            "plhe,pmhe->phlm", grad_heads, value_heads, preferred_element_type=jnp.float32
        )
        grad_scores = (
            attn_probs * (grad_probs - jnp.sum(attn_probs * grad_probs, -1, keepdims=True))
        ).astype(jnp.bfloat16)
        grad_queries = jnp.einsum(
            "phlm,pmhe->plhe", grad_scores, key_heads, preferred_element_type=jnp.float32
        ) * HEAD ** (-0.5)
        grad_keys = jnp.einsum(
            "phlm,plhe->pmhe", grad_scores, query_heads, preferred_element_type=jnp.float32
        ) * HEAD ** (-0.5)
        grad_q_list.append(grad_queries.reshape(span_rows, heads_here * HEAD))
        grad_k_list.append(grad_keys.reshape(span_rows, heads_here * HEAD))
        grad_v_list.append(grad_values.reshape(span_rows, heads_here * HEAD))
        row_at += span_rows
        page_at += amount
        bucket_index += 1
    return (
        jnp.concatenate(grad_q_list, 0).astype(jnp.bfloat16),
        jnp.concatenate(grad_k_list, 0).astype(jnp.bfloat16),
        jnp.concatenate(grad_v_list, 0).astype(jnp.bfloat16),
    )


def halves(rows):
    half = rows.shape[0] // 2
    return rows[:half], rows[half:]


def layer_forward(weights, small, inputs, inputs_share, page_lengths):
    w_proj, w_mix, w_grow, w_shrink = weights
    bias_q, bias_v, bias_grow, gains, biases = small
    inputs_here, inputs_there = inputs
    half = inputs_here.shape[0]
    width = w_proj.shape[2]

    def project(rows):
        queries = (dot(rows, w_proj[0]) + bias_q).astype(BF)
        keys_b = dot(rows, w_proj[1]).astype(BF)
        values_b = (dot(rows, w_proj[2]) + bias_v).astype(BF)
        return jnp.concatenate([queries, keys_b, values_b], 1)

    qkv = swap_slots(jnp.concatenate([project(inputs_here), project(inputs_there)], 0))
    queries, keys_b, values_b = qkv[:, :width], qkv[:, width : 2 * width], qkv[:, 2 * width :]
    context, log_totals = attention_forward(queries, keys_b, values_b, page_lengths)
    context_own = swap_slots(context)
    attn_share = reduce_rows(
        lambda: dot(context_own[:half], w_mix), lambda: dot(context_own[half:], w_mix)
    )
    y_one, normed_one, inverse_one = layer_norm(
        inputs_share + attn_share + biases[0], gains[0], biases[2]
    )
    middle = gather_rows(y_one.astype(BF))

    def grow(rows):
        activated, slope = gelu_parts(dot(rows, w_grow) + bias_grow)
        return activated.astype(BF), slope

    act_here, slope_here = grow(middle[0])
    act_there, slope_there = grow(middle[1])
    down_share = reduce_rows(lambda: dot(act_here, w_shrink), lambda: dot(act_there, w_shrink))
    result, normed_two, inverse_two = layer_norm(
        y_one + down_share + biases[1], gains[1], biases[3]
    )
    kept = (
        inputs,
        (queries, keys_b, values_b),
        log_totals,
        context_own,
        normed_one,
        inverse_one,
        middle,
        (slope_here, slope_there),
        (act_here, act_there),
        normed_two,
        inverse_two,
    )
    return result, kept


def layer_backward(weights, small, kept, grad_result, page_lengths):
    w_proj, w_mix, w_grow, w_shrink = weights
    bias_q, bias_v, bias_grow, gains, biases = small
    (
        inputs,
        qkv,
        log_totals,
        context_own,
        normed_one,
        inverse_one,
        middle,
        slopes,
        acts,
        normed_two,
        inverse_two,
    ) = kept
    half = inputs[0].shape[0]
    grad_two, grad_gain_two, grad_bias_two = norm_back(grad_result, normed_two, inverse_two, gains[1])
    grad_down_bias = jnp.sum(grad_two, 0)
    grad_down = gather_rows(grad_two.astype(BF))
    grad_up = [
        (dot_t(grad_down[i], w_shrink) * slopes[i]).astype(BF) for i in range(2)
    ]
    grad_middle = reduce_rows(lambda: dot_t(grad_up[0], w_grow), lambda: dot_t(grad_up[1], w_grow))
    grad_down_all = jnp.concatenate(grad_down, 0)
    grad_up_all = jnp.concatenate(grad_up, 0)
    grad_shrink = dot_rows(jnp.concatenate(acts, 0), grad_down_all).astype(BF)
    grad_grow = dot_rows(jnp.concatenate(middle, 0), grad_up_all).astype(BF)
    grad_grow_bias = jnp.sum(grad_up_all, 0, dtype=F32)
    grad_one, grad_gain_one, grad_bias_one = norm_back(
        grad_middle + grad_two, normed_one, inverse_one, gains[0]
    )
    grad_mix_bias = jnp.sum(grad_one, 0)
    grad_mix_rows = gather_rows(grad_one.astype(BF))
    grad_context = swap_slots(
        jnp.concatenate([dot_t(grad_mix_rows[i], w_mix).astype(BF) for i in range(2)], 0)
    )
    grad_mix = dot_rows(context_own, jnp.concatenate(grad_mix_rows, 0)).astype(BF)
    grads = attention_backward(*qkv, page_lengths, log_totals, grad_context)
    grad_qkv = swap_slots(jnp.concatenate(grads, 1))
    w_flat = jnp.concatenate([w_proj[0], w_proj[1], w_proj[2]], 1)
    grad_input = (
        reduce_rows(lambda: dot_t(grad_qkv[:half], w_flat), lambda: dot_t(grad_qkv[half:], w_flat))
        + grad_one
    )
    inputs_all = jnp.concatenate(inputs, 0)
    grad_proj = jnp.stack([dot_rows(inputs_all, g) for g in jnp.split(grad_qkv, 3, 1)]).astype(BF)
    column_sums = jnp.sum(grad_qkv, 0, dtype=F32)
    width = w_mix.shape[0]
    grad_heads_bias = jnp.stack([column_sums[:width], column_sums[2 * width :]])
    grad_gain_pair = jnp.stack([grad_gain_one, grad_gain_two])
    grad_bias_set = jnp.stack([grad_mix_bias, grad_down_bias, grad_bias_one, grad_bias_two])
    return grad_input, (
        (grad_proj, grad_mix, grad_grow, grad_shrink),
        (grad_heads_bias, grad_grow_bias, grad_gain_pair, grad_bias_set),
    )


def sum_line(value):
    size = lax.axis_size("dp")
    here = lax.axis_index("dp")
    middle = size // 2
    for step in range(middle - 1):
        came = lax.ppermute(value, "dp", [(step, step + 1), (size - 1 - step, size - 2 - step)])
        value = (value.astype(F32) + came.astype(F32)).astype(BF)
    came = lax.ppermute(value, "dp", [(middle - 1, middle), (middle, middle - 1)])
    value = (value.astype(F32) + came.astype(F32)).astype(BF)
    for step in reversed(range(middle - 1)):
        came = lax.ppermute(value, "dp", [(step + 1, step), (size - 2 - step, size - 1 - step)])
        takes = (here == step) | (here == size - 1 - step)
        value = jnp.where(takes, came, value)
    return value


def sum_weight(grad, axis):
    size = lax.axis_size("fsdp")
    width = grad.shape[axis] // size
    total = lax.slice_in_dim(grad, 0, width, axis=axis).astype(F32)
    for step in range(1, size):
        piece = lax.slice_in_dim(grad, step * width, (step + 1) * width, axis=axis)
        total = total + to_fsdp(piece, step).astype(F32)
    return sum_line(total.astype(BF)).astype(F32)


def per_device(
    activations, cotangent, lengths, w_qkv, w_out, w_up, w_down, b_qv, b_up, norm_gains, layer_biases
):
    fsdp_size = lax.axis_size("fsdp")
    fsdp_here = lax.axis_index("fsdp")
    share_rows = activations.shape[0] // lax.axis_size("tensor")
    half = 2 * share_rows

    smalls = (b_qv, b_up, norm_gains, layer_biases)
    flat = jnp.concatenate([value.reshape(-1) for value in smalls])
    pieces = [flat] + [from_fsdp(flat, step) for step in range(1, fsdp_size)]

    def unpack(at):
        found, start = [], 0
        for value in smalls:
            found.append(pieces[at][start : start + value.size].reshape(value.shape))
            start += value.size
        return found

    unpacked = [unpack(at) for at in range(fsdp_size)]
    bias_heads, bias_grow, gains, biases = (
        jnp.concatenate([u[i] for u in unpacked], -1).astype(F32) for i in range(4)
    )
    bias_heads, bias_grow = natural(bias_heads, 3), natural(bias_grow, 2)

    inputs_all = own_first(swap_slots(activations), 1)
    inputs = (inputs_all[:half], inputs_all[half:])
    inputs_share = inputs_all[:share_rows].astype(F32)
    grad_share = own_first(cotangent, 1).astype(F32)

    fetched, small_all, kept_all = [], [], []
    for layer in range(LAYERS):
        weights = (
            gather_own_first(w_qkv[layer], 1),
            gather_own_first(w_out[layer], 1),
            gather_own_first(w_up[layer], 0),
            gather_own_first(w_down[layer], 1),
        )
        small = (
            bias_heads[layer, 0].reshape(-1),
            bias_heads[layer, 1].reshape(-1),
            bias_grow[layer].reshape(-1),
            gains[layer],
            biases[layer],
        )
        result, kept = layer_forward(weights, small, inputs, inputs_share, lengths)
        fetched.append(weights)
        small_all.append(small)
        kept_all.append(kept)
        inputs_share = result
        if layer + 1 < LAYERS:
            inputs = gather_rows(result.astype(BF))
    layer_out = natural(inputs_share.astype(BF), 1)
    big, little = [None] * LAYERS, [None] * LAYERS
    for layer in reversed(range(LAYERS)):
        grad_share, (grads, little[layer]) = layer_backward(
            fetched[layer], small_all[layer], kept_all[layer], grad_share, lengths
        )
        big[layer] = [sum_weight(grad, axis) for grad, axis in zip(grads, (1, 1, 0, 1))]
    stacked = [jnp.stack([big[layer][i] for layer in range(LAYERS)]) for i in range(4)]

    heads_bias = jnp.stack([little[layer][0] for layer in range(LAYERS)]).reshape(bias_heads.shape)
    grow_bias = jnp.stack([little[layer][1] for layer in range(LAYERS)]).reshape(bias_grow.shape)
    gain_pair = jnp.stack([little[layer][2] for layer in range(LAYERS)])
    bias_set = jnp.stack([little[layer][3] for layer in range(LAYERS)])
    norms = jnp.concatenate([gain_pair.reshape(-1, gain_pair.shape[-1]), bias_set.reshape(-1, bias_set.shape[-1])])
    norms = norms + to_core(norms)
    norms = norms + to_chip(norms)
    own_heads, own_grow = own_first(heads_bias, 3), own_first(grow_bias, 2)
    little_all = []
    for step in range(fsdp_size):
        parts = []
        for value in (own_heads, own_grow, norms):
            width = value.shape[-1] // fsdp_size
            parts.append(value[..., step * width : (step + 1) * width].reshape(-1))
        little_all.append(jnp.concatenate(parts))
    total = little_all[0]
    for step in range(1, fsdp_size):
        total = total + to_fsdp(little_all[step], step)
    total = lax.psum(total, "dp")
    count = [v.size // fsdp_size for v in (own_heads, own_grow, gain_pair, bias_set)]
    shapes = [v.shape[:-1] + (v.shape[-1] // fsdp_size,) for v in (own_heads, own_grow, gain_pair, bias_set)]
    finals, start = [], 0
    for amount, shape in zip(count, shapes):
        finals.append(total[start : start + amount].reshape(shape))
        start += amount
    return (layer_out, natural(grad_share, 1), *stacked, *finals)


def solution(mesh):
    in_specs = (
        P(("dp", "fsdp"), None),
        P(("dp", "fsdp", "tensor"), None),
        P(("dp", "fsdp")),
        P(None, None, "fsdp", "tensor"),
        P(None, "tensor", "fsdp"),
        P(None, "fsdp", "tensor"),
        P(None, "tensor", "fsdp"),
        P(None, None, "tensor", "fsdp"),
        P(None, "tensor", "fsdp"),
        P(None, None, "fsdp"),
        P(None, None, "fsdp"),
    )
    out_specs = (
        P(("dp", "fsdp", "tensor"), None),
        P(("dp", "fsdp", "tensor"), None),
        P(None, None, "fsdp", "tensor"),
        P(None, "tensor", "fsdp"),
        P(None, "fsdp", "tensor"),
        P(None, "tensor", "fsdp"),
        P(None, None, "tensor", "fsdp"),
        P(None, "tensor", "fsdp"),
        P(None, None, "fsdp"),
        P(None, None, "fsdp"),
    )
    return jax.shard_map(
        per_device, mesh=mesh, in_specs=in_specs, out_specs=out_specs, check_vma=False
    )
```

```python
import functools

import jax
import jax.numpy as jnp
from jax import lax
from jax.experimental import pallas as pl
from jax.experimental.pallas import tpu as pltpu
from jax.sharding import PartitionSpec as P

HEAD = 64
PAIR = 2 * HEAD
LAYERS = 2
LENGTHS = (512, 256, 128, 128, 128)
STARTS = (0, 512, 768, 896, 1024)
STREAMS = ((0,), (1, 2, 3, 4))
HALVES = 2
BF = jnp.bfloat16
F32 = jnp.float32
MIB = 1 << 20
CORE_SWAP = [(0, 1), (1, 0), (2, 3), (3, 2)]
CHIP_SWAP = [(0, 2), (2, 0), (1, 3), (3, 1)]


def to_core(value):
    return lax.ppermute(value, "tensor", CORE_SWAP)


def to_chip(value):
    return lax.ppermute(value, "tensor", CHIP_SWAP)


def from_fsdp(value, step):
    size = lax.axis_size("fsdp")
    return lax.ppermute(value, "fsdp", [((i + step) % size, i) for i in range(size)])


def to_fsdp(value, step):
    size = lax.axis_size("fsdp")
    return lax.ppermute(value, "fsdp", [(i, (i + step) % size) for i in range(size)])


def own_first(whole, axis):
    size = lax.axis_size("fsdp")
    here = lax.axis_index("fsdp")
    width = whole.shape[axis] // size
    return jnp.concatenate(
        [lax.dynamic_slice_in_dim(whole, (here + k) % size * width, width, axis) for k in range(size)], axis
    )


def natural(relative, axis):
    size = lax.axis_size("fsdp")
    here = lax.axis_index("fsdp")
    width = relative.shape[axis] // size
    return jnp.concatenate(
        [
            lax.dynamic_slice_in_dim(relative, (k - here + size) % size * width, width, axis)
            for k in range(size)
        ],
        axis,
    )


def dot(left, right):
    return jnp.dot(left, right, preferred_element_type=F32)


def dot_t(left, right):
    return lax.dot_general(left, right, (((1,), (1,)), ((), ())), preferred_element_type=F32)


def dot_rows(left, right):
    return lax.dot_general(left, right, (((0,), (0,)), ((), ())), preferred_element_type=F32)


def share_rows(stream):
    return sum(LENGTHS[page] for page in stream) // HALVES


def page_places(stream):
    places, at = [], 0
    for page in stream:
        places.append((page, LENGTHS[page], at, at // HALVES))
        at += LENGTHS[page]
    return places


class Order:
    def __init__(self):
        self.last = None
        self.pins = []

    def pin(self, arrays):
        self.pins.extend(arrays)

    def hold(self):
        def body(out):
            out[...] = jnp.zeros(out.shape, F32)

        self.call(body, [], [shape_of((8, 128), F32)], name="hold")

    def call(
        self, body, inputs, outputs, scratch=(), grid=(), in_specs=None, out_specs=None, name=None, limit=16, alias=None
    ):
        pins, self.pins = self.pins, []
        count = len(inputs)
        in_specs = in_specs or [None] * count
        out_specs = out_specs or [None] * len(outputs)
        in_specs = [whole_of(v.shape, grid) if s is None else s for s, v in zip(in_specs, inputs)]
        out_specs = [whole_of(v.shape, grid) if s is None else s for s, v in zip(out_specs, outputs)]
        inputs = list(inputs)
        unread = pins + ([] if self.last is None else [self.last])
        extra = len(unread)
        inputs += unread
        in_specs += [pl.BlockSpec(memory_space=pl.ANY)] * extra

        def kernel(*refs):
            body(*refs[:count], *refs[count + extra :])

        result = pl.pallas_call(
            kernel,
            grid=grid,
            in_specs=in_specs,
            out_specs=out_specs,
            out_shape=outputs,
            scratch_shapes=list(scratch),
            input_output_aliases=alias or {},
            name=name,
            cost_estimate=pl.CostEstimate(flops=0, bytes_accessed=0, transcendentals=0),
            compiler_params=pltpu.CompilerParams(vmem_limit_bytes=limit * MIB),
        )(*inputs)
        self.last = result[0]
        return result


def whole_of(shape, grid):
    if not grid:
        return pl.BlockSpec(memory_space=pltpu.VMEM)
    return pl.BlockSpec(shape, lambda *at: (0,) * len(shape))


def shape_of(shape, dtype):
    return jax.ShapeDtypeStruct(tuple(shape), dtype)


SMEM = pl.BlockSpec(memory_space=pltpu.SMEM)
ANY = pl.BlockSpec(memory_space=pl.ANY)


def core_index():
    return lax.rem(lax.axis_index("tensor"), 2)


class Weight:
    def __init__(self, arrays, axis):
        self.arrays = arrays
        self.axis = axis
        self.widths = [v.shape[axis] for v in arrays]
        self.starts = [sum(self.widths[:i]) for i in range(len(arrays))]
        self.shape = arrays[0].shape

    def specs(self, block=None):
        if block is None:
            return [None] * len(self.arrays)
        found = []
        for v in self.arrays:
            shape = [block, block]
            shape[self.axis] = v.shape[self.axis]
            found.append(pl.BlockSpec(tuple(shape), (lambda i: (0, i)) if self.axis == 0 else (lambda i: (i, 0))))
        return found

    def take(self, refs):
        count = len(self.arrays)
        places = [slice(a, a + w) for a, w in zip(self.starts, self.widths)]
        return list(zip(refs[:count], places)), refs[count:]


def deal_rows(order, activations):
    features = activations.shape[1]
    size = lax.axis_size("fsdp")
    width = features // size

    def body(whole, *outs):
        here = core_index()
        mine = lax.axis_index("fsdp")
        for at, stream in enumerate(STREAMS):
            for slot in range(HALVES):
                out = outs[at * HALVES + slot]
                for page, length, _, offset in page_places(stream):
                    part = length // HALVES
                    row = pl.multiple_of(STARTS[page] + (here ^ slot) * part, 32)
                    for k in range(size):
                        column = pl.multiple_of(lax.rem(mine + k, size) * width, 128)
                        out[offset : offset + part, k * width : (k + 1) * width] = whole[
                            pl.ds(row, part), pl.ds(column, width)
                        ]

    outs = order.call(
        body,
        [activations],
        [shape_of((share_rows(stream), features), BF) for stream in STREAMS for _ in range(HALVES)],
        name="deal_rows",
    )
    return [outs[at * HALVES : (at + 1) * HALVES] for at in range(len(STREAMS))]


def deal_share(order, slots):
    rows, features = slots[0].shape
    size = lax.axis_size("fsdp")
    width = features // size

    def body(a, b, c, d, *outs):
        whole = outs[-1]
        here = lax.axis_index("tensor")
        core = core_index()
        mine = lax.axis_index("fsdp")
        for slot, ref in enumerate((a, b, c, d)):
            whole[pl.ds(pl.multiple_of((here ^ slot) * rows, 32), rows), :] = ref[...]
        for at, stream in enumerate(STREAMS):
            for page, length, _, offset in page_places(stream):
                part = length // HALVES
                row = pl.multiple_of(STARTS[page] + core * part, 32)
                for k in range(size):
                    column = pl.multiple_of(lax.rem(mine + k, size) * width, 128)
                    outs[at][offset : offset + part, k * width : (k + 1) * width] = whole[
                        pl.ds(row, part), pl.ds(column, width)
                    ]

    return order.call(
        body,
        slots,
        [shape_of((share_rows(stream), features), BF) for stream in STREAMS],
        scratch=[pltpu.VMEM((rows * 4, features), BF)],
        name="deal_share",
    )


def natural_share(order, slots, dtype):
    rows, features = slots[0].shape
    share = rows // 2
    size = lax.axis_size("fsdp")
    width = features // size

    def body(a, b, out, whole):
        here = lax.axis_index("tensor")
        core = core_index()
        mine = lax.axis_index("fsdp")
        for slot, ref in enumerate((a, b)):
            first = 0
            for stream in STREAMS:
                for page, length, _, offset in page_places(stream):
                    part = length // HALVES
                    row = pl.multiple_of(STARTS[page] + (core ^ slot) * part, 32)
                    whole[pl.ds(row, part), :] = ref[first + offset : first + offset + part, :]
                first += share_rows(stream)
        own = pl.multiple_of(here * share, 32)
        for k in range(size):
            column = pl.multiple_of(lax.rem(mine + k, size) * width, 128)
            out[:, pl.ds(column, width)] = whole[pl.ds(own, share), k * width : (k + 1) * width].astype(dtype)

    return order.call(
        body,
        slots,
        [shape_of((share, features), dtype)],
        scratch=[pltpu.VMEM((rows * 2, features), BF)],
        name="natural_share",
    )[0]


def add_send(order, kept, came):
    half = kept.shape[0] // 2

    def body(a, b, c, low, wide):
        for at, came_ref in ((0, b), (half, c)):
            total = a[at : at + half, :] + came_ref[...].astype(F32)
            wide[at : at + half, :] = total
            low[at : at + half, :] = total.astype(BF)

    return order.call(body, [kept, *came], [shape_of(kept.shape, BF), shape_of(kept.shape, F32)], name="add_send")


def row_of(ref, at):
    return ref[at : at + 1, :]


def norm_forward(order, terms, residual, vectors, rows_of_vectors):
    rows, features = terms[0].shape
    bias_at, gain_at, shift_at = rows_of_vectors

    def body(a, b, before, vec, low, normed, inverse):
        value = before[...].astype(F32)
        if residual[1] is not None:
            value = value * row_of(vec, residual[1]) + row_of(vec, residual[2])
        value = value + a[...] + b[...].astype(F32) + row_of(vec, bias_at)
        center = value - jnp.mean(value, -1, keepdims=True)
        scale = lax.rsqrt(jnp.mean(center * center, -1, keepdims=True) + 1e-05)
        unit = center * scale
        normed[...] = unit
        inverse[...] = scale
        low[...] = (unit * row_of(vec, gain_at) + row_of(vec, shift_at)).astype(BF)

    return order.call(
        body,
        [*terms, residual[0], vectors],
        [shape_of((rows, features), BF), shape_of((rows, features), F32), shape_of((rows, 1), F32)],
        name="norm_forward",
    )


def norm_backward(order, terms, normed, inverse, vectors, gain_at):
    rows, features = normed.shape
    count = len(terms)

    def body(*refs):
        unit, scale, vec, low, sums, wide = refs[count:]
        total = refs[0][...].astype(F32)
        for ref in refs[1:count]:
            total = total + ref[...].astype(F32)
        n = unit[...]
        grad = total * row_of(vec, gain_at)
        mean_one = jnp.mean(grad, -1, keepdims=True)
        mean_two = jnp.mean(grad * n, -1, keepdims=True)
        result = scale[...] * (grad - mean_one - n * mean_two)
        wide[...] = result
        low[...] = result.astype(BF)
        sums[0:1, :] = jnp.sum(total * n, 0, keepdims=True)
        sums[1:2, :] = jnp.sum(total, 0, keepdims=True)
        sums[2:3, :] = jnp.sum(result, 0, keepdims=True)

    return order.call(
        body,
        [*terms, normed, inverse, vectors],
        [shape_of((rows, features), BF), shape_of((3, features), F32), shape_of((rows, features), F32)],
        name="norm_backward",
    )


def last_sum(order, terms):
    def body(*refs):
        total = refs[0][...]
        for ref in refs[1:-1]:
            total = total + ref[...].astype(F32)
        refs[-1][...] = total.astype(BF)

    return order.call(body, terms, [shape_of(terms[0].shape, BF)], name="last_sum")[0]


def head_mask(which):
    lane = lax.broadcasted_iota(jnp.int32, (1, PAIR), 1)
    return (lane < HEAD) if which == 0 else (lane >= HEAD)


def key_bias(length, limit):
    part = length // HALVES
    place = lax.broadcasted_iota(jnp.int32, (1, length), 1)
    half = (place // part) ^ core_index()
    return jnp.where(half * part + place % part < limit, 0.0, -1000000000.0).astype(F32)


def put_rows(ref, lanes, value, row, part, share, offset):
    done = 0
    while done < value.shape[0]:
        at = row + done
        count = min(part - at % part, value.shape[0] - done)
        first = (at // part) * share + offset + at % part
        ref[first : first + count, lanes] = value[done : done + count]
        done += count


def attention_forward(order, stream, slots, weights, lengths):
    w_proj, w_mix, bias_rows = weights
    share, features = slots[0].shape
    span = w_mix.shape[0]
    heads = span // HEAD
    places = page_places(stream)

    def body(*refs):
        xs, refs = refs[:HALVES], refs[HALVES:]
        wp, refs = w_proj.take(refs)
        wm, refs = w_mix.take(refs)
        bias, limits, refs = refs[0], refs[1], refs[2:]
        others, part_own, qkv, ctx, probs = refs[:2], refs[2], refs[3], refs[4], refs[5:]
        for kind in range(3):
            value = None
            for w, at in wp:
                rows = jnp.concatenate([x[:, at] for x in xs], 0)
                term = dot(rows, w[kind])
                value = term if value is None else value + term
            if kind == 0:
                value = value + bias[0:1, :]
            elif kind == 2:
                value = value + bias[1:2, :]
            value = value.astype(BF)
            if kind == 0:
                value = value * jnp.asarray(HEAD ** (-0.5), BF)
            for _, length, base, offset in places:
                part = length // HALVES
                for slot in range(HALVES):
                    qkv[base + slot * part : base + (slot + 1) * part, kind * span : (kind + 1) * span] = value[
                        slot * share + offset : slot * share + offset + part, :
                    ]
        for index, (page, length, base, offset) in enumerate(places):
            part = length // HALVES
            shut = key_bias(length, limits[page])
            step = min(length, 256)
            for pair in range(heads // 2):
                lanes = slice(pair * PAIR, (pair + 1) * PAIR)
                keys = qkv[base : base + length, span + pair * PAIR : span + (pair + 1) * PAIR]
                values = qkv[base : base + length, 2 * span + pair * PAIR : 2 * span + (pair + 1) * PAIR]
                for row in range(0, length, step):
                    queries = qkv[base + row : base + row + step, lanes]
                    found = []
                    for which in range(2):
                        masked = queries * head_mask(which).astype(BF)
                        scores = dot_t(masked, keys) + shut
                        peak = jnp.max(scores, -1, keepdims=True)
                        raised = jnp.exp(scores - peak)
                        chance = raised * (1.0 / jnp.sum(raised, -1, keepdims=True))
                        chance = chance.astype(BF)
                        probs[index][2 * pair + which, row : row + step, :] = chance
                        found.append(dot(chance, values))
                    both = jnp.where(head_mask(0), found[0], found[1]).astype(BF)
                    put_rows(ctx, lanes, both, row, part, share, offset)
        for w, at in wm:
            value = dot(ctx[...], w[...])
            part_own[:, at] = value[:share]
            split_rows(others, at, value[share:])

    outs = order.call(
        body,
        [*slots, *w_proj.arrays, *w_mix.arrays, bias_rows, lengths],
        [
            *[shape_of((share // 2, features), BF)] * 2,
            shape_of((share, features), F32),
            shape_of((2 * share, 3 * span), BF),
            shape_of((2 * share, span), BF),
        ]
        + [shape_of((heads, length, length), BF) for _, length, _, _ in places],
        in_specs=[None] * HALVES + w_proj.specs() + w_mix.specs() + [None, SMEM],
        name="attention_forward",
    )
    return {"other": outs[:2], "own": outs[2], "qkv": outs[3], "ctx": outs[4], "probs": outs[5:]}


def attention_backward(order, stream, slots, weights, state):
    w_proj, w_mix = weights
    probs, qkv = state["probs"], state["qkv"]
    share, features = slots[0].shape
    span = w_mix.shape[0]
    heads = span // HEAD
    places = page_places(stream)

    def body(*refs):
        ds, refs = refs[:HALVES], refs[HALVES:]
        wp, refs = w_proj.take(refs)
        wm, refs = w_mix.take(refs)
        chances, refs = refs[: len(places)], refs[len(places) :]
        qkv_ref, *others, part_own, grad, sums, low = refs
        value = None
        for w, at in wm:
            rows = jnp.concatenate([d[:, at] for d in ds], 0)
            term = dot_t(rows, w[...])
            value = term if value is None else value + term
        value = value.astype(BF)
        for _, length, base, offset in places:
            part = length // HALVES
            for slot in range(HALVES):
                low[base + slot * part : base + (slot + 1) * part, :] = value[
                    slot * share + offset : slot * share + offset + part, :
                ]
        for index, (page, length, base, offset) in enumerate(places):
            part = length // HALVES
            step = min(length, 256)
            for pair in range(heads // 2):
                lanes = slice(pair * PAIR, (pair + 1) * PAIR)
                keys = qkv_ref[base : base + length, span + pair * PAIR : span + (pair + 1) * PAIR]
                values = qkv_ref[base : base + length, 2 * span + pair * PAIR : 2 * span + (pair + 1) * PAIR]
                grad_keys, grad_values = [None, None], [None, None]
                for row in range(0, length, step):
                    queries = qkv_ref[base + row : base + row + step, lanes]
                    grad_rows = low[base + row : base + row + step, lanes]
                    found = []
                    for which in range(2):
                        chance = chances[index][2 * pair + which, row : row + step, :]
                        wide = chance.astype(F32)
                        back = dot_t(grad_rows * head_mask(which).astype(BF), values)
                        inner = jnp.sum(wide * back, -1, keepdims=True)
                        grad_scores = (wide * (back - inner)).astype(BF)
                        found.append(dot(grad_scores, keys))
                        of_keys = dot_rows(grad_scores, queries)
                        of_values = dot_rows(chance, grad_rows)
                        first = grad_keys[which] is None
                        grad_keys[which] = of_keys if first else grad_keys[which] + of_keys
                        grad_values[which] = of_values if first else grad_values[which] + of_values
                    both = (jnp.where(head_mask(0), found[0], found[1]) * HEAD ** (-0.5)).astype(BF)
                    put_rows(grad, lanes, both, row, part, share, offset)
                for kind, parts in ((1, grad_keys), (2, grad_values)):
                    both = jnp.where(head_mask(0), parts[0], parts[1]).astype(BF)
                    for slot in range(HALVES):
                        grad[
                            slot * share + offset : slot * share + offset + part,
                            kind * span + pair * PAIR : kind * span + (pair + 1) * PAIR,
                        ] = both[slot * part : (slot + 1) * part, :]
        for w, at in wp:
            value = None
            for kind in range(3):
                term = dot_t(grad[:, kind * span : (kind + 1) * span], w[kind])
                value = term if value is None else value + term
            part_own[:, at] = value[:share]
            split_rows(others, at, value[share:])
        sums[...] = jnp.sum(grad[...].astype(F32), 0, keepdims=True)

    outs = order.call(
        body,
        [*slots, *w_proj.arrays, *w_mix.arrays, *probs, qkv],
        [
            *[shape_of((share // 2, features), BF)] * 2,
            shape_of((share, features), F32),
            shape_of((2 * share, 3 * span), BF),
            shape_of((1, 3 * span), F32),
        ],
        scratch=[pltpu.VMEM((2 * share, span), BF)],
        in_specs=[None] * HALVES + w_proj.specs() + w_mix.specs() + [None] * (len(places) + 1),
        name="attention_backward",
    )
    return {"other": outs[:2], "own": outs[2], "grad": outs[3], "sums": outs[4]}


FF_BLOCK = 256


def feed_forward(order, slots, weights):
    w_grow, w_shrink, bias = weights
    share, features = slots[0].shape
    hidden = w_shrink.shape[0]
    block = min(FF_BLOCK, hidden)
    steps = hidden // block

    def body(*refs):
        xs, refs = refs[:HALVES], refs[HALVES:]
        wg, refs = w_grow.take(refs)
        ws, refs = w_shrink.take(refs)
        b, *others, act, slope, part_own, total = refs
        step = pl.program_id(0)
        value = None
        for w, at in wg:
            rows = jnp.concatenate([x[:, at] for x in xs], 0)
            term = dot(rows, w[...])
            value = term if value is None else value + term
        up = value + b[...]
        cdf = 0.5 * (1.0 + lax.erf(up * 0.7071067811865476))
        density = jnp.exp(-0.5 * up * up) * 0.3989422804014327
        low = (up * cdf).astype(BF)
        act[...] = low
        slope[...] = (cdf + up * density).astype(BF)
        accumulate(step, steps, low, ws, dot, total, share, others, part_own)

    outs = order.call(
        body,
        [*slots, *w_grow.arrays, *w_shrink.arrays, bias],
        [
            *[shape_of((share // 2, features), BF)] * 2,
            shape_of((2 * share, hidden), BF),
            shape_of((2 * share, hidden), BF),
            shape_of((share, features), F32),
        ],
        scratch=[pltpu.VMEM((2 * share, features), F32)],
        grid=(steps,),
        in_specs=[None] * HALVES
        + w_grow.specs(block)
        + w_shrink.specs(block)
        + [pl.BlockSpec((1, block), lambda i: (0, i))],
        out_specs=[None] * 2 + [pl.BlockSpec((2 * share, block), lambda i: (0, i))] * 2 + [None],
        name="feed_forward",
    )
    return {"other": outs[:2], "act": outs[2], "slope": outs[3], "own": outs[4]}


def split_rows(refs, at, value):
    half = value.shape[0] // 2
    refs[0][:, at] = value[:half].astype(BF)
    refs[1][:, at] = value[half:].astype(BF)


def accumulate(step, steps, low, weight, product, total, share, others, part_own):
    for w, at in weight:
        term = product(low, w[...])

        @pl.when(step == 0)
        def _():
            total[:, at] = term

        @pl.when((step > 0) & (step < steps - 1))
        def _():
            total[:, at] += term

        @pl.when(step == steps - 1)
        def _():
            done = term if steps == 1 else total[:, at] + term
            part_own[:, at] = done[:share, :]
            split_rows(others, at, done[share:, :])


def feed_backward(order, slots, slope, weights):
    w_grow, w_shrink = weights
    share, features = slots[0].shape
    hidden = w_shrink.shape[0]
    block = min(FF_BLOCK, hidden)
    steps = hidden // block

    def body(*refs):
        ds, refs = refs[:HALVES], refs[HALVES:]
        wg, refs = w_grow.take(refs)
        ws, refs = w_shrink.take(refs)
        tilt, *others, grad, sums, part_own, total = refs
        step = pl.program_id(0)
        value = None
        for w, at in ws:
            rows = jnp.concatenate([d[:, at] for d in ds], 0)
            term = dot_t(rows, w[...])
            value = term if value is None else value + term
        low = (value * tilt[...].astype(F32)).astype(BF)
        grad[...] = low
        sums[...] = jnp.sum(low.astype(F32), 0, keepdims=True)
        accumulate(step, steps, low, wg, dot_t, total, share, others, part_own)

    outs = order.call(
        body,
        [*slots, *w_grow.arrays, *w_shrink.arrays, slope],
        [
            *[shape_of((share // 2, features), BF)] * 2,
            shape_of((2 * share, hidden), BF),
            shape_of((1, hidden), F32),
            shape_of((share, features), F32),
        ],
        scratch=[pltpu.VMEM((2 * share, features), F32)],
        grid=(steps,),
        in_specs=[None] * HALVES
        + w_grow.specs(block)
        + w_shrink.specs(block)
        + [pl.BlockSpec((2 * share, block), lambda i: (0, i))],
        out_specs=[
            None,
            None,
            pl.BlockSpec((2 * share, block), lambda i: (0, i)),
            pl.BlockSpec((1, block), lambda i: (0, i)),
            None,
        ],
        name="feed_backward",
    )
    return {"other": outs[:2], "grad": outs[2], "sums": outs[3], "own": outs[4]}


def weight_grad(order, pairs, part, parts, first=0, count=None):
    features = pairs[0][0][0].shape[1]
    width = features // parts
    count = count or width
    block = min(256, count)
    per, skip, wide = count // block, first // block, width // block
    start, shards = (0, 1) if part == 0 else (1, parts - 1)
    spans = [right[0].shape[1] for _, right in pairs]
    flat, specs = [], []
    for left, right in pairs:
        flat += [*left, *right]
        specs += [
            pl.BlockSpec((v.shape[0], block), lambda i: (0, (start + i // per) * wide + skip + i % per)) for v in left
        ]
        specs += [None] * len(right)

    def body(*refs):
        out, at, column = refs[-1], 0, 0
        for (left, right), span in zip(pairs, spans):
            a = jnp.concatenate([r[...] for r in refs[at : at + len(left)]], 0)
            at += len(left)
            b = jnp.concatenate([r[...] for r in refs[at : at + len(right)]], 0)
            at += len(right)
            out[0, :, column : column + span] = dot_rows(a, b).astype(BF)
            column += span

    return order.call(
        body,
        flat,
        [shape_of((shards, count, sum(spans)), BF)],
        grid=(shards * per,),
        in_specs=specs,
        out_specs=[pl.BlockSpec((1, block, sum(spans)), lambda i: (i // per, i % per, 0))],
        name="weight_grad",
    )[0]


class Pipeline:
    def __init__(self, order):
        self.order = order
        self.line = lax.axis_size("dp") == 4
        self.waiting, self.pieces, self.at = [], [], 0

    def offer(self, others, own, finish):
        self.waiting.append({"others": others, "own": own, "finish": finish})

    def piece(self, at):
        return self.pieces[at] if 0 <= at < len(self.pieces) else None

    def step(self):
        size = lax.axis_size("fsdp")
        now = self.at
        self.at += 1
        oldest, older, old, new = (self.piece(now - 1 - back) for back in (3, 2, 1, 0))
        if not self.line:
            if new is not None:
                total = lax.psum(combine(self.order, [new["own"], *new["came"]]), "dp")
                new["finish"](total, total)
        else:
            if old is not None:
                old["inner"] = combine(self.order, [old["sum"], old["swapped"]])
                old["met"] = lax.ppermute(old["inner"], "dp", [(1, 2), (2, 1)])
            if older is not None:
                older["total"] = combine(self.order, [older["inner"], older["met"]])
            if new is not None and older is not None and new["own"].shape == older["total"].shape:
                new["sum"], send = combine(self.order, [new["own"], *new["came"]], older["total"])
                new["swapped"] = older["back"] = lax.ppermute(send, "dp", [(0, 1), (1, 0), (2, 3), (3, 2)])
            else:
                if new is not None:
                    new["sum"] = combine(self.order, [new["own"], *new["came"]])
                    new["swapped"] = lax.ppermute(new["sum"], "dp", [(0, 1), (3, 2)])
                if older is not None:
                    older["back"] = lax.ppermute(older["total"], "dp", [(1, 0), (2, 3)])
            if oldest is not None:
                oldest["finish"](oldest["total"], oldest["back"])
        if self.waiting:
            piece = self.waiting.pop(0)
            piece["came"] = [to_fsdp(piece["others"][k], k + 1) for k in range(size - 1)]
            self.pieces.append(piece)
        else:
            self.pieces.append(None)

    def drain(self):
        while self.waiting or any(p is not None for p in self.pieces[self.at - 4 :]):
            self.step()


def at_end():
    here = lax.axis_index("dp")
    return (here == 0) | (here == lax.axis_size("dp") - 1)


def combine(order, terms, other=None):
    rows, width = terms[0].shape
    dtype = terms[0].dtype
    count = len(terms)
    block = max(rows // 2, 16)
    spec = pl.BlockSpec((block, width), lambda i: (i, 0))
    given = [*terms] + ([] if other is None else [other])

    def body(*refs):
        total = refs[0][...].astype(F32)
        for ref in refs[1:count]:
            total = total + ref[...].astype(F32)
        total = total.astype(dtype)
        refs[len(given)][...] = total
        if other is not None:
            refs[-1][...] = jnp.where(at_end(), total.astype(F32), refs[count][...].astype(F32)).astype(dtype)

    found = order.call(
        body,
        given,
        [shape_of((rows, width), dtype)] * (1 if other is None else 2),
        grid=(rows // block,),
        in_specs=[spec] * len(given),
        out_specs=[spec] * (1 if other is None else 2),
        name="combine",
    )
    return found[0] if other is None else found


def finish_piece(order, total, back, layer, first, held, parts, name):
    rows, width = total.shape
    given = [] if held is None else list(held)
    blocks = []
    for shape, axis, _, _ in parts:
        block, place = [1, *shape[1:]], [layer] + [0] * (len(shape) - 1)
        block[axis], place[axis] = rows, first // rows
        blocks.append(pl.BlockSpec(tuple(block), lambda i, place=tuple(place): place))

    def body(*refs):
        outs = refs[2 + len(given) :]
        value = jnp.where(at_end(), refs[1][...].astype(F32), refs[0][...].astype(F32))
        for out, (shape, axis, start, count) in zip(outs, parts):
            if len(shape) == 4:
                span = count // shape[1]
                for g in range(shape[1]):
                    out[0, g] = value[:, start + g * span : start + (g + 1) * span]
            elif axis == 2:
                out[0] = value[:, start : start + count].T
            else:
                out[0] = value[:, start : start + count]

    return order.call(
        body,
        [total, back, *given],
        [shape_of(shape, F32) for shape, *_ in parts],
        grid=(1,),
        in_specs=[None, None] + [ANY] * len(given),
        out_specs=blocks,
        alias={2 + i: i for i in range(len(given))},
        name=name,
        limit=24,
    )


STEPS = (0, 1, 0, 1, 0, 1, 0, 1)
MORE_STEPS = (0, 0, 1, 0, 1, 0, 1, 0)
LAST_CUT = 2


def gather_halves(share):
    return [share, to_core(share)]


def per_device(
    activations, cotangent, lengths, w_qkv, w_out, w_up, w_down, b_qv, b_up, norm_gains, layer_biases
):
    size = lax.axis_size("fsdp")
    order = Order()
    kinds = range(len(STREAMS))

    smalls = (b_qv, b_up, norm_gains, layer_biases)
    flat = jnp.concatenate([value.reshape(-1) for value in smalls])
    pieces = [flat] + [from_fsdp(flat, step) for step in range(1, size)]

    def unpack(at):
        found, start = [], 0
        for value in smalls:
            found.append(pieces[at][start : start + value.size].reshape(value.shape))
            start += value.size
        return found

    unpacked = [unpack(at) for at in range(size)]
    bias_heads, bias_grow, gains, biases = (
        jnp.concatenate([u[i] for u in unpacked], -1).astype(F32) for i in range(4)
    )
    bias_heads, bias_grow = natural(bias_heads, 3), natural(bias_grow, 2)
    features = gains.shape[-1]
    vectors = jnp.concatenate([gains.reshape(-1, features), biases.reshape(-1, features)], 0)
    head_rows = [bias_heads[layer].reshape(2, -1) for layer in range(LAYERS)]
    grow_rows = [bias_grow[layer].reshape(1, -1) for layer in range(LAYERS)]

    def fetch(whole, layer, axis, cut):
        shard = whole[layer]
        count = shard.shape[axis] // cut
        if count < 128:
            cut, count = 1, shard.shape[axis]
        came = []
        for step in range(1, size):
            for at in range(cut):
                piece = lax.slice_in_dim(shard, at * count, (at + 1) * count, axis=axis)
                came.append(from_fsdp(piece, step))
        return Weight([shard] + came, axis)

    weights = [
        [fetch(w_qkv, layer, 1, 1), fetch(w_out, layer, 1, 1), fetch(w_up, layer, 0, 2), fetch(w_down, layer, 1, 2)]
        for layer in range(LAYERS)
    ]

    def halves_of(weight):
        came = weight.arrays[1:]
        middle = (len(came) + 1) // 2
        return came[:middle], came[middle:]

    up_zero, down_zero = halves_of(weights[0][2]), halves_of(weights[0][3])
    up_one, down_one = halves_of(weights[1][2]), halves_of(weights[1][3])
    ahead = {
        1: up_zero[0],
        2: [*up_zero[1], *down_zero[0], *down_zero[1]],
        3: weights[1][0].arrays[1:],
        4: [*weights[1][1].arrays[1:], *up_one[0]],
        5: up_one[1],
        6: [*down_one[0], *down_one[1]],
    }

    slots = deal_rows(order, activations)
    residual = [(slots[s][0], None, None) for s in kinds]
    across = to_chip(cotangent)
    shares = deal_share(order, [cotangent, to_core(cotangent), across, to_core(across)])

    streams = len(STREAMS)
    kept = [{k: [None] * streams for k in ("x", "attended", "grown", "one", "two", "middle")} for _ in range(LAYERS)]
    terms = [None] * streams
    back_two, slots_two, fed = ([[None] * streams for _ in range(LAYERS)] for _ in range(3))
    back_one, slots_one, went = ([[None] * streams for _ in range(LAYERS)] for _ in range(3))

    def gain_at(layer, which):
        return 2 * layer + which

    def bias_at(layer, which):
        return 2 * LAYERS + 4 * layer + which

    def second_norm(layer, s):
        one = kept[layer]["one"][s]
        kept[layer]["two"][s] = norm_forward(
            order,
            terms[s],
            (one[1], gain_at(layer, 0), bias_at(layer, 2)),
            vectors,
            (bias_at(layer, 1), gain_at(layer, 1), bias_at(layer, 3)),
        )

    def attend(layer, s):
        def before():
            if layer > 0:
                second_norm(layer - 1, s)
                two = kept[layer - 1]["two"][s]
                slots[s] = gather_halves(two[0])
                residual[s] = (two[1], gain_at(layer - 1, 1), bias_at(layer - 1, 3))
            kept[layer]["x"][s] = slots[s]

        def products():
            w_proj, w_mix = weights[layer][:2]
            found = attention_forward(order, STREAMS[s], slots[s], (w_proj, w_mix, head_rows[layer]), lengths)
            kept[layer]["attended"][s] = found
            return found, []

        return before, products

    def feed(layer, s):
        def before():
            one = norm_forward(
                order, terms[s], residual[s], vectors, (bias_at(layer, 0), gain_at(layer, 0), bias_at(layer, 2))
            )
            kept[layer]["one"][s] = one
            kept[layer]["middle"][s] = gather_halves(one[0])

        def products():
            w_grow, w_shrink = weights[layer][2:]
            found = feed_forward(order, kept[layer]["middle"][s], (w_grow, w_shrink, grow_rows[layer]))
            kept[layer]["grown"][s] = found
            return found, []

        return before, products

    def feed_back(layer, s):
        def before():
            if layer + 1 == LAYERS:
                second_norm(layer, s)
                terms[s] = [shares[s]]
            two = kept[layer]["two"][s]
            back_two[layer][s] = norm_backward(order, terms[s], two[1], two[2], vectors, gain_at(layer, 1))
            slots_two[layer][s] = gather_halves(back_two[layer][s][0])

        def products():
            w_grow, w_shrink = weights[layer][2:]
            found = feed_backward(order, slots_two[layer][s], kept[layer]["grown"][s]["slope"], (w_grow, w_shrink))
            fed[layer][s] = found
            if s + 1 == streams:
                state = kept[layer]
                queue(layer, "down", [([v for t in kinds for v in slots_two[layer][t]], [state["grown"][t]["act"] for t in kinds])])
                queue(layer, "up", [([v for t in kinds for v in state["middle"][t]], [fed[layer][t]["grad"] for t in kinds])])
            return found, [back_two[layer][s][2]]

        return before, products

    def attend_back(layer, s):
        def before():
            one = kept[layer]["one"][s]
            back_one[layer][s] = norm_backward(order, terms[s], one[1], one[2], vectors, gain_at(layer, 0))
            slots_one[layer][s] = gather_halves(back_one[layer][s][0])

        def products():
            w_proj, w_mix = weights[layer][:2]
            state = kept[layer]
            found = attention_backward(order, STREAMS[s], slots_one[layer][s], (w_proj, w_mix), state["attended"][s])
            went[layer][s] = found
            if s + 1 == streams:
                queue(
                    layer,
                    "att",
                    [
                        ([v for t in kinds for v in state["x"][t]], [went[layer][t]["grad"] for t in kinds]),
                        ([v for t in kinds for v in slots_one[layer][t]], [state["attended"][t]["ctx"] for t in kinds]),
                    ],
                    1 if layer > 0 else LAST_CUT,
                )
            return found, [back_one[layer][s][2]]

        return before, products

    pipeline = Pipeline(order)
    fillers = []
    outputs = {}
    span, hidden = w_out.shape[1], w_down.shape[1]
    width = features // size
    forms = {
        "down": [((LAYERS, hidden, width), 2, 0, hidden)],
        "up": [((LAYERS, width, hidden), 1, 0, hidden)],
        "att": [((LAYERS, 3, width, span), 2, 0, 3 * span), ((LAYERS, span, width), 2, 3 * span, span)],
    }

    def queue(layer, name, pairs, cut=1):
        count = width // cut if width // cut >= 128 else width
        for first in range(0, width, count):
            queue_rows(layer, name, pairs, first, count)

    def queue_rows(layer, name, pairs, first, count):
        def finish(total, back):
            outputs[name] = finish_piece(
                order, total, back, layer, first, outputs.get(name), forms[name], "finish_" + name
            )

        found = {}

        def others():
            found["others"] = weight_grad(order, pairs, 1, size, first, count)

        def own():
            found["own"] = weight_grad(order, pairs, 0, size, first, count)[0]
            pipeline.offer(found["others"], found["own"], finish)

        fillers.extend([others, own])

    def fill(count):
        for _ in range(count):
            if fillers:
                fillers.pop(0)()

    items = []
    for layer in range(LAYERS):
        items += [attend(layer, s) for s in kinds] + [feed(layer, s) for s in kinds]
    forward_items = len(items)
    for layer in reversed(range(LAYERS)):
        items += [feed_back(layer, s) for s in kinds] + [attend_back(layer, s) for s in kinds]
    items[0][0]()
    for at, (_, products) in enumerate(items):
        s = at % streams
        found, more = products()
        beside = [to_core(part) for part in found["other"]]
        if at >= forward_items:
            fill(2)
            if STEPS[at - forward_items]:
                pipeline.step()
        order.pin(ahead.get(at + 1, []))
        if at == 0:
            order.hold()
        if at + 1 < len(items):
            items[at + 1][0]()
        if at == forward_items + 1:
            out_rows = gather_halves(jnp.concatenate([kept[-1]["two"][t][0] for t in kinds], 0))
        low, wide = add_send(order, found["own"], beside)
        terms[s] = [wide, to_chip(low), *more]
        if at >= forward_items and MORE_STEPS[at - forward_items]:
            pipeline.step()
    fill(len(fillers))
    pipeline.step()
    layer_out = natural_share(order, out_rows, BF)
    ends = [last_sum(order, terms[s]) for s in kinds]
    end_rows = gather_halves(jnp.concatenate(ends, 0))
    pipeline.step()
    input_grad = natural_share(order, end_rows, F32)
    pipeline.drain()

    sums, head_sums, grow_sums = {}, {}, {}
    for layer in range(LAYERS):
        sums[layer] = [sum(back_one[layer][s][1] for s in kinds), sum(back_two[layer][s][1] for s in kinds)]
        head_sums[layer] = sum(went[layer][s]["sums"] for s in kinds)
        grow_sums[layer] = sum(fed[layer][s]["sums"] for s in kinds)
    heads_bias = jnp.stack(
        [
            jnp.stack([head_sums[layer][0, :span], head_sums[layer][0, 2 * span :]])
            for layer in range(LAYERS)
        ]
    ).reshape(bias_heads.shape)
    grow_bias = jnp.stack([grow_sums[layer] for layer in range(LAYERS)]).reshape(bias_grow.shape)
    gain_pair = jnp.stack([jnp.stack([sums[layer][i][0] for i in range(2)]) for layer in range(LAYERS)])
    bias_set = jnp.stack(
        [
            jnp.stack([sums[layer][0][2], sums[layer][1][2], sums[layer][0][1], sums[layer][1][1]])
            for layer in range(LAYERS)
        ]
    )
    norms = jnp.concatenate([gain_pair.reshape(-1, features), bias_set.reshape(-1, features)])
    norms = norms + to_core(norms)
    own_heads, own_grow = own_first(heads_bias, 3), own_first(grow_bias, 2)
    little = []
    for step in range(size):
        parts = []
        for value in (own_heads, own_grow, norms):
            part = value.shape[-1] // size
            parts.append(value[..., step * part : (step + 1) * part].reshape(-1))
        little.append(jnp.concatenate(parts))
    total = little[0]
    for step in range(1, size):
        total = total + to_fsdp(little[step], step)
    dp_size = lax.axis_size("dp")
    reach = 1
    while reach < dp_size:
        total = total + lax.ppermute(total, "dp", [(i, i ^ reach) for i in range(dp_size)])
        reach *= 2
    finals, start = [], 0
    for value in (own_heads, own_grow, gain_pair, bias_set):
        amount = value.size // size
        finals.append(total[start : start + amount].reshape(value.shape[:-1] + (value.shape[-1] // size,)))
        start += amount
    return (layer_out, input_grad, *outputs["att"], *outputs["up"], *outputs["down"], *finals)


def solution(mesh):
    in_specs = (
        P(("dp", "fsdp"), None),
        P(("dp", "fsdp", "tensor"), None),
        P(("dp", "fsdp")),
        P(None, None, "fsdp", "tensor"),
        P(None, "tensor", "fsdp"),
        P(None, "fsdp", "tensor"),
        P(None, "tensor", "fsdp"),
        P(None, None, "tensor", "fsdp"),
        P(None, "tensor", "fsdp"),
        P(None, None, "fsdp"),
        P(None, None, "fsdp"),
    )
    out_specs = (
        P(("dp", "fsdp", "tensor"), None),
        P(("dp", "fsdp", "tensor"), None),
        P(None, None, "fsdp", "tensor"),
        P(None, "tensor", "fsdp"),
        P(None, "fsdp", "tensor"),
        P(None, "tensor", "fsdp"),
        P(None, None, "tensor", "fsdp"),
        P(None, "tensor", "fsdp"),
        P(None, None, "fsdp"),
        P(None, None, "fsdp"),
    )
    return jax.shard_map(
        per_device, mesh=mesh, in_specs=in_specs, out_specs=out_specs, check_vma=False
    )
```

```python
import functools

import jax
import jax.numpy as jnp
from jax import lax
from jax.experimental import pallas as pl
from jax.experimental.pallas import tpu as pltpu
from jax.sharding import PartitionSpec as P

HEAD = 64
PAIR = 2 * HEAD
LAYERS = 2
LENGTHS = (512, 256, 128, 128, 128)
STARTS = (0, 512, 768, 896, 1024)
STREAMS = ((0,), (1, 2, 3, 4))
HALVES = 2
BF = jnp.bfloat16
F32 = jnp.float32
MIB = 1 << 20
CORE_SWAP = [(0, 1), (1, 0), (2, 3), (3, 2)]
CHIP_SWAP = [(0, 2), (2, 0), (1, 3), (3, 1)]


def to_core(value):
    return lax.ppermute(value, "tensor", CORE_SWAP)


def to_chip(value):
    return lax.ppermute(value, "tensor", CHIP_SWAP)


def from_fsdp(value, step):
    size = lax.axis_size("fsdp")
    return lax.ppermute(value, "fsdp", [((i + step) % size, i) for i in range(size)])


def to_fsdp(value, step):
    size = lax.axis_size("fsdp")
    return lax.ppermute(value, "fsdp", [(i, (i + step) % size) for i in range(size)])


def own_first(whole, axis):
    size = lax.axis_size("fsdp")
    here = lax.axis_index("fsdp")
    width = whole.shape[axis] // size
    return jnp.concatenate(
        [lax.dynamic_slice_in_dim(whole, (here + k) % size * width, width, axis) for k in range(size)], axis
    )


def natural(relative, axis):
    size = lax.axis_size("fsdp")
    here = lax.axis_index("fsdp")
    width = relative.shape[axis] // size
    return jnp.concatenate(
        [
            lax.dynamic_slice_in_dim(relative, (k - here + size) % size * width, width, axis)
            for k in range(size)
        ],
        axis,
    )


def dot(left, right):
    return jnp.dot(left, right, preferred_element_type=F32)


def dot_t(left, right):
    return lax.dot_general(left, right, (((1,), (1,)), ((), ())), preferred_element_type=F32)


def dot_rows(left, right):
    return lax.dot_general(left, right, (((0,), (0,)), ((), ())), preferred_element_type=F32)


def share_rows(stream):
    return sum(LENGTHS[page] for page in stream) // HALVES


def page_places(stream):
    places, at = [], 0
    for page in stream:
        places.append((page, LENGTHS[page], at, at // HALVES))
        at += LENGTHS[page]
    return places


SCOPED = 8


class Order:
    def __init__(self):
        self.last = None
        self.pins = []

    def pin(self, arrays):
        self.pins.extend(v for v in arrays)

    def call(
        self,
        body,
        inputs,
        outputs,
        scratch=(),
        grid=(),
        in_specs=None,
        out_specs=None,
        name=None,
        limit=SCOPED,
        alias=None,
    ):
        pins, self.pins = self.pins, []
        count = len(inputs)
        in_specs = in_specs or [None] * count
        out_specs = out_specs or [None] * len(outputs)
        in_specs = [whole_of(v.shape, grid) if s is None else s for s, v in zip(in_specs, inputs)]
        out_specs = [whole_of(v.shape, grid) if s is None else s for s, v in zip(out_specs, outputs)]
        token = shape_of((8, 128), F32)
        inputs = list(inputs) + pins + ([] if self.last is None else [self.last])
        in_specs += [ANY] * (len(inputs) - count)
        extra = len(inputs) - count

        def kernel(*refs):
            given, refs = refs[:count], refs[count + extra :]
            outs, mark, own = refs[: len(outputs)], refs[len(outputs)], refs[len(outputs) + 1 :]
            mark[...] = jnp.zeros(mark.shape, F32)
            body(*given, *outs, *own)

        *result, self.last = pl.pallas_call(
            kernel,
            grid=grid,
            in_specs=in_specs,
            out_specs=[*out_specs, whole_of(token.shape, grid)],
            out_shape=[*outputs, token],
            scratch_shapes=list(scratch),
            input_output_aliases=alias or {},
            name=name,
            cost_estimate=pl.CostEstimate(flops=0, bytes_accessed=0, transcendentals=0),
            compiler_params=pltpu.CompilerParams(vmem_limit_bytes=limit * MIB),
        )(*inputs)
        return result


def whole_of(shape, grid):
    if not grid:
        return pl.BlockSpec(memory_space=pltpu.VMEM)
    return pl.BlockSpec(shape, lambda *at: (0,) * len(shape))


def shape_of(shape, dtype):
    return jax.ShapeDtypeStruct(tuple(shape), dtype)


SMEM = pl.BlockSpec(memory_space=pltpu.SMEM)
ANY = pl.BlockSpec(memory_space=pl.ANY)
HELD = pl.BlockSpec(memory_space=pltpu.HBM)


def core_index():
    return lax.rem(lax.axis_index("tensor"), 2)


class Weight:
    def __init__(self, order, whole, layer, axis):
        self.order, self.whole, self.layer, self.axis = order, whole, layer, axis
        self.size = lax.axis_size("fsdp")
        shape = whole.shape[1:]
        width = shape[axis]
        self.halved = self.size == 2 and lax.axis_size("dp") % 2 == 0 and width % 256 == 0
        self.widths = [width] + ([width // 2] * 2 if self.halved else [width] * (self.size - 1))
        self.shape = shape

    def places(self):
        width = self.widths[0]
        if not self.halved:
            return [pl.ds(k * width, width) for k in range(self.size)]
        parity = lax.rem(lax.axis_index("dp"), 2)
        half = width // 2
        return [
            pl.ds(0, width),
            pl.ds(pl.multiple_of(width + parity * half, 128), half),
            pl.ds(pl.multiple_of(width + (1 - parity) * half, 128), half),
        ]

    def start(self, own, half):
        if self.halved:
            self.early = [from_fsdp(half, 1)]
            size = lax.axis_size("dp")
            self.late = [lax.ppermute(self.early[0], "dp", [(i, i ^ 1) for i in range(size)])]
        else:
            self.early = [from_fsdp(own, step) for step in range(1, self.size)]
            self.late = []
        self.arrays = [own, *self.early, *self.late]

    def specs(self):
        return [None] * len(self.arrays)

    def take(self, refs):
        count = len(self.arrays)
        return list(zip(refs[:count], self.places())), refs[count:]


def fetch(order, weights):
    outputs = []
    for w in weights:
        outputs.append(shape_of(w.shape, BF))
        if w.halved:
            shape = list(w.shape)
            shape[w.axis] //= 2
            outputs.append(shape_of(shape, BF))

    def body(*refs):
        outs, sems = list(refs[len(weights) : -1]), refs[-1]
        parity = lax.rem(lax.axis_index("dp"), 2)
        copies = []
        for w, ref in zip(weights, refs):
            sources = [ref.at[w.layer]]
            if w.halved:
                half = w.widths[1]
                place = [slice(None)] * len(w.shape)
                place[w.axis] = pl.ds(pl.multiple_of(parity * half, 128), half)
                sources.append(ref.at[(w.layer, *place)])
            for source in sources:
                copy = pltpu.make_async_copy(source, outs.pop(0), sems.at[len(copies)])
                copy.start()
                copies.append(copy)
        for copy in copies:
            copy.wait()

    found = order.call(
        body,
        [w.whole for w in weights],
        outputs,
        scratch=[pltpu.SemaphoreType.DMA((len(outputs),))],
        in_specs=[HELD] * len(weights),
        name="fetch",
    )
    for w in weights:
        own = found.pop(0)
        w.start(own, found.pop(0) if w.halved else None)


def deal_rows(order, activations):
    features = activations.shape[1]
    size = lax.axis_size("fsdp")
    width = features // size

    def body(whole, *outs):
        here = core_index()
        mine = lax.axis_index("fsdp")
        for at, stream in enumerate(STREAMS):
            for slot in range(HALVES):
                out = outs[at * HALVES + slot]
                for page, length, _, offset in page_places(stream):
                    part = length // HALVES
                    row = pl.multiple_of(STARTS[page] + (here ^ slot) * part, 32)
                    for k in range(size):
                        column = pl.multiple_of(lax.rem(mine + k, size) * width, 128)
                        out[offset : offset + part, k * width : (k + 1) * width] = whole[
                            pl.ds(row, part), pl.ds(column, width)
                        ]

    outs = order.call(
        body,
        [activations],
        [shape_of((share_rows(stream), features), BF) for stream in STREAMS for _ in range(HALVES)],
        name="deal_rows",
    )
    return [outs[at * HALVES : (at + 1) * HALVES] for at in range(len(STREAMS))]


def copy_rows(order, rows):
    def body(a, out):
        out[...] = a[...]

    return order.call(body, [rows], [shape_of(rows.shape, rows.dtype)], name="copy_rows")[0]


def deal_share(order, slots):
    rows, features = slots[0].shape
    size = lax.axis_size("fsdp")
    width = features // size

    def body(a, b, c, d, *outs):
        whole = outs[-1]
        here = lax.axis_index("tensor")
        core = core_index()
        mine = lax.axis_index("fsdp")
        for slot, ref in enumerate((a, b, c, d)):
            whole[pl.ds(pl.multiple_of((here ^ slot) * rows, 32), rows), :] = ref[...]
        for at, stream in enumerate(STREAMS):
            for page, length, _, offset in page_places(stream):
                part = length // HALVES
                row = pl.multiple_of(STARTS[page] + core * part, 32)
                for k in range(size):
                    column = pl.multiple_of(lax.rem(mine + k, size) * width, 128)
                    outs[at][offset : offset + part, k * width : (k + 1) * width] = whole[
                        pl.ds(row, part), pl.ds(column, width)
                    ]

    return order.call(
        body,
        slots,
        [shape_of((share_rows(stream), features), BF) for stream in STREAMS],
        scratch=[pltpu.VMEM((rows * 4, features), BF)],
        name="deal_share",
    )


def natural_share(order, slots, dtype):
    rows, features = slots[0].shape
    share = rows // 2
    size = lax.axis_size("fsdp")
    width = features // size

    def body(a, b, out, whole):
        here = lax.axis_index("tensor")
        core = core_index()
        mine = lax.axis_index("fsdp")
        for slot, ref in enumerate((a, b)):
            first = 0
            for stream in STREAMS:
                for page, length, _, offset in page_places(stream):
                    part = length // HALVES
                    row = pl.multiple_of(STARTS[page] + (core ^ slot) * part, 32)
                    whole[pl.ds(row, part), :] = ref[first + offset : first + offset + part, :]
                first += share_rows(stream)
        own = pl.multiple_of(here * share, 32)
        for k in range(size):
            column = pl.multiple_of(lax.rem(mine + k, size) * width, 128)
            out[:, pl.ds(column, width)] = whole[pl.ds(own, share), k * width : (k + 1) * width].astype(dtype)

    return order.call(
        body,
        slots,
        [shape_of((share, features), dtype)],
        scratch=[pltpu.VMEM((rows * 2, features), BF)],
        name="natural_share",
    )[0]


def add_send(order, kept, came):
    half = kept.shape[0] // 2

    def body(a, b, c, low):
        for at, came_ref in ((0, b), (half, c)):
            low[at : at + half, :] = (a[at : at + half, :].astype(F32) + came_ref[...].astype(F32)).astype(BF)

    return order.call(body, [kept, *came], [shape_of(kept.shape, BF)], name="add_send")[0]


def sum_terms(own, first, second, across):
    beside = jnp.concatenate([first[...], second[...]], 0)
    return own[...].astype(F32) + beside.astype(F32) + across[...].astype(F32)


def row_of(ref, at):
    return ref[at : at + 1, :]


def norm_forward(order, terms, residual, vectors, rows_of_vectors):
    rows, features = terms[0].shape
    bias_at, gain_at, shift_at = rows_of_vectors

    def body(a, b, c, d, before, vec, low, normed, inverse, kept):
        value = before[...].astype(F32)
        if residual[1] is not None:
            value = value * row_of(vec, residual[1]) + row_of(vec, residual[2])
        value = value + sum_terms(a, b, c, d) + row_of(vec, bias_at)
        center = value - jnp.mean(value, -1, keepdims=True)
        scale = lax.rsqrt(jnp.mean(center * center, -1, keepdims=True) + 1e-05)
        unit = center * scale
        normed[...] = unit
        kept[...] = unit.astype(BF)
        inverse[...] = scale
        low[...] = (unit * row_of(vec, gain_at) + row_of(vec, shift_at)).astype(BF)

    return order.call(
        body,
        [*terms, residual[0], vectors],
        [
            shape_of((rows, features), BF),
            shape_of((rows, features), F32),
            shape_of((rows, 1), F32),
            shape_of((rows, features), BF),
        ],
        name="norm_forward",
    )


def norm_backward(order, terms, normed, inverse, vectors, gain_at):
    rows, features = normed.shape
    count = len(terms)

    def body(*refs):
        unit, scale, vec, low, sums, wide = refs[count:]
        total = refs[count - 1][...].astype(F32)
        if count > 1:
            total = total + sum_terms(*refs[: count - 1])
        n = unit[...].astype(F32)
        grad = total * row_of(vec, gain_at)
        mean_one = jnp.mean(grad, -1, keepdims=True)
        mean_two = jnp.mean(grad * n, -1, keepdims=True)
        result = scale[...] * (grad - mean_one - n * mean_two)
        wide[...] = result
        low[...] = result.astype(BF)
        sums[0:1, :] = jnp.sum(total * n, 0, keepdims=True)
        sums[1:2, :] = jnp.sum(total, 0, keepdims=True)
        sums[2:3, :] = jnp.sum(result, 0, keepdims=True)

    return order.call(
        body,
        [*terms, normed, inverse, vectors],
        [shape_of((rows, features), BF), shape_of((3, features), F32), shape_of((rows, features), F32)],
        name="norm_backward",
    )


def last_sum(order, terms):
    def body(*refs):
        refs[-1][...] = (refs[4][...] + sum_terms(*refs[:4])).astype(BF)

    return order.call(body, terms, [shape_of(terms[0].shape, BF)], name="last_sum")[0]


def head_mask(which):
    lane = lax.broadcasted_iota(jnp.int32, (1, PAIR), 1)
    return (lane < HEAD) if which == 0 else (lane >= HEAD)


def key_bias(length, limit):
    part = length // HALVES
    place = lax.broadcasted_iota(jnp.int32, (1, length), 1)
    half = (place // part) ^ core_index()
    return jnp.where(half * part + place % part < limit, 0.0, -1000000000.0).astype(F32)


def put_rows(ref, lanes, value, row, part, share, offset):
    done = 0
    while done < value.shape[0]:
        at = row + done
        count = min(part - at % part, value.shape[0] - done)
        first = (at // part) * share + offset + at % part
        ref[first : first + count, lanes] = value[done : done + count]
        done += count


def attention_forward(order, stream, slots, weights, lengths):
    w_proj, w_mix, bias_rows = weights
    share, features = slots[0].shape
    span = w_mix.shape[0]
    heads = span // HEAD
    places = page_places(stream)

    def body(*refs):
        xs, refs = refs[:HALVES], refs[HALVES:]
        wp, refs = w_proj.take(refs)
        wm, refs = w_mix.take(refs)
        bias, limits, refs = refs[0], refs[1], refs[2:]
        others, part_own, qkv, ctx, probs = refs[:2], refs[2], refs[3], refs[4], refs[5:]
        for kind in range(3):
            value = None
            for w, at in wp:
                rows = jnp.concatenate([x[:, at] for x in xs], 0)
                term = dot(rows, w[kind])
                value = term if value is None else value + term
            if kind == 0:
                value = value + bias[0:1, :]
            elif kind == 2:
                value = value + bias[1:2, :]
            value = value.astype(BF)
            if kind == 0:
                value = value * jnp.asarray(HEAD ** (-0.5), BF)
            for _, length, base, offset in places:
                part = length // HALVES
                for slot in range(HALVES):
                    qkv[base + slot * part : base + (slot + 1) * part, kind * span : (kind + 1) * span] = value[
                        slot * share + offset : slot * share + offset + part, :
                    ]
        for index, (page, length, base, offset) in enumerate(places):
            part = length // HALVES
            shut = key_bias(length, limits[page])
            step = min(length, 256)
            for pair in range(heads // 2):
                lanes = slice(pair * PAIR, (pair + 1) * PAIR)
                keys = qkv[base : base + length, span + pair * PAIR : span + (pair + 1) * PAIR]
                values = qkv[base : base + length, 2 * span + pair * PAIR : 2 * span + (pair + 1) * PAIR]
                for row in range(0, length, step):
                    queries = qkv[base + row : base + row + step, lanes]
                    found = []
                    for which in range(2):
                        masked = queries * head_mask(which).astype(BF)
                        scores = dot_t(masked, keys) + shut
                        peak = jnp.max(scores, -1, keepdims=True)
                        raised = jnp.exp(scores - peak)
                        chance = raised * (1.0 / jnp.sum(raised, -1, keepdims=True))
                        chance = chance.astype(BF)
                        probs[index][2 * pair + which, row : row + step, :] = chance
                        found.append(dot(chance, values))
                    both = jnp.where(head_mask(0), found[0], found[1]).astype(BF)
                    put_rows(ctx, lanes, both, row, part, share, offset)
        for w, at in wm:
            value = dot(ctx[...], w[...])
            part_own[:, at] = value[:share].astype(BF)
            split_rows(others, at, value[share:])

    outs = order.call(
        body,
        [*slots, *w_proj.arrays, *w_mix.arrays, bias_rows, lengths],
        [
            *[shape_of((share // 2, features), BF)] * 2,
            shape_of((share, features), BF),
            shape_of((2 * share, 3 * span), BF),
            shape_of((2 * share, span), BF),
        ]
        + [shape_of((heads, length, length), BF) for _, length, _, _ in places],
        in_specs=[None] * HALVES + w_proj.specs() + w_mix.specs() + [None, SMEM],
        name="attention_forward",
    )
    return {"other": outs[:2], "own": outs[2], "qkv": outs[3], "ctx": outs[4], "probs": outs[5:]}


def attention_backward(order, stream, slots, weights, state):
    w_proj, w_mix = weights
    probs, qkv = state["probs"], state["qkv"]
    share, features = slots[0].shape
    span = w_mix.shape[0]
    heads = span // HEAD
    places = page_places(stream)

    def body(*refs):
        ds, refs = refs[:HALVES], refs[HALVES:]
        wp, refs = w_proj.take(refs)
        wm, refs = w_mix.take(refs)
        chances, refs = refs[: len(places)], refs[len(places) :]
        qkv_ref, *others, part_own, grad, sums, low = refs
        value = None
        for w, at in wm:
            rows = jnp.concatenate([d[:, at] for d in ds], 0)
            term = dot_t(rows, w[...])
            value = term if value is None else value + term
        value = value.astype(BF)
        for _, length, base, offset in places:
            part = length // HALVES
            for slot in range(HALVES):
                low[base + slot * part : base + (slot + 1) * part, :] = value[
                    slot * share + offset : slot * share + offset + part, :
                ]
        for index, (page, length, base, offset) in enumerate(places):
            part = length // HALVES
            step = min(length, 256)
            for pair in range(heads // 2):
                lanes = slice(pair * PAIR, (pair + 1) * PAIR)
                keys = qkv_ref[base : base + length, span + pair * PAIR : span + (pair + 1) * PAIR]
                values = qkv_ref[base : base + length, 2 * span + pair * PAIR : 2 * span + (pair + 1) * PAIR]
                grad_keys, grad_values = [None, None], [None, None]
                for row in range(0, length, step):
                    queries = qkv_ref[base + row : base + row + step, lanes]
                    grad_rows = low[base + row : base + row + step, lanes]
                    found = []
                    for which in range(2):
                        chance = chances[index][2 * pair + which, row : row + step, :]
                        wide = chance.astype(F32)
                        back = dot_t(grad_rows * head_mask(which).astype(BF), values)
                        inner = jnp.sum(wide * back, -1, keepdims=True)
                        grad_scores = (wide * (back - inner)).astype(BF)
                        found.append(dot(grad_scores, keys))
                        of_keys = dot_rows(grad_scores, queries)
                        of_values = dot_rows(chance, grad_rows)
                        first = grad_keys[which] is None
                        grad_keys[which] = of_keys if first else grad_keys[which] + of_keys
                        grad_values[which] = of_values if first else grad_values[which] + of_values
                    both = (jnp.where(head_mask(0), found[0], found[1]) * HEAD ** (-0.5)).astype(BF)
                    put_rows(grad, lanes, both, row, part, share, offset)
                for kind, parts in ((1, grad_keys), (2, grad_values)):
                    both = jnp.where(head_mask(0), parts[0], parts[1]).astype(BF)
                    for slot in range(HALVES):
                        grad[
                            slot * share + offset : slot * share + offset + part,
                            kind * span + pair * PAIR : kind * span + (pair + 1) * PAIR,
                        ] = both[slot * part : (slot + 1) * part, :]
        for w, at in wp:
            value = None
            for kind in range(3):
                term = dot_t(grad[:, kind * span : (kind + 1) * span], w[kind])
                value = term if value is None else value + term
            part_own[:, at] = value[:share].astype(BF)
            split_rows(others, at, value[share:])
        sums[...] = jnp.sum(grad[...].astype(F32), 0, keepdims=True)

    outs = order.call(
        body,
        [*slots, *w_proj.arrays, *w_mix.arrays, *probs, qkv],
        [
            *[shape_of((share // 2, features), BF)] * 2,
            shape_of((share, features), BF),
            shape_of((2 * share, 3 * span), BF),
            shape_of((1, 3 * span), F32),
        ],
        scratch=[pltpu.VMEM((2 * share, span), BF)],
        in_specs=[None] * HALVES + w_proj.specs() + w_mix.specs() + [None] * (len(places) + 1),
        name="attention_backward",
    )
    return {"other": outs[:2], "own": outs[2], "grad": outs[3], "sums": outs[4]}


def split_rows(refs, at, value):
    half = value.shape[0] // 2
    refs[0][:, at] = value[:half].astype(BF)
    refs[1][:, at] = value[half:].astype(BF)


def leave_terms(low, weight, product, share, others, part_own):
    for w, at in weight:
        done = product(low, w[...])
        part_own[:, at] = done[:share, :].astype(BF)
        split_rows(others, at, done[share:, :])


def feed_forward(order, slots, weights):
    w_grow, w_shrink, bias = weights
    share, features = slots[0].shape
    hidden = w_shrink.shape[0]

    def body(*refs):
        xs, refs = refs[:HALVES], refs[HALVES:]
        wg, refs = w_grow.take(refs)
        ws, refs = w_shrink.take(refs)
        b, *others, act, slope, part_own = refs
        value = None
        for w, at in wg:
            rows = jnp.concatenate([x[:, at] for x in xs], 0)
            term = dot(rows, w[...])
            value = term if value is None else value + term
        up = value + b[...]
        cdf = 0.5 * (1.0 + lax.erf(up * 0.7071067811865476))
        density = jnp.exp(-0.5 * up * up) * 0.3989422804014327
        low = (up * cdf).astype(BF)
        act[...] = low
        slope[...] = (cdf + up * density).astype(BF)
        leave_terms(low, ws, dot, share, others, part_own)

    outs = order.call(
        body,
        [*slots, *w_grow.arrays, *w_shrink.arrays, bias],
        [
            *[shape_of((share // 2, features), BF)] * 2,
            shape_of((2 * share, hidden), BF),
            shape_of((2 * share, hidden), BF),
            shape_of((share, features), BF),
        ],
        name="feed_forward",
        limit=FEED_LIMIT,
    )
    return {"other": outs[:2], "act": outs[2], "slope": outs[3], "own": outs[4]}


def feed_backward(order, slots, slope, weights):
    w_grow, w_shrink = weights
    share, features = slots[0].shape
    hidden = w_shrink.shape[0]

    def body(*refs):
        ds, refs = refs[:HALVES], refs[HALVES:]
        wg, refs = w_grow.take(refs)
        ws, refs = w_shrink.take(refs)
        tilt, *others, grad, sums, part_own = refs
        value = None
        for w, at in ws:
            rows = jnp.concatenate([d[:, at] for d in ds], 0)
            term = dot_t(rows, w[...])
            value = term if value is None else value + term
        low = (value * tilt[...].astype(F32)).astype(BF)
        grad[...] = low
        sums[...] = jnp.sum(low.astype(F32), 0, keepdims=True)
        leave_terms(low, wg, dot_t, share, others, part_own)

    outs = order.call(
        body,
        [*slots, *w_grow.arrays, *w_shrink.arrays, slope],
        [
            *[shape_of((share // 2, features), BF)] * 2,
            shape_of((2 * share, hidden), BF),
            shape_of((1, hidden), F32),
            shape_of((share, features), BF),
        ],
        name="feed_backward",
        limit=FEED_LIMIT,
    )
    return {"other": outs[:2], "grad": outs[2], "sums": outs[3], "own": outs[4]}


def weight_grad(order, pairs, part, parts, extra=None):
    features = pairs[0][0][0].shape[1]
    width = features // parts
    start, shards = (0, 1) if part == 0 else (1, parts - 1)
    flat, specs, total = [], [], 0
    for left, right, first, count in pairs:
        flat += [*left, *right]
        specs += [pl.BlockSpec((v.shape[0], width), lambda i: (0, start + i)) for v in left]
        specs += [pl.BlockSpec((v.shape[0], count), lambda i, at=first // count: (0, at)) for v in right]
        total += count
    more = 0 if extra is None else extra.shape[1]
    if more:
        flat.append(extra)
        specs.append(pl.BlockSpec((1, *extra.shape[1:]), lambda i: (start + i, 0, 0)))

    def body(*refs):
        out, at, column = refs[-1], 0, 0
        if more:
            out[0, width:, :] = refs[len(flat) - 1][0].astype(BF)
        for left, right, _, count in pairs:
            a = jnp.concatenate([r[...] for r in refs[at : at + len(left)]], 0)
            at += len(left)
            b = jnp.concatenate([r[...] for r in refs[at : at + len(right)]], 0)
            at += len(right)
            out[0, :width, column : column + count] = dot_rows(a, b).astype(BF)
            column += count

    return order.call(
        body,
        flat,
        [shape_of((shards, width + more, total), BF)],
        grid=(shards,),
        in_specs=specs,
        out_specs=[pl.BlockSpec((1, width + more, total), lambda i: (i, 0, 0))],
        name="weight_grad",
        limit=GRAD_LIMIT,
    )[0]


class Pipeline:
    def __init__(self, order):
        self.order = order
        self.line = lax.axis_size("dp") == 4
        self.waiting, self.pieces, self.at = [], [], 0

    def offer(self, others, own, finish):
        self.waiting.append({"others": others, "own": own, "finish": finish})

    def piece(self, at):
        return self.pieces[at] if 0 <= at < len(self.pieces) else None

    def step(self, last=False):
        size = lax.axis_size("fsdp")
        now = self.at
        self.at += 1
        oldest, older, old, new = (self.piece(now - 1 - back) for back in (3, 2, 1, 0))
        if last and self.line and oldest is not None:
            oldest["finish"](oldest["total"], oldest["back"])
            oldest = None
        sums = []
        if new is not None:
            sums.append(("sum", new, [new["own"], *new["came"]]))
        if self.line and old is not None:
            sums.append(("inner", old, [old["sum"], old["swapped"]]))
        if self.line and older is not None:
            sums.append(("total", older, [older["inner"], older["met"]]))
        if sums:
            send = [piece[0] for piece in sums] if self.line else []
            found = combine(self.order, [terms for *_, terms in sums], send)
            for (name, piece, _), value in zip(sums, found):
                piece[name] = value
        if not self.line and new is not None:
            total = lax.psum(new["sum"], "dp")
            new["finish"](total, total)
        elif self.line:
            if old is not None:
                old["met"] = lax.ppermute(old["inner"], "dp", [(1, 2), (2, 1)])
            if new is not None and older is not None:
                new["swapped"] = older["back"] = lax.ppermute(found[-1], "dp", [(0, 1), (1, 0), (2, 3), (3, 2)])
            elif new is not None:
                new["swapped"] = lax.ppermute(new["sum"], "dp", [(0, 1), (3, 2)])
            elif older is not None:
                older["back"] = lax.ppermute(older["total"], "dp", [(1, 0), (2, 3)])
        if self.waiting:
            piece = self.waiting.pop(0)
            piece["came"] = [to_fsdp(piece["others"][k], k + 1) for k in range(size - 1)]
            self.pieces.append(piece)
        else:
            self.pieces.append(None)
        if self.line and oldest is not None:
            oldest["finish"](oldest["total"], oldest["back"])

    def drain(self):
        while self.waiting or any(p is not None for p in self.pieces[max(self.at - 4, 0) :]):
            self.step(True)


def at_end():
    here = lax.axis_index("dp")
    return (here == 0) | (here == lax.axis_size("dp") - 1)


def combine(order, groups, names):
    width = groups[0][0].shape[1]
    rows = [terms[0].shape[0] for terms in groups]
    both = "sum" in names and "total" in names
    given = [v for terms in groups for v in terms]
    outputs = [shape_of((count, width), BF) for count in rows]
    if both:
        ends, inside = names.index("sum"), names.index("total")
        outputs.append(shape_of((max(rows[ends], rows[inside]), width), BF))

    def body(*refs):
        at, sums = 0, []
        for index, (terms, count) in enumerate(zip(groups, rows)):
            total = refs[at][...].astype(F32)
            for ref in refs[at + 1 : at + len(terms)]:
                total = total + ref[:count, :].astype(F32)
            at += len(terms)
            sums.append(total)
            refs[len(given) + index][...] = total.astype(BF)
        if both:
            a, b, send = sums[ends], sums[inside], refs[-1]
            short = min(rows[ends], rows[inside])
            send[:short, :] = jnp.where(at_end(), a[:short], b[:short]).astype(BF)
            if send.shape[0] > short:
                send[short:, :] = (a if rows[ends] > short else b)[short:].astype(BF)

    return order.call(body, given, outputs, name="combine")


def finish_piece(order, total, back, layer, rows, held, parts, name):
    more = total.shape[0] - rows
    width = total.shape[1]
    given = [v for v in held if v is not None]
    both = [total, back]
    scratch = []
    for shape, form, _, _, count in parts:
        if form == "kinds":
            scratch.append(pltpu.VMEM((shape[1], rows, count // shape[1]), F32))
        else:
            scratch.append(pltpu.VMEM((rows, count) if form == "columns" else (count, rows), F32))

    def body(*refs):
        outs = refs[len(both) + len(given) : len(both) + len(given) + len(parts)]
        rest = refs[len(both) + len(given) + len(parts) :]
        if more:
            extra, rest = rest[0], rest[1:]
        blocks, sems = rest[:-1], rest[-1]
        value = jnp.where(at_end(), refs[1][: total.shape[0], :].astype(F32), refs[0][...].astype(F32))
        if more:
            extra[...] = value[rows:]
            value = value[:rows]
        copies = []
        for at, (out, block, (shape, form, place, first, count)) in enumerate(zip(outs, blocks, parts)):
            if form == "kinds":
                span = count // shape[1]
                for g in range(shape[1]):
                    block[g] = value[:, first + g * span : first + (g + 1) * span]
                there = out.at[layer]
            elif form == "turned":
                block[...] = value[:, first : first + count].T
                there = out.at[layer, pl.ds(place, count), :]
            else:
                block[...] = value[:, first : first + count]
                there = out.at[layer, :, pl.ds(place, count)]
            copy = pltpu.make_async_copy(block, there, sems.at[at])
            copy.start()
            copies.append(copy)
        for copy in copies:
            copy.wait()

    alias, at = {}, 0
    for index, v in enumerate(held):
        if v is not None:
            alias[len(both) + at] = index
            at += 1
    return order.call(
        body,
        [*both, *given],
        [shape_of(shape, F32) for shape, *_ in parts] + ([shape_of((more, width), F32)] if more else []),
        scratch=[*scratch, pltpu.SemaphoreType.DMA((len(parts),))],
        in_specs=[None] * len(both) + [HELD] * len(given),
        out_specs=[HELD] * len(parts) + ([None] if more else []),
        alias=alias,
        name=name,
        limit=12,
    )


def sum_norm_rows(order, sums):
    streams = len(sums[0])
    features = sums[0][0].shape[1]

    def body(*refs):
        out = refs[-1]
        found = []
        for at in range(len(sums)):
            total = refs[at * streams][...]
            for ref in refs[at * streams + 1 : (at + 1) * streams]:
                total = total + ref[...]
            found.append(total)
        rows = [found[at][0:1] for at in range(2 * LAYERS)]
        for layer in range(LAYERS):
            one, two = found[2 * layer], found[2 * layer + 1]
            rows += [one[2:3], two[2:3], one[1:2], two[1:2]]
        for at, row in enumerate(rows):
            out[at : at + 1, :] = row

    return order.call(
        body,
        [v for group in sums for v in group],
        [shape_of((6 * LAYERS, features), F32)],
        name="sum_norm_rows",
    )[0]


def little_gradients(order, norms, grow, heads, span):
    size = lax.axis_size("fsdp")
    features = norms[0].shape[1]
    width = features // size
    columns = 3 * span
    hidden = grow[0][0].shape[1]
    streams = len(grow[0])

    def body(a, b, *refs):
        out = refs[-1]
        out[...] = jnp.zeros(out.shape, F32)
        total = a[...] + b[...]
        rows = 6 * LAYERS
        for k in range(size):
            out[k, :rows, :width] = total[:, k * width : (k + 1) * width]
        for layer in range(LAYERS):
            at = layer * streams
            up = sum(ref[...] for ref in refs[at : at + streams])
            at += LAYERS * streams
            qkv = sum(ref[...] for ref in refs[at : at + streams])
            for k in range(size):
                row = rows + 2 * layer
                rest = hidden - columns
                out[k, row : row + 1, :] = up[:, :columns]
                out[k, row + 1 : row + 2, :rest] = up[:, columns:]
                out[k, row + 1 : row + 2, rest : rest + span] = qkv[:, :span]
                out[k, row + 1 : row + 2, rest + span : rest + 2 * span] = qkv[:, 2 * span :]

    return order.call(
        body,
        [*norms, *[v for group in grow for v in group], *[v for group in heads for v in group]],
        [shape_of((size, 8 * LAYERS, columns), F32)],
        name="little_gradients",
    )[0]


FILLS = (0, 2, 2, 2, 2, 2, 2, 2)
STEPS = (0, 1, 1, 1, 1, 1, 1, 1)
MORE_STEPS = (0, 0, 0, 0, 0, 0, 0, 0)
GRAD_LIMIT = 12
ADD_FIRST = (0,) * 16
FEED_LIMIT = 12


def gather_halves(share):
    return [share, to_core(share)]


def per_device(
    activations, cotangent, lengths, w_qkv, w_out, w_up, w_down, b_qv, b_up, norm_gains, layer_biases
):
    size = lax.axis_size("fsdp")
    order = Order()
    kinds = range(len(STREAMS))

    smalls = (b_qv, b_up, norm_gains, layer_biases)
    flat = jnp.concatenate([value.reshape(-1) for value in smalls])
    pieces = [flat] + [from_fsdp(flat, step) for step in range(1, size)]

    def unpack(at):
        found, start = [], 0
        for value in smalls:
            found.append(pieces[at][start : start + value.size].reshape(value.shape))
            start += value.size
        return found

    unpacked = [unpack(at) for at in range(size)]
    bias_heads, bias_grow, gains, biases = (
        jnp.concatenate([u[i] for u in unpacked], -1).astype(F32) for i in range(4)
    )
    bias_heads, bias_grow = natural(bias_heads, 3), natural(bias_grow, 2)
    features = gains.shape[-1]
    vectors = jnp.concatenate([gains.reshape(-1, features), biases.reshape(-1, features)], 0)
    head_rows = [bias_heads[layer].reshape(2, -1) for layer in range(LAYERS)]
    grow_rows = [bias_grow[layer].reshape(1, -1) for layer in range(LAYERS)]

    weights = [
        [
            Weight(order, w_qkv, layer, 1),
            Weight(order, w_out, layer, 1),
            Weight(order, w_up, layer, 0),
            Weight(order, w_down, layer, 1),
        ]
        for layer in range(LAYERS)
    ]
    fetch(order, weights[0][:2])

    slots = deal_rows(order, activations)
    fetch(order, weights[1])
    residual = [(slots[s][0], None, None) for s in kinds]
    cotangent = copy_rows(order, cotangent)
    across = to_chip(cotangent)
    cotangents = [cotangent, to_core(cotangent), across, to_core(across)]

    order.pin([*pieces[1:], *weights[0][0].early, *weights[0][0].late, *weights[0][1].early, *weights[0][1].late])
    fetch(order, weights[0][2:3])

    def ahead(at):
        zero, one = weights
        waits = {
            1: lambda: zero[2].early,
            2: lambda: [*zero[3].early, *zero[2].late],
            3: lambda: [*one[0].early, *one[1].early],
            4: lambda: [*one[0].late, *one[1].late, *one[2].early],
            5: lambda: [*one[2].late, *one[3].early],
            6: lambda: one[3].late,
        }
        return waits[at]() if at in waits else []

    streams = len(STREAMS)
    kept = [{k: [None] * streams for k in ("x", "attended", "grown", "one", "two", "middle")} for _ in range(LAYERS)]
    terms = [None] * streams
    back_two, slots_two, fed = ([[None] * streams for _ in range(LAYERS)] for _ in range(3))
    back_one, slots_one, went = ([[None] * streams for _ in range(LAYERS)] for _ in range(3))

    def gain_at(layer, which):
        return 2 * layer + which

    def bias_at(layer, which):
        return 2 * LAYERS + 4 * layer + which

    def second_norm(layer, s):
        one = kept[layer]["one"][s]
        kept[layer]["two"][s] = norm_forward(
            order,
            terms[s],
            (one[1], gain_at(layer, 0), bias_at(layer, 2)),
            vectors,
            (bias_at(layer, 1), gain_at(layer, 1), bias_at(layer, 3)),
        )

    def attend(layer, s):
        def before():
            if layer > 0:
                second_norm(layer - 1, s)
                two = kept[layer - 1]["two"][s]
                slots[s] = gather_halves(two[0])
                residual[s] = (two[1], gain_at(layer - 1, 1), bias_at(layer - 1, 3))
            kept[layer]["x"][s] = slots[s]

        def products():
            w_proj, w_mix = weights[layer][:2]
            found = attention_forward(order, STREAMS[s], slots[s], (w_proj, w_mix, head_rows[layer]), lengths)
            kept[layer]["attended"][s] = found
            return found, []

        return before, products

    def feed(layer, s):
        def before():
            one = norm_forward(
                order, terms[s], residual[s], vectors, (bias_at(layer, 0), gain_at(layer, 0), bias_at(layer, 2))
            )
            kept[layer]["one"][s] = one
            kept[layer]["middle"][s] = gather_halves(one[0])

        def products():
            w_grow, w_shrink = weights[layer][2:]
            found = feed_forward(order, kept[layer]["middle"][s], (w_grow, w_shrink, grow_rows[layer]))
            kept[layer]["grown"][s] = found
            return found, []

        return before, products

    def feed_back(layer, s):
        def before():
            if layer + 1 == LAYERS:
                second_norm(layer, s)
                terms[s] = [shares[s]]
            two = kept[layer]["two"][s]
            back_two[layer][s] = norm_backward(order, terms[s], two[3], two[2], vectors, gain_at(layer, 1))
            slots_two[layer][s] = gather_halves(back_two[layer][s][0])

        def products():
            w_grow, w_shrink = weights[layer][2:]
            found = feed_backward(order, slots_two[layer][s], kept[layer]["grown"][s]["slope"], (w_grow, w_shrink))
            fed[layer][s] = found
            if s + 1 == streams:
                queue_feed(layer)
            return found, [back_two[layer][s][2]]

        return before, products

    def attend_back(layer, s):
        def before():
            one = kept[layer]["one"][s]
            back_one[layer][s] = norm_backward(order, terms[s], one[3], one[2], vectors, gain_at(layer, 0))
            slots_one[layer][s] = gather_halves(back_one[layer][s][0])

        def products():
            w_proj, w_mix = weights[layer][:2]
            state = kept[layer]
            found = attention_backward(order, STREAMS[s], slots_one[layer][s], (w_proj, w_mix), state["attended"][s])
            went[layer][s] = found
            if s + 1 == streams:
                queue_attend(layer)
            return found, [back_one[layer][s][2]]

        return before, products

    pipeline = Pipeline(order)
    fillers = []
    outputs = {}
    span, hidden = w_out.shape[1], w_down.shape[1]
    width = features // size
    shapes = {
        "proj": (LAYERS, 3, width, span),
        "mix": (LAYERS, span, width),
        "up": (LAYERS, width, hidden),
        "down": (LAYERS, hidden, width),
    }
    forms = {"proj": "kinds", "mix": "turned", "up": "columns", "down": "turned"}

    def queue(layer, sources, extra=None):
        pairs = [source[1:] for source in sources]
        starts = [sum(source[4] for source in sources[:i]) for i in range(len(sources))]
        parts = [
            (shapes[name], forms[name], first, start, count)
            for (name, _, _, first, count), start in zip(sources, starts)
        ]

        def finish(total, back):
            names = [source[0] for source in sources]
            found = finish_piece(
                order, total, back, layer, width, [outputs.get(n) for n in names], parts, "finish_" + names[0]
            )
            outputs.update(zip(names, found))
            if extra is not None:
                outputs["little"] = found[-1]

        found = {}

        def others():
            found["rows"] = None if extra is None else extra()
            rows = found["rows"]
            found["others"] = weight_grad(order, pairs, 1, size, rows)

        def own():
            rows = found["rows"]
            found["own"] = weight_grad(order, pairs, 0, size, rows)[0]
            pipeline.offer(found["others"], found["own"], finish)

        fillers.extend([others, own])

    def queue_feed(layer):
        state = kept[layer]
        down = [v for t in kinds for v in slots_two[layer][t]], [state["grown"][t]["act"] for t in kinds]
        up = [v for t in kinds for v in state["middle"][t]], [fed[layer][t]["grad"] for t in kinds]
        most, half = 3 * hidden // 4, hidden // 2
        queue(layer, [("down", *down, 0, most)])
        queue(layer, [("down", *down, most, hidden - most), ("up", *up, 0, half)])

    def queue_attend(layer):
        state = kept[layer]
        up = [v for t in kinds for v in state["middle"][t]], [fed[layer][t]["grad"] for t in kinds]
        mix = [v for t in kinds for v in slots_one[layer][t]], [state["attended"][t]["ctx"] for t in kinds]
        proj = [v for t in kinds for v in state["x"][t]], [went[layer][t]["grad"] for t in kinds]
        half = hidden // 2
        queue(layer, [("up", *up, half, half), ("mix", *mix, 0, span)])
        queue(layer, [("proj", *proj, 0, 3 * span)], None if layer > 0 else little_rows)

    def fill(count):
        for _ in range(count):
            if fillers:
                fillers.pop(0)()

    norm_sums = []

    def sum_norms():
        found = sum_norm_rows(
            order, [[back[layer][s][1] for s in kinds] for layer in range(LAYERS) for back in (back_one, back_two)]
        )
        norm_sums.extend([found, to_core(found)])

    def little_rows():
        return little_gradients(
            order,
            norm_sums,
            [[fed[layer][s]["sums"] for s in kinds] for layer in range(LAYERS)],
            [[went[layer][s]["sums"] for s in kinds] for layer in range(LAYERS)],
            span,
        )

    items = []
    for layer in range(LAYERS):
        items += [attend(layer, s) for s in kinds] + [feed(layer, s) for s in kinds]
    forward_items = len(items)
    for layer in reversed(range(LAYERS)):
        items += [feed_back(layer, s) for s in kinds] + [attend_back(layer, s) for s in kinds]
    items[0][0]()
    for at, (_, products) in enumerate(items):
        s = at % streams
        found, more = products()
        beside = [to_core(part) for part in found["other"]]
        if at >= forward_items:
            fill(FILLS[at - forward_items])
            for _ in range(STEPS[at - forward_items]):
                pipeline.step()
        early = ADD_FIRST[at]
        if early:
            low = add_send(order, found["own"], beside)
        order.pin(ahead(at + 1))
        if at == 0:
            fetch(order, weights[0][3:])
            shares = deal_share(order, cotangents)
        if at + 1 < len(items):
            items[at + 1][0]()
        if at == forward_items + 1:
            out_rows = gather_halves(jnp.concatenate([kept[-1]["two"][t][0] for t in kinds], 0))
        if at + 2 == len(items):
            sum_norms()
        if not early:
            low = add_send(order, found["own"], beside)
        terms[s] = [found["own"], *beside, to_chip(low), *more]
        for _ in range(MORE_STEPS[at - forward_items] if at >= forward_items else 0):
            pipeline.step()
    while fillers:
        fill(2)
        pipeline.step(True)
    layer_out = natural_share(order, out_rows, BF)
    pipeline.step(True)
    ends = [last_sum(order, terms[s]) for s in kinds]
    end_rows = gather_halves(jnp.concatenate(ends, 0))
    pipeline.step(True)
    input_grad = natural_share(order, end_rows, F32)
    pipeline.drain()

    little = outputs["little"]
    grad_gains = little[: 2 * LAYERS, :width].reshape(LAYERS, 2, width)
    grad_biases = little[2 * LAYERS : 6 * LAYERS, :width].reshape(LAYERS, 4, width)
    rest = little[6 * LAYERS : 8 * LAYERS].reshape(LAYERS, -1)
    here = lax.axis_index("fsdp")
    grow = rest[:, :hidden].reshape(bias_grow.shape)
    heads = rest[:, hidden : hidden + 2 * span].reshape(bias_heads.shape)
    part = grow.shape[-1] // size
    grow = lax.dynamic_slice_in_dim(grow, here * part, part, grow.ndim - 1)
    part = heads.shape[-1] // size
    heads = lax.dynamic_slice_in_dim(heads, here * part, part, heads.ndim - 1)
    return (
        layer_out,
        input_grad,
        outputs["proj"],
        outputs["mix"],
        outputs["up"],
        outputs["down"],
        heads,
        grow,
        grad_gains,
        grad_biases,
    )


def solution(mesh):
    in_specs = (
        P(("dp", "fsdp"), None),
        P(("dp", "fsdp", "tensor"), None),
        P(("dp", "fsdp")),
        P(None, None, "fsdp", "tensor"),
        P(None, "tensor", "fsdp"),
        P(None, "fsdp", "tensor"),
        P(None, "tensor", "fsdp"),
        P(None, None, "tensor", "fsdp"),
        P(None, "tensor", "fsdp"),
        P(None, None, "fsdp"),
        P(None, None, "fsdp"),
    )
    out_specs = (
        P(("dp", "fsdp", "tensor"), None),
        P(("dp", "fsdp", "tensor"), None),
        P(None, None, "fsdp", "tensor"),
        P(None, "tensor", "fsdp"),
        P(None, "fsdp", "tensor"),
        P(None, "tensor", "fsdp"),
        P(None, None, "tensor", "fsdp"),
        P(None, "tensor", "fsdp"),
        P(None, None, "fsdp"),
        P(None, None, "fsdp"),
    )
    return jax.shard_map(
        per_device, mesh=mesh, in_specs=in_specs, out_specs=out_specs, check_vma=False
    )
```

```python
import functools

import jax
import jax.numpy as jnp
from jax import lax
from jax.experimental import pallas as pl
from jax.experimental.pallas import tpu as pltpu
from jax.sharding import PartitionSpec as P

HEAD = 64
PAIR = 2 * HEAD
LAYERS = 2
LENGTHS = (512, 256, 128, 128, 128)
STARTS = (0, 512, 768, 896, 1024)
STREAMS = ((0,), (1, 2, 3, 4))
CUT = 2
HALVES = 2
BF = jnp.bfloat16
DP, FSDP, TENSOR = "dp", "fsdp", "tensor"
F32 = jnp.float32
MIB = 1 << 20
CORE_SWAP = [(0, 1), (1, 0), (2, 3), (3, 2)]
CHIP_SWAP = [(0, 2), (2, 0), (1, 3), (3, 1)]


def to_core(value):
    return lax.ppermute(value, TENSOR, CORE_SWAP)


def to_chip(value):
    return lax.ppermute(value, TENSOR, CHIP_SWAP)


def from_fsdp(value, step):
    size = lax.axis_size(FSDP)
    return lax.ppermute(value, FSDP, [((i + step) % size, i) for i in range(size)])


def to_fsdp(value, step):
    size = lax.axis_size(FSDP)
    return lax.ppermute(value, FSDP, [(i, (i + step) % size) for i in range(size)])


def own_first(whole, axis):
    size = lax.axis_size(FSDP)
    here = lax.axis_index(FSDP)
    width = whole.shape[axis] // size
    return jnp.concatenate(
        [lax.dynamic_slice_in_dim(whole, (here + k) % size * width, width, axis) for k in range(size)], axis
    )


def natural(relative, axis):
    size = lax.axis_size(FSDP)
    here = lax.axis_index(FSDP)
    width = relative.shape[axis] // size
    return jnp.concatenate(
        [
            lax.dynamic_slice_in_dim(relative, (k - here + size) % size * width, width, axis)
            for k in range(size)
        ],
        axis,
    )


def dot(left, right):
    return jnp.dot(left, right, preferred_element_type=F32)


def dot_t(left, right):
    return lax.dot_general(left, right, (((1,), (1,)), ((), ())), preferred_element_type=F32)


def dot_rows(left, right):
    return lax.dot_general(left, right, (((0,), (0,)), ((), ())), preferred_element_type=F32)


def share_rows(stream):
    return sum(LENGTHS[page] for page in stream) // HALVES


def page_places(stream):
    places, at = [], 0
    for page in stream:
        places.append((page, LENGTHS[page], at, at // HALVES))
        at += LENGTHS[page]
    return places


SCOPED = 8


class Order:
    def __init__(self):
        self.last = None
        self.pins = []

    def pin(self, arrays):
        self.pins.extend(v for v in arrays)

    def call(
        self,
        body,
        inputs,
        outputs,
        scratch=(),
        grid=(),
        in_specs=None,
        out_specs=None,
        name=None,
        limit=SCOPED,
        alias=None,
    ):
        pins, self.pins = self.pins, []
        count = len(inputs)
        in_specs = in_specs or [None] * count
        out_specs = out_specs or [None] * len(outputs)
        in_specs = [whole_of(v.shape, grid) if s is None else s for s, v in zip(in_specs, inputs)]
        out_specs = [whole_of(v.shape, grid) if s is None else s for s, v in zip(out_specs, outputs)]
        token = shape_of((8, 128), F32)
        inputs = list(inputs) + pins + ([] if self.last is None else [self.last])
        in_specs += [ANY] * (len(inputs) - count)
        extra = len(inputs) - count

        def kernel(*refs):
            given, refs = refs[:count], refs[count + extra :]
            outs, mark, own = refs[: len(outputs)], refs[len(outputs)], refs[len(outputs) + 1 :]
            mark[...] = jnp.zeros(mark.shape, F32)
            body(*given, *outs, *own)

        *result, self.last = pl.pallas_call(
            kernel,
            grid=grid,
            in_specs=in_specs,
            out_specs=[*out_specs, whole_of(token.shape, grid)],
            out_shape=[*outputs, token],
            scratch_shapes=list(scratch),
            input_output_aliases=alias or {},
            name=name,
            cost_estimate=pl.CostEstimate(flops=0, bytes_accessed=0, transcendentals=0),
            compiler_params=pltpu.CompilerParams(vmem_limit_bytes=limit * MIB),
        )(*inputs)
        return result


def whole_of(shape, grid):
    if not grid:
        return pl.BlockSpec(memory_space=pltpu.VMEM)
    return pl.BlockSpec(shape, lambda *at: (0,) * len(shape))


def shape_of(shape, dtype):
    return jax.ShapeDtypeStruct(tuple(shape), dtype)


SMEM = pl.BlockSpec(memory_space=pltpu.SMEM)
ANY = pl.BlockSpec(memory_space=pl.ANY)
HELD = pl.BlockSpec(memory_space=pltpu.HBM)


def core_index():
    return lax.rem(lax.axis_index(TENSOR), 2)


class Weight:
    def __init__(self, order, whole, layer, axis):
        self.order, self.whole, self.layer, self.axis = order, whole, layer, axis
        self.size = lax.axis_size(FSDP)
        shape = whole.shape[1:]
        width = shape[axis]
        self.halved = self.size == 2 and lax.axis_size(DP) % 2 == 0 and width % 256 == 0
        self.widths = [width] + ([width // 2] * 2 if self.halved else [width] * (self.size - 1))
        self.shape = shape

    def places(self):
        width = self.widths[0]
        if not self.halved:
            return [pl.ds(k * width, width) for k in range(self.size)]
        parity = lax.rem(lax.axis_index(DP), 2)
        half = width // 2
        return [
            pl.ds(0, width),
            pl.ds(pl.multiple_of(width + parity * half, 128), half),
            pl.ds(pl.multiple_of(width + (1 - parity) * half, 128), half),
        ]

    def start(self, own, half):
        if self.halved:
            self.early = [from_fsdp(half, 1)]
            size = lax.axis_size(DP)
            self.late = [lax.ppermute(self.early[0], DP, [(i, i ^ 1) for i in range(size)])]
        else:
            self.early = [from_fsdp(own, step) for step in range(1, self.size)]
            self.late = []
        self.arrays = [own, *self.early, *self.late]

    def specs(self):
        return [None] * len(self.arrays)

    def take(self, refs):
        count = len(self.arrays)
        return list(zip(refs[:count], self.places())), refs[count:]


def fetch(order, weights):
    outputs = []
    for w in weights:
        outputs.append(shape_of(w.shape, BF))
        if w.halved:
            shape = list(w.shape)
            shape[w.axis] //= 2
            outputs.append(shape_of(shape, BF))

    def body(*refs):
        outs, sems = list(refs[len(weights) : -1]), refs[-1]
        parity = lax.rem(lax.axis_index(DP), 2)
        copies = []
        for w, ref in zip(weights, refs):
            sources = [ref.at[w.layer]]
            if w.halved:
                half = w.widths[1]
                place = [slice(None)] * len(w.shape)
                place[w.axis] = pl.ds(pl.multiple_of(parity * half, 128), half)
                sources.append(ref.at[(w.layer, *place)])
            for source in sources:
                copy = pltpu.make_async_copy(source, outs.pop(0), sems.at[len(copies)])
                copy.start()
                copies.append(copy)
        for copy in copies:
            copy.wait()

    found = order.call(
        body,
        [w.whole for w in weights],
        outputs,
        scratch=[pltpu.SemaphoreType.DMA((len(outputs),))],
        in_specs=[HELD] * len(weights),
        name="fetch",
    )
    for w in weights:
        own = found.pop(0)
        w.start(own, found.pop(0) if w.halved else None)


def deal_rows(order, activations):
    features = activations.shape[1]
    size = lax.axis_size(FSDP)
    width = features // size

    def body(whole, *outs):
        here = core_index()
        mine = lax.axis_index(FSDP)
        for at, stream in enumerate(STREAMS):
            for slot in range(HALVES):
                out = outs[at * HALVES + slot]
                for page, length, _, offset in page_places(stream):
                    part = length // HALVES
                    row = pl.multiple_of(STARTS[page] + (here ^ slot) * part, 32)
                    for k in range(size):
                        column = pl.multiple_of(lax.rem(mine + k, size) * width, 128)
                        out[offset : offset + part, k * width : (k + 1) * width] = whole[
                            pl.ds(row, part), pl.ds(column, width)
                        ]

    outs = order.call(
        body,
        [activations],
        [shape_of((share_rows(stream), features), BF) for stream in STREAMS for _ in range(HALVES)],
        name="deal_rows",
    )
    return [outs[at * HALVES : (at + 1) * HALVES] for at in range(len(STREAMS))]


def copy_rows(order, rows):
    def body(a, out):
        out[...] = a[...]

    return order.call(body, [rows], [shape_of(rows.shape, rows.dtype)], name="copy_rows")[0]


def deal_share(order, slots):
    rows, features = slots[0].shape
    size = lax.axis_size(FSDP)
    width = features // size

    def body(a, b, c, d, *outs):
        whole = outs[-1]
        here = lax.axis_index(TENSOR)
        core = core_index()
        mine = lax.axis_index(FSDP)
        for slot, ref in enumerate((a, b, c, d)):
            whole[pl.ds(pl.multiple_of((here ^ slot) * rows, 32), rows), :] = ref[...]
        for at, stream in enumerate(STREAMS):
            for page, length, _, offset in page_places(stream):
                part = length // HALVES
                row = pl.multiple_of(STARTS[page] + core * part, 32)
                for k in range(size):
                    column = pl.multiple_of(lax.rem(mine + k, size) * width, 128)
                    outs[at][offset : offset + part, k * width : (k + 1) * width] = whole[
                        pl.ds(row, part), pl.ds(column, width)
                    ]

    return order.call(
        body,
        slots,
        [shape_of((share_rows(stream), features), BF) for stream in STREAMS],
        scratch=[pltpu.VMEM((rows * 4, features), BF)],
        name="deal_share",
    )


def natural_share(order, slots, dtype):
    rows, features = slots[0].shape
    share = rows // 2
    size = lax.axis_size(FSDP)
    width = features // size

    def body(a, b, out, whole):
        here = lax.axis_index(TENSOR)
        core = core_index()
        mine = lax.axis_index(FSDP)
        for slot, ref in enumerate((a, b)):
            first = 0
            for stream in STREAMS:
                for page, length, _, offset in page_places(stream):
                    part = length // HALVES
                    row = pl.multiple_of(STARTS[page] + (core ^ slot) * part, 32)
                    whole[pl.ds(row, part), :] = ref[first + offset : first + offset + part, :]
                first += share_rows(stream)
        own = pl.multiple_of(here * share, 32)
        for k in range(size):
            column = pl.multiple_of(lax.rem(mine + k, size) * width, 128)
            out[:, pl.ds(column, width)] = whole[pl.ds(own, share), k * width : (k + 1) * width].astype(dtype)

    return order.call(
        body,
        slots,
        [shape_of((share, features), dtype)],
        scratch=[pltpu.VMEM((rows * 2, features), BF)],
        name="natural_share",
    )[0]


def add_send(order, kept, came):
    def body(a, *refs):
        low, at = refs[-1], 0
        for ref in refs[:-1]:
            rows = slice(at, at + ref.shape[0])
            low[rows, :] = (a[rows, :].astype(F32) + ref[...].astype(F32)).astype(BF)
            at += ref.shape[0]

    return order.call(body, [kept, *came], [shape_of(kept.shape, BF)], name="add_send")[0]


def sum_terms(own, *refs):
    *pieces, across = refs
    beside = jnp.concatenate([ref[...] for ref in pieces], 0)
    return own[...].astype(F32) + beside.astype(F32) + across[...].astype(F32)


def row_of(ref, at):
    return ref[at : at + 1, :]


def norm_forward(order, terms, residual, vectors, rows_of_vectors):
    rows, features = terms[0].shape
    bias_at, gain_at, shift_at = rows_of_vectors

    def body(*refs):
        parts, (before, vec, *lows, normed, inverse, kept) = refs[: len(terms)], refs[len(terms) :]
        value = before[...].astype(F32)
        if residual[1] is not None:
            value = value * row_of(vec, residual[1]) + row_of(vec, residual[2])
        value = value + sum_terms(*parts) + row_of(vec, bias_at)
        center = value - jnp.mean(value, -1, keepdims=True)
        scale = lax.rsqrt(jnp.mean(center * center, -1, keepdims=True) + 1e-05)
        unit = center * scale
        normed[...] = unit
        kept[...] = unit.astype(BF)
        inverse[...] = scale
        split_rows(lows, slice(None), unit * row_of(vec, gain_at) + row_of(vec, shift_at))

    outs = order.call(
        body,
        [*terms, residual[0], vectors],
        [
            *[shape_of((rows // CUT, features), BF)] * CUT,
            shape_of((rows, features), F32),
            shape_of((rows, 1), F32),
            shape_of((rows, features), BF),
        ],
        name="norm_forward",
    )
    return [outs[:CUT], *outs[CUT:]]


def norm_backward(order, terms, normed, inverse, vectors, gain_at):
    rows, features = normed.shape
    count = len(terms)

    def body(*refs):
        unit, scale, vec, *lows, sums, wide = refs[count:]
        total = refs[count - 1][...].astype(F32)
        if count > 1:
            total = total + sum_terms(*refs[: count - 1])
        n = unit[...].astype(F32)
        grad = total * row_of(vec, gain_at)
        mean_one = jnp.mean(grad, -1, keepdims=True)
        mean_two = jnp.mean(grad * n, -1, keepdims=True)
        result = scale[...] * (grad - mean_one - n * mean_two)
        wide[...] = result
        split_rows(lows, slice(None), result)
        sums[0:1, :] = jnp.sum(total * n, 0, keepdims=True)
        sums[1:2, :] = jnp.sum(total, 0, keepdims=True)
        sums[2:3, :] = jnp.sum(result, 0, keepdims=True)

    outs = order.call(
        body,
        [*terms, normed, inverse, vectors],
        [
            *[shape_of((rows // CUT, features), BF)] * CUT,
            shape_of((3, features), F32),
            shape_of((rows, features), F32),
        ],
        name="norm_backward",
    )
    return [outs[:CUT], *outs[CUT:]]


def last_sum(order, terms):
    def body(*refs):
        refs[-1][...] = (refs[-2][...] + sum_terms(*refs[:-2])).astype(BF)

    return order.call(body, terms, [shape_of(terms[0].shape, BF)], name="last_sum")[0]


def head_mask(which):
    lane = lax.broadcasted_iota(jnp.int32, (1, PAIR), 1)
    return (lane < HEAD) if which == 0 else (lane >= HEAD)


def key_bias(length, limit):
    part = length // HALVES
    place = lax.broadcasted_iota(jnp.int32, (1, length), 1)
    half = (place // part) ^ core_index()
    return jnp.where(half * part + place % part < limit, 0.0, -1000000000.0).astype(F32)


def put_rows(ref, lanes, value, row, part, share, offset):
    done = 0
    while done < value.shape[0]:
        at = row + done
        count = min(part - at % part, value.shape[0] - done)
        first = (at // part) * share + offset + at % part
        ref[first : first + count, lanes] = value[done : done + count]
        done += count


def attention_forward(order, stream, slots, weights, lengths):
    w_proj, w_mix, bias_rows = weights
    share, features = slots_shape(slots)
    span = w_mix.shape[0]
    heads = span // HEAD
    places = page_places(stream)

    def body(*refs):
        xs, refs = refs[: len(slots)], refs[len(slots) :]
        wp, refs = w_proj.take(refs)
        wm, refs = w_mix.take(refs)
        bias, limits, refs = refs[0], refs[1], refs[2:]
        others, (part_own, qkv, ctx), probs = refs[:CUT], refs[CUT : CUT + 3], refs[CUT + 3 :]
        for kind in range(3):
            value = None
            for w, at in wp:
                rows = jnp.concatenate([x[:, at] for x in xs], 0)
                term = dot(rows, w[kind])
                value = term if value is None else value + term
            if kind == 0:
                value = value + bias[0:1, :]
            elif kind == 2:
                value = value + bias[1:2, :]
            value = value.astype(BF)
            if kind == 0:
                value = value * jnp.asarray(HEAD ** (-0.5), BF)
            for _, length, base, offset in places:
                part = length // HALVES
                for slot in range(HALVES):
                    qkv[base + slot * part : base + (slot + 1) * part, kind * span : (kind + 1) * span] = value[
                        slot * share + offset : slot * share + offset + part, :
                    ]
        for index, (page, length, base, offset) in enumerate(places):
            part = length // HALVES
            shut = key_bias(length, limits[page])
            step = min(length, 256)
            for pair in range(heads // 2):
                lanes = slice(pair * PAIR, (pair + 1) * PAIR)
                keys = qkv[base : base + length, span + pair * PAIR : span + (pair + 1) * PAIR]
                values = qkv[base : base + length, 2 * span + pair * PAIR : 2 * span + (pair + 1) * PAIR]
                for row in range(0, length, step):
                    queries = qkv[base + row : base + row + step, lanes]
                    found = []
                    for which in range(2):
                        masked = queries * head_mask(which).astype(BF)
                        scores = dot_t(masked, keys) + shut
                        peak = jnp.max(scores, -1, keepdims=True)
                        raised = jnp.exp(scores - peak)
                        chance = raised * (1.0 / jnp.sum(raised, -1, keepdims=True))
                        chance = chance.astype(BF)
                        probs[index][2 * pair + which, row : row + step, :] = chance
                        found.append(dot(chance, values))
                    both = jnp.where(head_mask(0), found[0], found[1]).astype(BF)
                    put_rows(ctx, lanes, both, row, part, share, offset)
        for w, at in wm:
            value = dot(ctx[...], w[...])
            part_own[:, at] = value[:share].astype(BF)
            split_rows(others, at, value[share:])

    outs = order.call(
        body,
        [*slots, *w_proj.arrays, *w_mix.arrays, bias_rows, lengths],
        [
            *[shape_of((share // CUT, features), BF)] * CUT,
            shape_of((share, features), BF),
            shape_of((2 * share, 3 * span), BF),
            shape_of((2 * share, span), BF),
        ]
        + [shape_of((heads, length, length), BF) for _, length, _, _ in places],
        in_specs=[None] * len(slots) + w_proj.specs() + w_mix.specs() + [None, SMEM],
        name="attention_forward",
    )
    return {"other": outs[:CUT], "own": outs[CUT], "qkv": outs[CUT + 1], "ctx": outs[CUT + 2], "probs": outs[CUT + 3 :]}


def attention_backward(order, stream, slots, weights, state):
    w_proj, w_mix = weights
    probs, qkv = state["probs"], state["qkv"]
    share, features = slots_shape(slots)
    span = w_mix.shape[0]
    heads = span // HEAD
    places = page_places(stream)

    def body(*refs):
        ds, refs = refs[: len(slots)], refs[len(slots) :]
        wp, refs = w_proj.take(refs)
        wm, refs = w_mix.take(refs)
        chances, refs = refs[: len(places)], refs[len(places) :]
        qkv_ref, *others, part_own, grad, sums, low = refs
        value = None
        for w, at in wm:
            rows = jnp.concatenate([d[:, at] for d in ds], 0)
            term = dot_t(rows, w[...])
            value = term if value is None else value + term
        value = value.astype(BF)
        for _, length, base, offset in places:
            part = length // HALVES
            for slot in range(HALVES):
                low[base + slot * part : base + (slot + 1) * part, :] = value[
                    slot * share + offset : slot * share + offset + part, :
                ]
        for index, (page, length, base, offset) in enumerate(places):
            part = length // HALVES
            step = min(length, 256)
            for pair in range(heads // 2):
                lanes = slice(pair * PAIR, (pair + 1) * PAIR)
                keys = qkv_ref[base : base + length, span + pair * PAIR : span + (pair + 1) * PAIR]
                values = qkv_ref[base : base + length, 2 * span + pair * PAIR : 2 * span + (pair + 1) * PAIR]
                grad_keys, grad_values = [None, None], [None, None]
                for row in range(0, length, step):
                    queries = qkv_ref[base + row : base + row + step, lanes]
                    grad_rows = low[base + row : base + row + step, lanes]
                    found = []
                    for which in range(2):
                        chance = chances[index][2 * pair + which, row : row + step, :]
                        wide = chance.astype(F32)
                        back = dot_t(grad_rows * head_mask(which).astype(BF), values)
                        inner = jnp.sum(wide * back, -1, keepdims=True)
                        grad_scores = (wide * (back - inner)).astype(BF)
                        found.append(dot(grad_scores, keys))
                        of_keys = dot_rows(grad_scores, queries)
                        of_values = dot_rows(chance, grad_rows)
                        first = grad_keys[which] is None
                        grad_keys[which] = of_keys if first else grad_keys[which] + of_keys
                        grad_values[which] = of_values if first else grad_values[which] + of_values
                    both = (jnp.where(head_mask(0), found[0], found[1]) * HEAD ** (-0.5)).astype(BF)
                    put_rows(grad, lanes, both, row, part, share, offset)
                for kind, parts in ((1, grad_keys), (2, grad_values)):
                    both = jnp.where(head_mask(0), parts[0], parts[1]).astype(BF)
                    for slot in range(HALVES):
                        grad[
                            slot * share + offset : slot * share + offset + part,
                            kind * span + pair * PAIR : kind * span + (pair + 1) * PAIR,
                        ] = both[slot * part : (slot + 1) * part, :]
        for w, at in wp:
            value = None
            for kind in range(3):
                term = dot_t(grad[:, kind * span : (kind + 1) * span], w[kind])
                value = term if value is None else value + term
            part_own[:, at] = value[:share].astype(BF)
            split_rows(others, at, value[share:])
        sums[...] = jnp.sum(grad[...].astype(F32), 0, keepdims=True)

    outs = order.call(
        body,
        [*slots, *w_proj.arrays, *w_mix.arrays, *probs, qkv],
        [
            *[shape_of((share // CUT, features), BF)] * CUT,
            shape_of((share, features), BF),
            shape_of((2 * share, 3 * span), BF),
            shape_of((1, 3 * span), F32),
        ],
        scratch=[pltpu.VMEM((2 * share, span), BF)],
        in_specs=[None] * len(slots) + w_proj.specs() + w_mix.specs() + [None] * (len(places) + 1),
        name="attention_backward",
    )
    return {"other": outs[:CUT], "own": outs[CUT], "grad": outs[CUT + 1], "sums": outs[CUT + 2]}


def slots_shape(slots):
    return sum(v.shape[0] for v in slots) // 2, slots[0].shape[1]


def split_rows(refs, at, value):
    count = value.shape[0] // CUT
    for i, ref in enumerate(refs):
        ref[:, at] = value[i * count : (i + 1) * count].astype(BF)


def leave_terms(low, weight, product, share, others, part_own):
    for w, at in weight:
        done = product(low, w[...])
        part_own[:, at] = done[:share, :].astype(BF)
        split_rows(others, at, done[share:, :])


def feed_forward(order, slots, weights):
    w_grow, w_shrink, bias = weights
    share, features = slots_shape(slots)
    hidden = w_shrink.shape[0]

    def body(*refs):
        xs, refs = refs[: len(slots)], refs[len(slots) :]
        wg, refs = w_grow.take(refs)
        ws, refs = w_shrink.take(refs)
        b, *others, act, slope, part_own = refs
        value = None
        for w, at in wg:
            rows = jnp.concatenate([x[:, at] for x in xs], 0)
            term = dot(rows, w[...])
            value = term if value is None else value + term
        up = value + b[...]
        cdf = 0.5 * (1.0 + lax.erf(up * 0.7071067811865476))
        density = jnp.exp(-0.5 * up * up) * 0.3989422804014327
        low = (up * cdf).astype(BF)
        act[...] = low
        slope[...] = (cdf + up * density).astype(BF)
        leave_terms(low, ws, dot, share, others, part_own)

    outs = order.call(
        body,
        [*slots, *w_grow.arrays, *w_shrink.arrays, bias],
        [
            *[shape_of((share // CUT, features), BF)] * CUT,
            shape_of((2 * share, hidden), BF),
            shape_of((2 * share, hidden), BF),
            shape_of((share, features), BF),
        ],
        name="feed_forward",
        limit=FEED_LIMIT,
    )
    return {"other": outs[:CUT], "act": outs[CUT], "slope": outs[CUT + 1], "own": outs[CUT + 2]}


def feed_backward(order, slots, slope, weights):
    w_grow, w_shrink = weights
    share, features = slots_shape(slots)
    hidden = w_shrink.shape[0]

    def body(*refs):
        ds, refs = refs[: len(slots)], refs[len(slots) :]
        wg, refs = w_grow.take(refs)
        ws, refs = w_shrink.take(refs)
        tilt, *others, grad, sums, part_own = refs
        value = None
        for w, at in ws:
            rows = jnp.concatenate([d[:, at] for d in ds], 0)
            term = dot_t(rows, w[...])
            value = term if value is None else value + term
        low = (value * tilt[...].astype(F32)).astype(BF)
        grad[...] = low
        sums[...] = jnp.sum(low.astype(F32), 0, keepdims=True)
        leave_terms(low, wg, dot_t, share, others, part_own)

    outs = order.call(
        body,
        [*slots, *w_grow.arrays, *w_shrink.arrays, slope],
        [
            *[shape_of((share // CUT, features), BF)] * CUT,
            shape_of((2 * share, hidden), BF),
            shape_of((1, hidden), F32),
            shape_of((share, features), BF),
        ],
        name="feed_backward",
        limit=FEED_LIMIT,
    )
    return {"other": outs[:CUT], "grad": outs[CUT], "sums": outs[CUT + 1], "own": outs[CUT + 2]}


def weight_grad(order, pairs, part, parts, extra=None):
    features = pairs[0][0][0].shape[1]
    width = features // parts
    start, shards = (0, 1) if part == 0 else (1, parts - 1)
    flat, specs, total = [], [], 0
    for left, right, first, count in pairs:
        flat += [*left, *right]
        specs += [pl.BlockSpec((v.shape[0], width), lambda i: (0, start + i)) for v in left]
        specs += [pl.BlockSpec((v.shape[0], count), lambda i, at=first // count: (0, at)) for v in right]
        total += count
    more = 0 if extra is None else extra.shape[1]
    if more:
        flat.append(extra)
        specs.append(pl.BlockSpec((1, *extra.shape[1:]), lambda i: (start + i, 0, 0)))

    def body(*refs):
        out, at, column = refs[-1], 0, 0
        if more:
            out[0, width:, :] = refs[len(flat) - 1][0].astype(BF)
        for left, right, _, count in pairs:
            a = jnp.concatenate([r[...] for r in refs[at : at + len(left)]], 0)
            at += len(left)
            b = jnp.concatenate([r[...] for r in refs[at : at + len(right)]], 0)
            at += len(right)
            out[0, :width, column : column + count] = dot_rows(a, b).astype(BF)
            column += count

    return order.call(
        body,
        flat,
        [shape_of((shards, width + more, total), BF)],
        grid=(shards,),
        in_specs=specs,
        out_specs=[pl.BlockSpec((1, width + more, total), lambda i: (i, 0, 0))],
        name="weight_grad",
        limit=GRAD_LIMIT,
    )[0]


class Pipeline:
    def __init__(self, order):
        self.order = order
        self.line = lax.axis_size(DP) == 4
        self.waiting, self.pieces, self.at = [], [], 0

    def offer(self, others, own, finish):
        self.waiting.append({"others": others, "own": own, "finish": finish})

    def piece(self, at):
        return self.pieces[at] if 0 <= at < len(self.pieces) else None

    def step(self, last=False):
        size = lax.axis_size(FSDP)
        now = self.at
        self.at += 1
        oldest, older, old, new = (self.piece(now - 1 - back) for back in (3, 2, 1, 0))
        if last and self.line and oldest is not None:
            oldest["finish"](oldest["total"], oldest["back"])
            oldest = None
        sums = []
        if new is not None:
            sums.append(("sum", new, [new["own"], *new["came"]]))
        if self.line and old is not None:
            sums.append(("inner", old, [old["sum"], old["swapped"]]))
        if self.line and older is not None:
            sums.append(("total", older, [older["inner"], older["met"]]))
        if sums:
            send = [piece[0] for piece in sums] if self.line else []
            found = combine(self.order, [terms for *_, terms in sums], send)
            for (name, piece, _), value in zip(sums, found):
                piece[name] = value
        if not self.line and new is not None:
            total = lax.psum(new["sum"], DP)
            new["finish"](total, total)
        elif self.line:
            if old is not None:
                old["met"] = lax.ppermute(old["inner"], DP, [(1, 2), (2, 1)])
            if new is not None and older is not None:
                new["swapped"] = older["back"] = lax.ppermute(found[-1], DP, [(0, 1), (1, 0), (2, 3), (3, 2)])
            elif new is not None:
                new["swapped"] = lax.ppermute(new["sum"], DP, [(0, 1), (3, 2)])
            elif older is not None:
                older["back"] = lax.ppermute(older["total"], DP, [(1, 0), (2, 3)])
        if self.waiting:
            piece = self.waiting.pop(0)
            piece["came"] = [to_fsdp(piece["others"][k], k + 1) for k in range(size - 1)]
            self.pieces.append(piece)
        else:
            self.pieces.append(None)
        if self.line and oldest is not None:
            oldest["finish"](oldest["total"], oldest["back"])

    def drain(self):
        while self.waiting or any(p is not None for p in self.pieces[max(self.at - 4, 0) :]):
            self.step(True)


def at_end():
    here = lax.axis_index(DP)
    return (here == 0) | (here == lax.axis_size(DP) - 1)


def combine(order, groups, names):
    width = groups[0][0].shape[1]
    rows = [terms[0].shape[0] for terms in groups]
    both = "sum" in names and "total" in names
    given = [v for terms in groups for v in terms]
    outputs = [shape_of((count, width), BF) for count in rows]
    if both:
        ends, inside = names.index("sum"), names.index("total")
        outputs.append(shape_of((max(rows[ends], rows[inside]), width), BF))

    def body(*refs):
        at, sums = 0, []
        for index, (terms, count) in enumerate(zip(groups, rows)):
            total = refs[at][...].astype(F32)
            for ref in refs[at + 1 : at + len(terms)]:
                total = total + ref[:count, :].astype(F32)
            at += len(terms)
            sums.append(total)
            refs[len(given) + index][...] = total.astype(BF)
        if both:
            a, b, send = sums[ends], sums[inside], refs[-1]
            short = min(rows[ends], rows[inside])
            send[:short, :] = jnp.where(at_end(), a[:short], b[:short]).astype(BF)
            if send.shape[0] > short:
                send[short:, :] = (a if rows[ends] > short else b)[short:].astype(BF)

    return order.call(body, given, outputs, name="combine")


def finish_piece(order, total, back, layer, rows, held, parts, name):
    more = total.shape[0] - rows
    width = total.shape[1]
    given = [v for v in held if v is not None]
    both = [total, back]
    scratch = []
    for shape, form, _, _, count in parts:
        if form == "kinds":
            scratch.append(pltpu.VMEM((shape[1], rows, count // shape[1]), F32))
        else:
            scratch.append(pltpu.VMEM((rows, count) if form == "columns" else (count, rows), F32))

    def body(*refs):
        outs = refs[len(both) + len(given) : len(both) + len(given) + len(parts)]
        rest = refs[len(both) + len(given) + len(parts) :]
        if more:
            extra, rest = rest[0], rest[1:]
        blocks, sems = rest[:-1], rest[-1]
        value = jnp.where(at_end(), refs[1][: total.shape[0], :].astype(F32), refs[0][...].astype(F32))
        if more:
            extra[...] = value[rows:]
            value = value[:rows]
        copies = []
        for at, (out, block, (shape, form, place, first, count)) in enumerate(zip(outs, blocks, parts)):
            if form == "kinds":
                span = count // shape[1]
                for g in range(shape[1]):
                    block[g] = value[:, first + g * span : first + (g + 1) * span]
                there = out.at[layer]
            elif form == "turned":
                block[...] = value[:, first : first + count].T
                there = out.at[layer, pl.ds(place, count), :]
            else:
                block[...] = value[:, first : first + count]
                there = out.at[layer, :, pl.ds(place, count)]
            copy = pltpu.make_async_copy(block, there, sems.at[at])
            copy.start()
            copies.append(copy)
        for copy in copies:
            copy.wait()

    alias, at = {}, 0
    for index, v in enumerate(held):
        if v is not None:
            alias[len(both) + at] = index
            at += 1
    return order.call(
        body,
        [*both, *given],
        [shape_of(shape, F32) for shape, *_ in parts] + ([shape_of((more, width), F32)] if more else []),
        scratch=[*scratch, pltpu.SemaphoreType.DMA((len(parts),))],
        in_specs=[None] * len(both) + [HELD] * len(given),
        out_specs=[HELD] * len(parts) + ([None] if more else []),
        alias=alias,
        name=name,
        limit=12,
    )


def sum_norm_rows(order, sums):
    streams = len(sums[0])
    features = sums[0][0].shape[1]

    def body(*refs):
        out = refs[-1]
        found = []
        for at in range(len(sums)):
            total = refs[at * streams][...]
            for ref in refs[at * streams + 1 : (at + 1) * streams]:
                total = total + ref[...]
            found.append(total)
        rows = [found[at][0:1] for at in range(2 * LAYERS)]
        for layer in range(LAYERS):
            one, two = found[2 * layer], found[2 * layer + 1]
            rows += [one[2:3], two[2:3], one[1:2], two[1:2]]
        for at, row in enumerate(rows):
            out[at : at + 1, :] = row

    return order.call(
        body,
        [v for group in sums for v in group],
        [shape_of((6 * LAYERS, features), F32)],
        name="sum_norm_rows",
    )[0]


def little_gradients(order, norms, grow, heads, span):
    size = lax.axis_size(FSDP)
    features = norms[0].shape[1]
    width = features // size
    columns = 3 * span
    hidden = grow[0][0].shape[1]
    streams = len(grow[0])

    def body(a, b, *refs):
        out = refs[-1]
        out[...] = jnp.zeros(out.shape, F32)
        total = a[...] + b[...]
        rows = 6 * LAYERS
        for k in range(size):
            out[k, :rows, :width] = total[:, k * width : (k + 1) * width]
        for layer in range(LAYERS):
            at = layer * streams
            up = sum(ref[...] for ref in refs[at : at + streams])
            at += LAYERS * streams
            qkv = sum(ref[...] for ref in refs[at : at + streams])
            for k in range(size):
                row = rows + 2 * layer
                rest = hidden - columns
                out[k, row : row + 1, :] = up[:, :columns]
                out[k, row + 1 : row + 2, :rest] = up[:, columns:]
                out[k, row + 1 : row + 2, rest : rest + span] = qkv[:, :span]
                out[k, row + 1 : row + 2, rest + span : rest + 2 * span] = qkv[:, 2 * span :]

    return order.call(
        body,
        [*norms, *[v for group in grow for v in group], *[v for group in heads for v in group]],
        [shape_of((size, 8 * LAYERS, columns), F32)],
        name="little_gradients",
    )[0]


FILLS = (0, 2, 2, 2, 2, 2, 2, 2)
STEPS = (0, 1, 1, 1, 1, 1, 1, 1)
MORE_STEPS = (0, 0, 0, 0, 0, 0, 0, 0)
GRAD_LIMIT = 12
ADD_FIRST = (1,) * 16
FEED_LIMIT = 12


def gather_halves(pieces):
    return [*pieces, *[to_core(piece) for piece in pieces]]


def per_device(
    activations, cotangent, lengths, w_qkv, w_out, w_up, w_down, b_qv, b_up, norm_gains, layer_biases
):
    size = lax.axis_size(FSDP)
    order = Order()
    kinds = range(len(STREAMS))

    smalls = (b_qv, b_up, norm_gains, layer_biases)
    flat = jnp.concatenate([value.reshape(-1) for value in smalls])
    pieces = [flat] + [from_fsdp(flat, step) for step in range(1, size)]

    def unpack(at):
        found, start = [], 0
        for value in smalls:
            found.append(pieces[at][start : start + value.size].reshape(value.shape))
            start += value.size
        return found

    unpacked = [unpack(at) for at in range(size)]
    bias_heads, bias_grow, gains, biases = (
        jnp.concatenate([u[i] for u in unpacked], -1).astype(F32) for i in range(4)
    )
    bias_heads, bias_grow = natural(bias_heads, 3), natural(bias_grow, 2)
    features = gains.shape[-1]
    vectors = jnp.concatenate([gains.reshape(-1, features), biases.reshape(-1, features)], 0)
    head_rows = [bias_heads[layer].reshape(2, -1) for layer in range(LAYERS)]
    grow_rows = [bias_grow[layer].reshape(1, -1) for layer in range(LAYERS)]

    weights = [
        [
            Weight(order, w_qkv, layer, 1),
            Weight(order, w_out, layer, 1),
            Weight(order, w_up, layer, 0),
            Weight(order, w_down, layer, 1),
        ]
        for layer in range(LAYERS)
    ]
    fetch(order, weights[0][:2])

    slots = deal_rows(order, activations)
    order.pin([*weights[0][0].early, *weights[0][1].early])
    fetch(order, weights[1])
    residual = [(slots[s][0], None, None) for s in kinds]
    cotangent = copy_rows(order, cotangent)
    across = to_chip(cotangent)
    cotangents = [cotangent, to_core(cotangent), across, to_core(across)]

    order.pin([*weights[0][0].early, *weights[0][0].late, *weights[0][1].early, *weights[0][1].late])
    fetch(order, weights[0][2:3])

    def ahead(at):
        zero, one = weights
        waits = {
            1: lambda: zero[2].early,
            2: lambda: [*zero[3].early, *zero[2].late, *one[0].early, *one[1].early],
            3: lambda: [*one[0].late, *one[1].late],
            4: lambda: one[2].early,
            5: lambda: [*one[2].late, *one[3].early],
            6: lambda: one[3].late,
        }
        return waits[at]() if at in waits else []

    streams = len(STREAMS)
    kept = [{k: [None] * streams for k in ("x", "attended", "grown", "one", "two", "middle")} for _ in range(LAYERS)]
    terms = [None] * streams
    back_two, slots_two, fed = ([[None] * streams for _ in range(LAYERS)] for _ in range(3))
    back_one, slots_one, went = ([[None] * streams for _ in range(LAYERS)] for _ in range(3))

    def gain_at(layer, which):
        return 2 * layer + which

    def bias_at(layer, which):
        return 2 * LAYERS + 4 * layer + which

    def second_norm(layer, s):
        one = kept[layer]["one"][s]
        kept[layer]["two"][s] = norm_forward(
            order,
            terms[s],
            (one[1], gain_at(layer, 0), bias_at(layer, 2)),
            vectors,
            (bias_at(layer, 1), gain_at(layer, 1), bias_at(layer, 3)),
        )

    def attend(layer, s):
        def before():
            if layer > 0:
                second_norm(layer - 1, s)
                two = kept[layer - 1]["two"][s]
                slots[s] = gather_halves(two[0])
                residual[s] = (two[1], gain_at(layer - 1, 1), bias_at(layer - 1, 3))
            kept[layer]["x"][s] = slots[s]

        def products():
            w_proj, w_mix = weights[layer][:2]
            found = attention_forward(order, STREAMS[s], slots[s], (w_proj, w_mix, head_rows[layer]), lengths)
            kept[layer]["attended"][s] = found
            return found, []

        return before, products

    def feed(layer, s):
        def before():
            one = norm_forward(
                order, terms[s], residual[s], vectors, (bias_at(layer, 0), gain_at(layer, 0), bias_at(layer, 2))
            )
            kept[layer]["one"][s] = one
            kept[layer]["middle"][s] = gather_halves(one[0])

        def products():
            w_grow, w_shrink = weights[layer][2:]
            found = feed_forward(order, kept[layer]["middle"][s], (w_grow, w_shrink, grow_rows[layer]))
            kept[layer]["grown"][s] = found
            return found, []

        return before, products

    def feed_back(layer, s):
        def before():
            if layer + 1 == LAYERS:
                second_norm(layer, s)
                terms[s] = [shares[s]]
            two = kept[layer]["two"][s]
            back_two[layer][s] = norm_backward(order, terms[s], two[3], two[2], vectors, gain_at(layer, 1))
            slots_two[layer][s] = gather_halves(back_two[layer][s][0])

        def products():
            w_grow, w_shrink = weights[layer][2:]
            found = feed_backward(order, slots_two[layer][s], kept[layer]["grown"][s]["slope"], (w_grow, w_shrink))
            fed[layer][s] = found
            if s + 1 == streams:
                queue_feed(layer)
            return found, [back_two[layer][s][2]]

        return before, products

    def attend_back(layer, s):
        def before():
            one = kept[layer]["one"][s]
            back_one[layer][s] = norm_backward(order, terms[s], one[3], one[2], vectors, gain_at(layer, 0))
            slots_one[layer][s] = gather_halves(back_one[layer][s][0])

        def products():
            w_proj, w_mix = weights[layer][:2]
            state = kept[layer]
            found = attention_backward(order, STREAMS[s], slots_one[layer][s], (w_proj, w_mix), state["attended"][s])
            went[layer][s] = found
            if s + 1 == streams:
                queue_attend(layer)
            return found, [back_one[layer][s][2]]

        return before, products

    pipeline = Pipeline(order)
    fillers = []
    outputs = {}
    span, hidden = w_out.shape[1], w_down.shape[1]
    width = features // size
    shapes = {
        "proj": (LAYERS, 3, width, span),
        "mix": (LAYERS, span, width),
        "up": (LAYERS, width, hidden),
        "down": (LAYERS, hidden, width),
    }
    forms = {"proj": "kinds", "mix": "turned", "up": "columns", "down": "turned"}

    def queue(layer, sources, extra=None):
        pairs = [source[1:] for source in sources]
        starts = [sum(source[4] for source in sources[:i]) for i in range(len(sources))]
        parts = [
            (shapes[name], forms[name], first, start, count)
            for (name, _, _, first, count), start in zip(sources, starts)
        ]

        def finish(total, back):
            names = [source[0] for source in sources]
            found = finish_piece(
                order, total, back, layer, width, [outputs.get(n) for n in names], parts, "finish_" + names[0]
            )
            outputs.update(zip(names, found))
            if extra is not None:
                outputs["little"] = found[-1]

        found = {}

        def others():
            found["rows"] = None if extra is None else extra()
            rows = found["rows"]
            found["others"] = weight_grad(order, pairs, 1, size, rows)

        def own():
            rows = found["rows"]
            found["own"] = weight_grad(order, pairs, 0, size, rows)[0]
            pipeline.offer(found["others"], found["own"], finish)

        fillers.extend([others, own])

    def queue_feed(layer):
        state = kept[layer]
        down = [v for t in kinds for v in slots_two[layer][t]], [state["grown"][t]["act"] for t in kinds]
        up = [v for t in kinds for v in state["middle"][t]], [fed[layer][t]["grad"] for t in kinds]
        most, half = 3 * hidden // 4, hidden // 2
        queue(layer, [("down", *down, 0, most)])
        queue(layer, [("down", *down, most, hidden - most), ("up", *up, 0, half)])

    def queue_attend(layer):
        state = kept[layer]
        up = [v for t in kinds for v in state["middle"][t]], [fed[layer][t]["grad"] for t in kinds]
        mix = [v for t in kinds for v in slots_one[layer][t]], [state["attended"][t]["ctx"] for t in kinds]
        proj = [v for t in kinds for v in state["x"][t]], [went[layer][t]["grad"] for t in kinds]
        half = hidden // 2
        queue(layer, [("up", *up, half, half), ("mix", *mix, 0, span)])
        queue(layer, [("proj", *proj, 0, 3 * span)], None if layer > 0 else little_rows)

    def fill(count):
        for _ in range(count):
            if fillers:
                fillers.pop(0)()

    norm_sums = []

    def sum_norms():
        found = sum_norm_rows(
            order, [[back[layer][s][1] for s in kinds] for layer in range(LAYERS) for back in (back_one, back_two)]
        )
        norm_sums.extend([found, to_core(found)])

    def little_rows():
        return little_gradients(
            order,
            norm_sums,
            [[fed[layer][s]["sums"] for s in kinds] for layer in range(LAYERS)],
            [[went[layer][s]["sums"] for s in kinds] for layer in range(LAYERS)],
            span,
        )

    items = []
    for layer in range(LAYERS):
        items += [attend(layer, s) for s in kinds] + [feed(layer, s) for s in kinds]
    forward_items = len(items)
    for layer in reversed(range(LAYERS)):
        items += [feed_back(layer, s) for s in kinds] + [attend_back(layer, s) for s in kinds]
    items[0][0]()
    for at, (_, products) in enumerate(items):
        s = at % streams
        found, more = products()
        beside = [to_core(part) for part in found["other"]]
        if at >= forward_items:
            fill(FILLS[at - forward_items])
            for _ in range(STEPS[at - forward_items]):
                pipeline.step()
        early = ADD_FIRST[at]
        if early:
            low = add_send(order, found["own"], beside)
        order.pin(ahead(at + 1))
        if at == 0:
            fetch(order, weights[0][3:])
            shares = deal_share(order, cotangents)
        if at + 1 < len(items):
            items[at + 1][0]()
        if at == forward_items + 1:
            out_rows = gather_halves([jnp.concatenate([v for t in kinds for v in kept[-1]["two"][t][0]], 0)])
        if at + 2 == len(items):
            sum_norms()
        if not early:
            low = add_send(order, found["own"], beside)
        terms[s] = [found["own"], *beside, to_chip(low), *more]
        for _ in range(MORE_STEPS[at - forward_items] if at >= forward_items else 0):
            pipeline.step()
    while fillers:
        fill(2)
        pipeline.step(True)
    layer_out = natural_share(order, out_rows, BF)
    pipeline.step(True)
    ends = [last_sum(order, terms[s]) for s in kinds]
    end_rows = gather_halves([jnp.concatenate(ends, 0)])
    pipeline.step(True)
    input_grad = natural_share(order, end_rows, F32)
    pipeline.drain()

    little = outputs["little"]
    grad_gains = little[: 2 * LAYERS, :width].reshape(LAYERS, 2, width)
    grad_biases = little[2 * LAYERS : 6 * LAYERS, :width].reshape(LAYERS, 4, width)
    rest = little[6 * LAYERS : 8 * LAYERS].reshape(LAYERS, -1)
    here = lax.axis_index(FSDP)
    grow = rest[:, :hidden].reshape(bias_grow.shape)
    heads = rest[:, hidden : hidden + 2 * span].reshape(bias_heads.shape)
    part = grow.shape[-1] // size
    grow = lax.dynamic_slice_in_dim(grow, here * part, part, grow.ndim - 1)
    part = heads.shape[-1] // size
    heads = lax.dynamic_slice_in_dim(heads, here * part, part, heads.ndim - 1)
    return (
        layer_out,
        input_grad,
        outputs["proj"],
        outputs["mix"],
        outputs["up"],
        outputs["down"],
        heads,
        grow,
        grad_gains,
        grad_biases,
    )


def solution(mesh):
    in_specs = (
        P((DP, FSDP), None),
        P((DP, FSDP, TENSOR), None),
        P((DP, FSDP)),
        P(None, None, FSDP, TENSOR),
        P(None, TENSOR, FSDP),
        P(None, FSDP, TENSOR),
        P(None, TENSOR, FSDP),
        P(None, None, TENSOR, FSDP),
        P(None, TENSOR, FSDP),
        P(None, None, FSDP),
        P(None, None, FSDP),
    )
    out_specs = (
        P((DP, FSDP, TENSOR), None),
        P((DP, FSDP, TENSOR), None),
        P(None, None, FSDP, TENSOR),
        P(None, TENSOR, FSDP),
        P(None, FSDP, TENSOR),
        P(None, TENSOR, FSDP),
        P(None, None, TENSOR, FSDP),
        P(None, TENSOR, FSDP),
        P(None, None, FSDP),
        P(None, None, FSDP),
    )
    return jax.shard_map(
        per_device, mesh=mesh, in_specs=in_specs, out_specs=out_specs, check_vma=False
    )
```

```python
import functools

import jax
import jax.numpy as jnp
from jax import lax
from jax.experimental import pallas as pl
from jax.experimental.pallas import tpu as pltpu
from jax.sharding import PartitionSpec as P

HEAD = 64
PAIR = 2 * HEAD
LAYERS = 2
LENGTHS = (512, 256, 128, 128, 128)
STARTS = (0, 512, 768, 896, 1024)
STREAMS = ((0,), (1, 2, 3, 4))
CUT = 2
HALVES = 2
BF = jnp.bfloat16
DP, FSDP, TENSOR = "dp", "fsdp", "tensor"
F32 = jnp.float32
MIB = 1 << 20
CORE_SWAP = [(0, 1), (1, 0), (2, 3), (3, 2)]
CHIP_SWAP = [(0, 2), (2, 0), (1, 3), (3, 1)]


def to_core(value):
    return lax.ppermute(value, TENSOR, CORE_SWAP)


def to_chip(value):
    return lax.ppermute(value, TENSOR, CHIP_SWAP)


def from_fsdp(value, step):
    size = lax.axis_size(FSDP)
    return lax.ppermute(value, FSDP, [((i + step) % size, i) for i in range(size)])


def to_fsdp(value, step):
    size = lax.axis_size(FSDP)
    return lax.ppermute(value, FSDP, [(i, (i + step) % size) for i in range(size)])


def own_first(whole, axis):
    size = lax.axis_size(FSDP)
    here = lax.axis_index(FSDP)
    width = whole.shape[axis] // size
    return jnp.concatenate(
        [lax.dynamic_slice_in_dim(whole, (here + k) % size * width, width, axis) for k in range(size)], axis
    )


def natural(relative, axis):
    size = lax.axis_size(FSDP)
    here = lax.axis_index(FSDP)
    width = relative.shape[axis] // size
    return jnp.concatenate(
        [
            lax.dynamic_slice_in_dim(relative, (k - here + size) % size * width, width, axis)
            for k in range(size)
        ],
        axis,
    )


def dot(left, right):
    return jnp.dot(left, right, preferred_element_type=F32)


def dot_t(left, right):
    return lax.dot_general(left, right, (((1,), (1,)), ((), ())), preferred_element_type=F32)


def dot_rows(left, right):
    return lax.dot_general(left, right, (((0,), (0,)), ((), ())), preferred_element_type=F32)


def share_rows(stream):
    return sum(LENGTHS[page] for page in stream) // HALVES


def page_places(stream):
    places, at = [], 0
    for page in stream:
        places.append((page, LENGTHS[page], at, at // HALVES))
        at += LENGTHS[page]
    return places


SCOPED = 8


class Order:
    def __init__(self):
        self.last = None
        self.pins = []

    def pin(self, arrays):
        self.pins.extend(v for v in arrays)

    def call(
        self,
        body,
        inputs,
        outputs,
        scratch=(),
        grid=(),
        in_specs=None,
        out_specs=None,
        name=None,
        limit=SCOPED,
        alias=None,
    ):
        pins, self.pins = self.pins, []
        count = len(inputs)
        in_specs = in_specs or [None] * count
        out_specs = out_specs or [None] * len(outputs)
        in_specs = [whole_of(v.shape, grid) if s is None else s for s, v in zip(in_specs, inputs)]
        out_specs = [whole_of(v.shape, grid) if s is None else s for s, v in zip(out_specs, outputs)]
        token = shape_of((8, 128), F32)
        inputs = list(inputs) + pins + ([] if self.last is None else [self.last])
        in_specs += [ANY] * (len(inputs) - count)
        extra = len(inputs) - count

        def kernel(*refs):
            given, refs = refs[:count], refs[count + extra :]
            outs, mark, own = refs[: len(outputs)], refs[len(outputs)], refs[len(outputs) + 1 :]
            mark[...] = jnp.zeros(mark.shape, F32)
            body(*given, *outs, *own)

        *result, self.last = pl.pallas_call(
            kernel,
            grid=grid,
            in_specs=in_specs,
            out_specs=[*out_specs, whole_of(token.shape, grid)],
            out_shape=[*outputs, token],
            scratch_shapes=list(scratch),
            input_output_aliases=alias or {},
            name=name,
            cost_estimate=pl.CostEstimate(flops=0, bytes_accessed=0, transcendentals=0),
            compiler_params=pltpu.CompilerParams(vmem_limit_bytes=limit * MIB),
        )(*inputs)
        return result


def whole_of(shape, grid):
    if not grid:
        return pl.BlockSpec(memory_space=pltpu.VMEM)
    return pl.BlockSpec(shape, lambda *at: (0,) * len(shape))


def shape_of(shape, dtype):
    return jax.ShapeDtypeStruct(tuple(shape), dtype)


SMEM = pl.BlockSpec(memory_space=pltpu.SMEM)
ANY = pl.BlockSpec(memory_space=pl.ANY)
HELD = pl.BlockSpec(memory_space=pltpu.HBM)


def core_index():
    return lax.rem(lax.axis_index(TENSOR), 2)


class Weight:
    def __init__(self, order, whole, layer, axis):
        self.order, self.whole, self.layer, self.axis = order, whole, layer, axis
        self.size = lax.axis_size(FSDP)
        shape = whole.shape[1:]
        width = shape[axis]
        self.halved = self.size == 2 and lax.axis_size(DP) % 2 == 0 and width % 256 == 0
        self.widths = [width] + ([width // 2] * 2 if self.halved else [width] * (self.size - 1))
        self.shape = shape

    def places(self):
        width = self.widths[0]
        if not self.halved:
            return [pl.ds(k * width, width) for k in range(self.size)]
        parity = lax.rem(lax.axis_index(DP), 2)
        half = width // 2
        return [
            pl.ds(0, width),
            pl.ds(pl.multiple_of(width + parity * half, 128), half),
            pl.ds(pl.multiple_of(width + (1 - parity) * half, 128), half),
        ]

    def start(self, own, half):
        if self.halved:
            self.early = [from_fsdp(half, 1)]
            size = lax.axis_size(DP)
            self.late = [lax.ppermute(self.early[0], DP, [(i, i ^ 1) for i in range(size)])]
        else:
            self.early = [from_fsdp(own, step) for step in range(1, self.size)]
            self.late = []
        self.arrays = [own, *self.early, *self.late]

    def specs(self):
        return [None] * len(self.arrays)

    def take(self, refs):
        count = len(self.arrays)
        return list(zip(refs[:count], self.places())), refs[count:]


def fetch(order, weights):
    outputs = []
    for w in weights:
        outputs.append(shape_of(w.shape, BF))
        if w.halved:
            shape = list(w.shape)
            shape[w.axis] //= 2
            outputs.append(shape_of(shape, BF))

    def body(*refs):
        outs, sems = list(refs[len(weights) : -1]), refs[-1]
        parity = lax.rem(lax.axis_index(DP), 2)
        copies = []
        for w, ref in zip(weights, refs):
            sources = [ref.at[w.layer]]
            if w.halved:
                half = w.widths[1]
                place = [slice(None)] * len(w.shape)
                place[w.axis] = pl.ds(pl.multiple_of(parity * half, 128), half)
                sources.append(ref.at[(w.layer, *place)])
            for source in sources:
                copy = pltpu.make_async_copy(source, outs.pop(0), sems.at[len(copies)])
                copy.start()
                copies.append(copy)
        for copy in copies:
            copy.wait()

    found = order.call(
        body,
        [w.whole for w in weights],
        outputs,
        scratch=[pltpu.SemaphoreType.DMA((len(outputs),))],
        in_specs=[HELD] * len(weights),
        name="fetch",
    )
    for w in weights:
        own = found.pop(0)
        w.start(own, found.pop(0) if w.halved else None)


def deal_rows(order, activations):
    features = activations.shape[1]
    size = lax.axis_size(FSDP)
    width = features // size

    def body(whole, *outs):
        here = core_index()
        mine = lax.axis_index(FSDP)
        for at, stream in enumerate(STREAMS):
            for slot in range(HALVES):
                out = outs[at * HALVES + slot]
                for page, length, _, offset in page_places(stream):
                    part = length // HALVES
                    row = pl.multiple_of(STARTS[page] + (here ^ slot) * part, 32)
                    for k in range(size):
                        column = pl.multiple_of(lax.rem(mine + k, size) * width, 128)
                        out[offset : offset + part, k * width : (k + 1) * width] = whole[
                            pl.ds(row, part), pl.ds(column, width)
                        ]

    outs = order.call(
        body,
        [activations],
        [shape_of((share_rows(stream), features), BF) for stream in STREAMS for _ in range(HALVES)],
        name="deal_rows",
    )
    return [outs[at * HALVES : (at + 1) * HALVES] for at in range(len(STREAMS))]


def copy_rows(order, rows):
    def body(a, out):
        out[...] = a[...]

    return order.call(body, [rows], [shape_of(rows.shape, rows.dtype)], name="copy_rows")[0]


def deal_share(order, slots):
    rows, features = slots[0].shape
    size = lax.axis_size(FSDP)
    width = features // size

    def body(a, b, c, d, *outs):
        whole = outs[-1]
        here = lax.axis_index(TENSOR)
        core = core_index()
        mine = lax.axis_index(FSDP)
        for slot, ref in enumerate((a, b, c, d)):
            whole[pl.ds(pl.multiple_of((here ^ slot) * rows, 32), rows), :] = ref[...]
        for at, stream in enumerate(STREAMS):
            for page, length, _, offset in page_places(stream):
                part = length // HALVES
                row = pl.multiple_of(STARTS[page] + core * part, 32)
                for k in range(size):
                    column = pl.multiple_of(lax.rem(mine + k, size) * width, 128)
                    outs[at][offset : offset + part, k * width : (k + 1) * width] = whole[
                        pl.ds(row, part), pl.ds(column, width)
                    ]

    return order.call(
        body,
        slots,
        [shape_of((share_rows(stream), features), BF) for stream in STREAMS],
        scratch=[pltpu.VMEM((rows * 4, features), BF)],
        name="deal_share",
    )


def natural_share(order, slots, dtype):
    rows, features = slots[0].shape
    share = rows // 2
    size = lax.axis_size(FSDP)
    width = features // size

    def body(a, b, out, whole):
        here = lax.axis_index(TENSOR)
        core = core_index()
        mine = lax.axis_index(FSDP)
        for slot, ref in enumerate((a, b)):
            first = 0
            for stream in STREAMS:
                for page, length, _, offset in page_places(stream):
                    part = length // HALVES
                    row = pl.multiple_of(STARTS[page] + (core ^ slot) * part, 32)
                    whole[pl.ds(row, part), :] = ref[first + offset : first + offset + part, :]
                first += share_rows(stream)
        own = pl.multiple_of(here * share, 32)
        for k in range(size):
            column = pl.multiple_of(lax.rem(mine + k, size) * width, 128)
            out[:, pl.ds(column, width)] = whole[pl.ds(own, share), k * width : (k + 1) * width].astype(dtype)

    return order.call(
        body,
        slots,
        [shape_of((share, features), dtype)],
        scratch=[pltpu.VMEM((rows * 2, features), BF)],
        name="natural_share",
    )[0]


def add_send(order, kept, came):
    def body(a, *refs):
        low, at = refs[-1], 0
        for ref in refs[:-1]:
            rows = slice(at, at + ref.shape[0])
            low[rows, :] = (a[rows, :].astype(F32) + ref[...].astype(F32)).astype(BF)
            at += ref.shape[0]

    return order.call(body, [kept, *came], [shape_of(kept.shape, BF)], name="add_send")[0]


def sum_terms(own, *refs):
    *pieces, across = refs
    beside = jnp.concatenate([ref[...] for ref in pieces], 0)
    return own[...].astype(F32) + beside.astype(F32) + across[...].astype(F32)


def row_of(ref, at):
    return ref[at : at + 1, :]


def norm_forward(order, terms, residual, vectors, rows_of_vectors):
    rows, features = terms[0].shape
    bias_at, gain_at, shift_at = rows_of_vectors

    def body(*refs):
        parts, (before, vec, *lows, normed, inverse, kept) = refs[: len(terms)], refs[len(terms) :]
        value = before[...].astype(F32)
        if residual[1] is not None:
            value = value * row_of(vec, residual[1]) + row_of(vec, residual[2])
        value = value + sum_terms(*parts) + row_of(vec, bias_at)
        center = value - jnp.mean(value, -1, keepdims=True)
        scale = lax.rsqrt(jnp.mean(center * center, -1, keepdims=True) + 1e-05)
        unit = center * scale
        normed[...] = unit
        kept[...] = unit.astype(BF)
        inverse[...] = scale
        split_rows(lows, slice(None), unit * row_of(vec, gain_at) + row_of(vec, shift_at))

    outs = order.call(
        body,
        [*terms, residual[0], vectors],
        [
            *[shape_of((rows // CUT, features), BF)] * CUT,
            shape_of((rows, features), F32),
            shape_of((rows, 1), F32),
            shape_of((rows, features), BF),
        ],
        name="norm_forward",
    )
    return [outs[:CUT], *outs[CUT:]]


def norm_backward(order, terms, normed, inverse, vectors, gain_at):
    rows, features = normed.shape
    count = len(terms)

    def body(*refs):
        unit, scale, vec, *lows, sums, wide = refs[count:]
        total = refs[count - 1][...].astype(F32)
        if count > 1:
            total = total + sum_terms(*refs[: count - 1])
        n = unit[...].astype(F32)
        grad = total * row_of(vec, gain_at)
        mean_one = jnp.mean(grad, -1, keepdims=True)
        mean_two = jnp.mean(grad * n, -1, keepdims=True)
        result = scale[...] * (grad - mean_one - n * mean_two)
        wide[...] = result
        split_rows(lows, slice(None), result)
        sums[0:1, :] = jnp.sum(total * n, 0, keepdims=True)
        sums[1:2, :] = jnp.sum(total, 0, keepdims=True)
        sums[2:3, :] = jnp.sum(result, 0, keepdims=True)

    outs = order.call(
        body,
        [*terms, normed, inverse, vectors],
        [
            *[shape_of((rows // CUT, features), BF)] * CUT,
            shape_of((3, features), F32),
            shape_of((rows, features), F32),
        ],
        name="norm_backward",
    )
    return [outs[:CUT], *outs[CUT:]]


def last_sum(order, terms):
    def body(*refs):
        refs[-1][...] = (refs[-2][...] + sum_terms(*refs[:-2])).astype(BF)

    return order.call(body, terms, [shape_of(terms[0].shape, BF)], name="last_sum")[0]


def head_mask(which):
    lane = lax.broadcasted_iota(jnp.int32, (1, PAIR), 1)
    return (lane < HEAD) if which == 0 else (lane >= HEAD)


def key_bias(length, limit):
    part = length // HALVES
    place = lax.broadcasted_iota(jnp.int32, (1, length), 1)
    half = (place // part) ^ core_index()
    return jnp.where(half * part + place % part < limit, 0.0, -1000000000.0).astype(F32)


def put_rows(ref, lanes, value, row, part, share, offset):
    done = 0
    while done < value.shape[0]:
        at = row + done
        count = min(part - at % part, value.shape[0] - done)
        first = (at // part) * share + offset + at % part
        ref[first : first + count, lanes] = value[done : done + count]
        done += count


def attention_forward(order, stream, slots, weights, lengths):
    w_proj, w_mix, bias_rows = weights
    share, features = slots_shape(slots)
    span = w_mix.shape[0]
    heads = span // HEAD
    places = page_places(stream)

    def body(*refs):
        xs, refs = refs[: len(slots)], refs[len(slots) :]
        wp, refs = w_proj.take(refs)
        wm, refs = w_mix.take(refs)
        bias, limits, refs = refs[0], refs[1], refs[2:]
        others, (part_own, qkv, ctx), probs = refs[:CUT], refs[CUT : CUT + 3], refs[CUT + 3 :]
        for kind in range(3):
            value = None
            for w, at in wp:
                rows = jnp.concatenate([x[:, at] for x in xs], 0)
                term = dot(rows, w[kind])
                value = term if value is None else value + term
            if kind == 0:
                value = value + bias[0:1, :]
            elif kind == 2:
                value = value + bias[1:2, :]
            value = value.astype(BF)
            if kind == 0:
                value = value * jnp.asarray(HEAD ** (-0.5), BF)
            for _, length, base, offset in places:
                part = length // HALVES
                for slot in range(HALVES):
                    qkv[base + slot * part : base + (slot + 1) * part, kind * span : (kind + 1) * span] = value[
                        slot * share + offset : slot * share + offset + part, :
                    ]
        for index, (page, length, base, offset) in enumerate(places):
            part = length // HALVES
            shut = key_bias(length, limits[page])
            step = min(length, 256)
            for pair in range(heads // 2):
                lanes = slice(pair * PAIR, (pair + 1) * PAIR)
                keys = qkv[base : base + length, span + pair * PAIR : span + (pair + 1) * PAIR]
                values = qkv[base : base + length, 2 * span + pair * PAIR : 2 * span + (pair + 1) * PAIR]
                for row in range(0, length, step):
                    queries = qkv[base + row : base + row + step, lanes]
                    found = []
                    for which in range(2):
                        masked = queries * head_mask(which).astype(BF)
                        scores = dot_t(masked, keys) + shut
                        peak = jnp.max(scores, -1, keepdims=True)
                        raised = jnp.exp(scores - peak)
                        chance = raised * (1.0 / jnp.sum(raised, -1, keepdims=True))
                        chance = chance.astype(BF)
                        probs[index][2 * pair + which, row : row + step, :] = chance
                        found.append(dot(chance, values))
                    both = jnp.where(head_mask(0), found[0], found[1]).astype(BF)
                    put_rows(ctx, lanes, both, row, part, share, offset)
        for w, at in wm:
            value = dot(ctx[...], w[...])
            part_own[:, at] = value[:share].astype(BF)
            split_rows(others, at, value[share:])

    outs = order.call(
        body,
        [*slots, *w_proj.arrays, *w_mix.arrays, bias_rows, lengths],
        [
            *[shape_of((share // CUT, features), BF)] * CUT,
            shape_of((share, features), BF),
            shape_of((2 * share, 3 * span), BF),
            shape_of((2 * share, span), BF),
        ]
        + [shape_of((heads, length, length), BF) for _, length, _, _ in places],
        in_specs=[None] * len(slots) + w_proj.specs() + w_mix.specs() + [None, SMEM],
        name="attention_forward",
    )
    return {"other": outs[:CUT], "own": outs[CUT], "qkv": outs[CUT + 1], "ctx": outs[CUT + 2], "probs": outs[CUT + 3 :]}


def attention_backward(order, stream, slots, weights, state):
    w_proj, w_mix = weights
    probs, qkv = state["probs"], state["qkv"]
    share, features = slots_shape(slots)
    span = w_mix.shape[0]
    heads = span // HEAD
    places = page_places(stream)

    def body(*refs):
        ds, refs = refs[: len(slots)], refs[len(slots) :]
        wp, refs = w_proj.take(refs)
        wm, refs = w_mix.take(refs)
        chances, refs = refs[: len(places)], refs[len(places) :]
        qkv_ref, *others, part_own, grad, sums, low = refs
        value = None
        for w, at in wm:
            rows = jnp.concatenate([d[:, at] for d in ds], 0)
            term = dot_t(rows, w[...])
            value = term if value is None else value + term
        value = value.astype(BF)
        for _, length, base, offset in places:
            part = length // HALVES
            for slot in range(HALVES):
                low[base + slot * part : base + (slot + 1) * part, :] = value[
                    slot * share + offset : slot * share + offset + part, :
                ]
        for index, (page, length, base, offset) in enumerate(places):
            part = length // HALVES
            step = min(length, 256)
            for pair in range(heads // 2):
                lanes = slice(pair * PAIR, (pair + 1) * PAIR)
                keys = qkv_ref[base : base + length, span + pair * PAIR : span + (pair + 1) * PAIR]
                values = qkv_ref[base : base + length, 2 * span + pair * PAIR : 2 * span + (pair + 1) * PAIR]
                grad_keys, grad_values = [None, None], [None, None]
                for row in range(0, length, step):
                    queries = qkv_ref[base + row : base + row + step, lanes]
                    grad_rows = low[base + row : base + row + step, lanes]
                    found = []
                    for which in range(2):
                        chance = chances[index][2 * pair + which, row : row + step, :]
                        wide = chance.astype(F32)
                        back = dot_t(grad_rows * head_mask(which).astype(BF), values)
                        inner = jnp.sum(wide * back, -1, keepdims=True)
                        grad_scores = (wide * (back - inner)).astype(BF)
                        found.append(dot(grad_scores, keys))
                        of_keys = dot_rows(grad_scores, queries)
                        of_values = dot_rows(chance, grad_rows)
                        first = grad_keys[which] is None
                        grad_keys[which] = of_keys if first else grad_keys[which] + of_keys
                        grad_values[which] = of_values if first else grad_values[which] + of_values
                    both = (jnp.where(head_mask(0), found[0], found[1]) * HEAD ** (-0.5)).astype(BF)
                    put_rows(grad, lanes, both, row, part, share, offset)
                for kind, parts in ((1, grad_keys), (2, grad_values)):
                    both = jnp.where(head_mask(0), parts[0], parts[1]).astype(BF)
                    for slot in range(HALVES):
                        grad[
                            slot * share + offset : slot * share + offset + part,
                            kind * span + pair * PAIR : kind * span + (pair + 1) * PAIR,
                        ] = both[slot * part : (slot + 1) * part, :]
        for w, at in wp:
            value = None
            for kind in range(3):
                term = dot_t(grad[:, kind * span : (kind + 1) * span], w[kind])
                value = term if value is None else value + term
            part_own[:, at] = value[:share].astype(BF)
            split_rows(others, at, value[share:])
        sums[...] = jnp.sum(grad[...].astype(F32), 0, keepdims=True)

    outs = order.call(
        body,
        [*slots, *w_proj.arrays, *w_mix.arrays, *probs, qkv],
        [
            *[shape_of((share // CUT, features), BF)] * CUT,
            shape_of((share, features), BF),
            shape_of((2 * share, 3 * span), BF),
            shape_of((1, 3 * span), F32),
        ],
        scratch=[pltpu.VMEM((2 * share, span), BF)],
        in_specs=[None] * len(slots) + w_proj.specs() + w_mix.specs() + [None] * (len(places) + 1),
        name="attention_backward",
    )
    return {"other": outs[:CUT], "own": outs[CUT], "grad": outs[CUT + 1], "sums": outs[CUT + 2]}


def slots_shape(slots):
    return sum(v.shape[0] for v in slots) // 2, slots[0].shape[1]


def split_rows(refs, at, value):
    count = value.shape[0] // CUT
    for i, ref in enumerate(refs):
        ref[:, at] = value[i * count : (i + 1) * count].astype(BF)


def leave_terms(low, weight, product, share, others, part_own):
    for w, at in weight:
        done = product(low, w[...])
        part_own[:, at] = done[:share, :].astype(BF)
        split_rows(others, at, done[share:, :])


def feed_forward(order, slots, weights):
    w_grow, w_shrink, bias = weights
    share, features = slots_shape(slots)
    hidden = w_shrink.shape[0]

    def body(*refs):
        xs, refs = refs[: len(slots)], refs[len(slots) :]
        wg, refs = w_grow.take(refs)
        ws, refs = w_shrink.take(refs)
        b, *others, act, slope, part_own = refs
        value = None
        for w, at in wg:
            rows = jnp.concatenate([x[:, at] for x in xs], 0)
            term = dot(rows, w[...])
            value = term if value is None else value + term
        up = value + b[...]
        cdf = 0.5 * (1.0 + lax.erf(up * 0.7071067811865476))
        density = jnp.exp(-0.5 * up * up) * 0.3989422804014327
        low = (up * cdf).astype(BF)
        act[...] = low
        slope[...] = (cdf + up * density).astype(BF)
        leave_terms(low, ws, dot, share, others, part_own)

    outs = order.call(
        body,
        [*slots, *w_grow.arrays, *w_shrink.arrays, bias],
        [
            *[shape_of((share // CUT, features), BF)] * CUT,
            shape_of((2 * share, hidden), BF),
            shape_of((2 * share, hidden), BF),
            shape_of((share, features), BF),
        ],
        name="feed_forward",
        limit=FEED_LIMIT,
    )
    return {"other": outs[:CUT], "act": outs[CUT], "slope": outs[CUT + 1], "own": outs[CUT + 2]}


def feed_backward(order, slots, slope, weights):
    w_grow, w_shrink = weights
    share, features = slots_shape(slots)
    hidden = w_shrink.shape[0]

    def body(*refs):
        ds, refs = refs[: len(slots)], refs[len(slots) :]
        wg, refs = w_grow.take(refs)
        ws, refs = w_shrink.take(refs)
        tilt, *others, grad, sums, part_own = refs
        value = None
        for w, at in ws:
            rows = jnp.concatenate([d[:, at] for d in ds], 0)
            term = dot_t(rows, w[...])
            value = term if value is None else value + term
        low = (value * tilt[...].astype(F32)).astype(BF)
        grad[...] = low
        sums[...] = jnp.sum(low.astype(F32), 0, keepdims=True)
        leave_terms(low, wg, dot_t, share, others, part_own)

    outs = order.call(
        body,
        [*slots, *w_grow.arrays, *w_shrink.arrays, slope],
        [
            *[shape_of((share // CUT, features), BF)] * CUT,
            shape_of((2 * share, hidden), BF),
            shape_of((1, hidden), F32),
            shape_of((share, features), BF),
        ],
        name="feed_backward",
        limit=FEED_LIMIT,
    )
    return {"other": outs[:CUT], "grad": outs[CUT], "sums": outs[CUT + 1], "own": outs[CUT + 2]}


def weight_grad(order, pairs, part, parts, extra=None):
    features = pairs[0][0][0].shape[1]
    width = features // parts
    start, shards = (0, 1) if part == 0 else (1, parts - 1)
    flat, specs, total = [], [], 0
    for left, right, first, count in pairs:
        flat += [*left, *right]
        specs += [pl.BlockSpec((v.shape[0], width), lambda i: (0, start + i)) for v in left]
        specs += [pl.BlockSpec((v.shape[0], count), lambda i, at=first // count: (0, at)) for v in right]
        total += count
    more = 0 if extra is None else extra.shape[1]
    if more:
        flat.append(extra)
        specs.append(pl.BlockSpec((1, *extra.shape[1:]), lambda i: (start + i, 0, 0)))

    def body(*refs):
        out, at, column = refs[-1], 0, 0
        if more:
            out[0, width:, :] = refs[len(flat) - 1][0].astype(BF)
        for left, right, _, count in pairs:
            a = jnp.concatenate([r[...] for r in refs[at : at + len(left)]], 0)
            at += len(left)
            b = jnp.concatenate([r[...] for r in refs[at : at + len(right)]], 0)
            at += len(right)
            out[0, :width, column : column + count] = dot_rows(a, b).astype(BF)
            column += count

    return order.call(
        body,
        flat,
        [shape_of((shards, width + more, total), BF)],
        grid=(shards,),
        in_specs=specs,
        out_specs=[pl.BlockSpec((1, width + more, total), lambda i: (i, 0, 0))],
        name="weight_grad",
        limit=GRAD_LIMIT,
    )[0]


class Pipeline:
    def __init__(self, order):
        self.order = order
        self.line = lax.axis_size(DP) == 4
        self.waiting, self.pieces, self.at = [], [], 0

    def offer(self, others, own, finish):
        self.waiting.append({"others": others, "own": own, "finish": finish})

    def piece(self, at):
        return self.pieces[at] if 0 <= at < len(self.pieces) else None

    def step(self, last=False):
        size = lax.axis_size(FSDP)
        now = self.at
        self.at += 1
        oldest, older, old, new = (self.piece(now - 1 - back) for back in (3, 2, 1, 0))
        if last and self.line and oldest is not None:
            oldest["finish"](oldest["total"], oldest["back"])
            oldest = None
        sums = []
        if new is not None:
            sums.append(("sum", new, [new["own"], *new["came"]]))
        if self.line and old is not None:
            sums.append(("inner", old, [old["sum"], old["swapped"]]))
        if self.line and older is not None:
            sums.append(("total", older, [older["inner"], older["met"]]))
        if sums:
            send = [piece[0] for piece in sums] if self.line else []
            found = combine(self.order, [terms for *_, terms in sums], send)
            for (name, piece, _), value in zip(sums, found):
                piece[name] = value
        if not self.line and new is not None:
            total = lax.psum(new["sum"], DP)
            new["finish"](total, total)
        elif self.line:
            if old is not None:
                old["met"] = lax.ppermute(old["inner"], DP, [(1, 2), (2, 1)])
            if new is not None and older is not None:
                new["swapped"] = older["back"] = lax.ppermute(found[-1], DP, [(0, 1), (1, 0), (2, 3), (3, 2)])
            elif new is not None:
                new["swapped"] = lax.ppermute(new["sum"], DP, [(0, 1), (3, 2)])
            elif older is not None:
                older["back"] = lax.ppermute(older["total"], DP, [(1, 0), (2, 3)])
        if self.waiting:
            piece = self.waiting.pop(0)
            piece["came"] = [to_fsdp(piece["others"][k], k + 1) for k in range(size - 1)]
            self.pieces.append(piece)
        else:
            self.pieces.append(None)
        if self.line and oldest is not None:
            oldest["finish"](oldest["total"], oldest["back"])

    def drain(self):
        while self.waiting or any(p is not None for p in self.pieces[max(self.at - 4, 0) :]):
            self.step(True)


def at_end():
    here = lax.axis_index(DP)
    return (here == 0) | (here == lax.axis_size(DP) - 1)


def combine(order, groups, names):
    width = groups[0][0].shape[1]
    rows = [terms[0].shape[0] for terms in groups]
    both = "sum" in names and "total" in names
    given = [v for terms in groups for v in terms]
    outputs = [shape_of((count, width), BF) for count in rows]
    if both:
        ends, inside = names.index("sum"), names.index("total")
        outputs.append(shape_of((max(rows[ends], rows[inside]), width), BF))

    def body(*refs):
        at, sums = 0, []
        for index, (terms, count) in enumerate(zip(groups, rows)):
            total = refs[at][...].astype(F32)
            for ref in refs[at + 1 : at + len(terms)]:
                total = total + ref[:count, :].astype(F32)
            at += len(terms)
            sums.append(total)
            refs[len(given) + index][...] = total.astype(BF)
        if both:
            a, b, send = sums[ends], sums[inside], refs[-1]
            short = min(rows[ends], rows[inside])
            send[:short, :] = jnp.where(at_end(), a[:short], b[:short]).astype(BF)
            if send.shape[0] > short:
                send[short:, :] = (a if rows[ends] > short else b)[short:].astype(BF)

    return order.call(body, given, outputs, name="combine")


def finish_piece(order, total, back, layer, rows, held, parts, name):
    more = total.shape[0] - rows
    width = total.shape[1]
    given = [v for v in held if v is not None]
    both = [total, back]
    scratch = []
    for shape, form, _, _, count in parts:
        if form == "kinds":
            scratch.append(pltpu.VMEM((shape[1], rows, count // shape[1]), F32))
        else:
            scratch.append(pltpu.VMEM((rows, count) if form == "columns" else (count, rows), F32))

    def body(*refs):
        outs = refs[len(both) + len(given) : len(both) + len(given) + len(parts)]
        rest = refs[len(both) + len(given) + len(parts) :]
        if more:
            extra, rest = rest[0], rest[1:]
        blocks, sems = rest[:-1], rest[-1]
        value = jnp.where(at_end(), refs[1][: total.shape[0], :].astype(F32), refs[0][...].astype(F32))
        if more:
            extra[...] = value[rows:]
            value = value[:rows]
        copies = []
        for at, (out, block, (shape, form, place, first, count)) in enumerate(zip(outs, blocks, parts)):
            if form == "kinds":
                span = count // shape[1]
                for g in range(shape[1]):
                    block[g] = value[:, first + g * span : first + (g + 1) * span]
                there = out.at[layer]
            elif form == "turned":
                block[...] = value[:, first : first + count].T
                there = out.at[layer, pl.ds(place, count), :]
            else:
                block[...] = value[:, first : first + count]
                there = out.at[layer, :, pl.ds(place, count)]
            copy = pltpu.make_async_copy(block, there, sems.at[at])
            copy.start()
            copies.append(copy)
        for copy in copies:
            copy.wait()

    alias, at = {}, 0
    for index, v in enumerate(held):
        if v is not None:
            alias[len(both) + at] = index
            at += 1
    return order.call(
        body,
        [*both, *given],
        [shape_of(shape, F32) for shape, *_ in parts] + ([shape_of((more, width), F32)] if more else []),
        scratch=[*scratch, pltpu.SemaphoreType.DMA((len(parts),))],
        in_specs=[None] * len(both) + [HELD] * len(given),
        out_specs=[HELD] * len(parts) + ([None] if more else []),
        alias=alias,
        name=name,
        limit=12,
    )


def sum_norm_rows(order, sums):
    streams = len(sums[0])
    features = sums[0][0].shape[1]

    def body(*refs):
        out = refs[-1]
        found = []
        for at in range(len(sums)):
            total = refs[at * streams][...]
            for ref in refs[at * streams + 1 : (at + 1) * streams]:
                total = total + ref[...]
            found.append(total)
        rows = [found[at][0:1] for at in range(2 * LAYERS)]
        for layer in range(LAYERS):
            one, two = found[2 * layer], found[2 * layer + 1]
            rows += [one[2:3], two[2:3], one[1:2], two[1:2]]
        for at, row in enumerate(rows):
            out[at : at + 1, :] = row

    return order.call(
        body,
        [v for group in sums for v in group],
        [shape_of((6 * LAYERS, features), F32)],
        name="sum_norm_rows",
    )[0]


def little_gradients(order, norms, grow, heads, span):
    size = lax.axis_size(FSDP)
    features = norms[0].shape[1]
    width = features // size
    columns = 3 * span
    hidden = grow[0][0].shape[1]
    streams = len(grow[0])

    def body(a, b, *refs):
        out = refs[-1]
        out[...] = jnp.zeros(out.shape, F32)
        total = a[...] + b[...]
        rows = 6 * LAYERS
        for k in range(size):
            out[k, :rows, :width] = total[:, k * width : (k + 1) * width]
        for layer in range(LAYERS):
            at = layer * streams
            up = sum(ref[...] for ref in refs[at : at + streams])
            at += LAYERS * streams
            qkv = sum(ref[...] for ref in refs[at : at + streams])
            for k in range(size):
                row = rows + 2 * layer
                rest = hidden - columns
                out[k, row : row + 1, :] = up[:, :columns]
                out[k, row + 1 : row + 2, :rest] = up[:, columns:]
                out[k, row + 1 : row + 2, rest : rest + span] = qkv[:, :span]
                out[k, row + 1 : row + 2, rest + span : rest + 2 * span] = qkv[:, 2 * span :]

    return order.call(
        body,
        [*norms, *[v for group in grow for v in group], *[v for group in heads for v in group]],
        [shape_of((size, 8 * LAYERS, columns), F32)],
        name="little_gradients",
    )[0]


FILLS = (0, 2, 2, 2, 2, 2, 2, 2)
STEPS = (0, 1, 1, 1, 1, 1, 1, 1)
MORE_STEPS = (0, 0, 0, 0, 0, 0, 0, 0)
GRAD_LIMIT = 12
ADD_FIRST = (1,) * 16
FEED_LIMIT = 12


def gather_halves(pieces):
    return [*pieces, *[to_core(piece) for piece in pieces]]


def per_device(
    activations, cotangent, lengths, w_qkv, w_out, w_up, w_down, b_qv, b_up, norm_gains, layer_biases
):
    size = lax.axis_size(FSDP)
    order = Order()
    kinds = range(len(STREAMS))

    smalls = (b_qv, b_up, norm_gains, layer_biases)
    flat = jnp.concatenate([value.reshape(-1) for value in smalls])
    pieces = [flat] + [from_fsdp(flat, step) for step in range(1, size)]

    def unpack(at):
        found, start = [], 0
        for value in smalls:
            found.append(pieces[at][start : start + value.size].reshape(value.shape))
            start += value.size
        return found

    unpacked = [unpack(at) for at in range(size)]
    bias_heads, bias_grow, gains, biases = (
        jnp.concatenate([u[i] for u in unpacked], -1).astype(F32) for i in range(4)
    )
    bias_heads, bias_grow = natural(bias_heads, 3), natural(bias_grow, 2)
    features = gains.shape[-1]
    vectors = jnp.concatenate([gains.reshape(-1, features), biases.reshape(-1, features)], 0)
    head_rows = [bias_heads[layer].reshape(2, -1) for layer in range(LAYERS)]
    grow_rows = [bias_grow[layer].reshape(1, -1) for layer in range(LAYERS)]

    weights = [
        [
            Weight(order, w_qkv, layer, 1),
            Weight(order, w_out, layer, 1),
            Weight(order, w_up, layer, 0),
            Weight(order, w_down, layer, 1),
        ]
        for layer in range(LAYERS)
    ]
    fetch(order, weights[0][:2])

    slots = deal_rows(order, activations)
    order.pin([*weights[0][0].early, *weights[0][1].early])
    fetch(order, weights[1])
    residual = [(slots[s][0], None, None) for s in kinds]
    cotangent = copy_rows(order, cotangent)
    across = to_chip(cotangent)
    cotangents = [cotangent, to_core(cotangent), across, to_core(across)]

    order.pin([*weights[0][0].early, *weights[0][0].late, *weights[0][1].early, *weights[0][1].late])
    fetch(order, weights[0][2:3])

    def ahead(at):
        zero, one = weights
        waits = {
            1: lambda: zero[2].early,
            2: lambda: [*zero[3].early, *zero[2].late, *one[0].early],
            3: lambda: [*one[1].early, *one[0].late],
            4: lambda: [*one[1].late, *one[2].early],
            5: lambda: [*one[2].late, *one[3].early],
            6: lambda: one[3].late,
        }
        return waits[at]() if at in waits else []

    streams = len(STREAMS)
    kept = [{k: [None] * streams for k in ("x", "attended", "grown", "one", "two", "middle")} for _ in range(LAYERS)]
    terms = [None] * streams
    back_two, slots_two, fed = ([[None] * streams for _ in range(LAYERS)] for _ in range(3))
    back_one, slots_one, went = ([[None] * streams for _ in range(LAYERS)] for _ in range(3))

    def gain_at(layer, which):
        return 2 * layer + which

    def bias_at(layer, which):
        return 2 * LAYERS + 4 * layer + which

    def second_norm(layer, s):
        one = kept[layer]["one"][s]
        kept[layer]["two"][s] = norm_forward(
            order,
            terms[s],
            (one[1], gain_at(layer, 0), bias_at(layer, 2)),
            vectors,
            (bias_at(layer, 1), gain_at(layer, 1), bias_at(layer, 3)),
        )

    def attend(layer, s):
        def before():
            if layer > 0:
                second_norm(layer - 1, s)
                two = kept[layer - 1]["two"][s]
                slots[s] = gather_halves(two[0])
                residual[s] = (two[1], gain_at(layer - 1, 1), bias_at(layer - 1, 3))
            kept[layer]["x"][s] = slots[s]

        def products():
            w_proj, w_mix = weights[layer][:2]
            found = attention_forward(order, STREAMS[s], slots[s], (w_proj, w_mix, head_rows[layer]), lengths)
            kept[layer]["attended"][s] = found
            return found, []

        return before, products

    def feed(layer, s):
        def before():
            one = norm_forward(
                order, terms[s], residual[s], vectors, (bias_at(layer, 0), gain_at(layer, 0), bias_at(layer, 2))
            )
            kept[layer]["one"][s] = one
            kept[layer]["middle"][s] = gather_halves(one[0])

        def products():
            w_grow, w_shrink = weights[layer][2:]
            found = feed_forward(order, kept[layer]["middle"][s], (w_grow, w_shrink, grow_rows[layer]))
            kept[layer]["grown"][s] = found
            return found, []

        return before, products

    def feed_back(layer, s):
        def before():
            if layer + 1 == LAYERS:
                second_norm(layer, s)
                terms[s] = [shares[s]]
            two = kept[layer]["two"][s]
            back_two[layer][s] = norm_backward(order, terms[s], two[3], two[2], vectors, gain_at(layer, 1))
            slots_two[layer][s] = gather_halves(back_two[layer][s][0])

        def products():
            w_grow, w_shrink = weights[layer][2:]
            found = feed_backward(order, slots_two[layer][s], kept[layer]["grown"][s]["slope"], (w_grow, w_shrink))
            fed[layer][s] = found
            if s + 1 == streams:
                queue_feed(layer)
            return found, [back_two[layer][s][2]]

        return before, products

    def attend_back(layer, s):
        def before():
            one = kept[layer]["one"][s]
            back_one[layer][s] = norm_backward(order, terms[s], one[3], one[2], vectors, gain_at(layer, 0))
            slots_one[layer][s] = gather_halves(back_one[layer][s][0])

        def products():
            w_proj, w_mix = weights[layer][:2]
            state = kept[layer]
            found = attention_backward(order, STREAMS[s], slots_one[layer][s], (w_proj, w_mix), state["attended"][s])
            went[layer][s] = found
            if s + 1 == streams:
                queue_attend(layer)
            return found, [back_one[layer][s][2]]

        return before, products

    pipeline = Pipeline(order)
    fillers = []
    outputs = {}
    span, hidden = w_out.shape[1], w_down.shape[1]
    width = features // size
    shapes = {
        "proj": (LAYERS, 3, width, span),
        "mix": (LAYERS, span, width),
        "up": (LAYERS, width, hidden),
        "down": (LAYERS, hidden, width),
    }
    forms = {"proj": "kinds", "mix": "turned", "up": "columns", "down": "turned"}

    def queue(layer, sources, extra=None):
        pairs = [source[1:] for source in sources]
        starts = [sum(source[4] for source in sources[:i]) for i in range(len(sources))]
        parts = [
            (shapes[name], forms[name], first, start, count)
            for (name, _, _, first, count), start in zip(sources, starts)
        ]

        def finish(total, back):
            names = [source[0] for source in sources]
            found = finish_piece(
                order, total, back, layer, width, [outputs.get(n) for n in names], parts, "finish_" + names[0]
            )
            outputs.update(zip(names, found))
            if extra is not None:
                outputs["little"] = found[-1]

        found = {}

        def others():
            found["rows"] = None if extra is None else extra()
            rows = found["rows"]
            found["others"] = weight_grad(order, pairs, 1, size, rows)

        def own():
            rows = found["rows"]
            found["own"] = weight_grad(order, pairs, 0, size, rows)[0]
            pipeline.offer(found["others"], found["own"], finish)

        fillers.extend([others, own])

    def queue_feed(layer):
        state = kept[layer]
        down = [v for t in kinds for v in slots_two[layer][t]], [state["grown"][t]["act"] for t in kinds]
        up = [v for t in kinds for v in state["middle"][t]], [fed[layer][t]["grad"] for t in kinds]
        most, half = 3 * hidden // 4, hidden // 2
        queue(layer, [("down", *down, 0, most)])
        queue(layer, [("down", *down, most, hidden - most), ("up", *up, 0, half)])

    def queue_attend(layer):
        state = kept[layer]
        up = [v for t in kinds for v in state["middle"][t]], [fed[layer][t]["grad"] for t in kinds]
        mix = [v for t in kinds for v in slots_one[layer][t]], [state["attended"][t]["ctx"] for t in kinds]
        proj = [v for t in kinds for v in state["x"][t]], [went[layer][t]["grad"] for t in kinds]
        half = hidden // 2
        queue(layer, [("up", *up, half, half), ("mix", *mix, 0, span)])
        queue(layer, [("proj", *proj, 0, 3 * span)], None if layer > 0 else little_rows)

    def fill(count):
        for _ in range(count):
            if fillers:
                fillers.pop(0)()

    norm_sums = []

    def sum_norms():
        found = sum_norm_rows(
            order, [[back[layer][s][1] for s in kinds] for layer in range(LAYERS) for back in (back_one, back_two)]
        )
        norm_sums.extend([found, to_core(found)])

    def little_rows():
        return little_gradients(
            order,
            norm_sums,
            [[fed[layer][s]["sums"] for s in kinds] for layer in range(LAYERS)],
            [[went[layer][s]["sums"] for s in kinds] for layer in range(LAYERS)],
            span,
        )

    items = []
    for layer in range(LAYERS):
        items += [attend(layer, s) for s in kinds] + [feed(layer, s) for s in kinds]
    forward_items = len(items)
    for layer in reversed(range(LAYERS)):
        items += [feed_back(layer, s) for s in kinds] + [attend_back(layer, s) for s in kinds]
    items[0][0]()
    for at, (_, products) in enumerate(items):
        s = at % streams
        found, more = products()
        beside = [to_core(part) for part in found["other"]]
        if at >= forward_items:
            fill(FILLS[at - forward_items])
            for _ in range(STEPS[at - forward_items]):
                pipeline.step()
        early = ADD_FIRST[at]
        if early:
            low = add_send(order, found["own"], beside)
        order.pin(ahead(at + 1))
        if at == 0:
            fetch(order, weights[0][3:])
            shares = deal_share(order, cotangents)
        if at + 1 < len(items):
            items[at + 1][0]()
        if at == forward_items + 1:
            out_rows = gather_halves([jnp.concatenate([v for t in kinds for v in kept[-1]["two"][t][0]], 0)])
        if at + 2 == len(items):
            sum_norms()
        if not early:
            low = add_send(order, found["own"], beside)
        terms[s] = [found["own"], *beside, to_chip(low), *more]
        for _ in range(MORE_STEPS[at - forward_items] if at >= forward_items else 0):
            pipeline.step()
    while fillers:
        fill(2)
        pipeline.step(True)
    layer_out = natural_share(order, out_rows, BF)
    pipeline.step(True)
    ends = [last_sum(order, terms[s]) for s in kinds]
    end_rows = gather_halves([jnp.concatenate(ends, 0)])
    pipeline.step(True)
    input_grad = natural_share(order, end_rows, F32)
    pipeline.drain()

    little = outputs["little"]
    grad_gains = little[: 2 * LAYERS, :width].reshape(LAYERS, 2, width)
    grad_biases = little[2 * LAYERS : 6 * LAYERS, :width].reshape(LAYERS, 4, width)
    rest = little[6 * LAYERS : 8 * LAYERS].reshape(LAYERS, -1)
    here = lax.axis_index(FSDP)
    grow = rest[:, :hidden].reshape(bias_grow.shape)
    heads = rest[:, hidden : hidden + 2 * span].reshape(bias_heads.shape)
    part = grow.shape[-1] // size
    grow = lax.dynamic_slice_in_dim(grow, here * part, part, grow.ndim - 1)
    part = heads.shape[-1] // size
    heads = lax.dynamic_slice_in_dim(heads, here * part, part, heads.ndim - 1)
    return (
        layer_out,
        input_grad,
        outputs["proj"],
        outputs["mix"],
        outputs["up"],
        outputs["down"],
        heads,
        grow,
        grad_gains,
        grad_biases,
    )


def solution(mesh):
    in_specs = (
        P((DP, FSDP), None),
        P((DP, FSDP, TENSOR), None),
        P((DP, FSDP)),
        P(None, None, FSDP, TENSOR),
        P(None, TENSOR, FSDP),
        P(None, FSDP, TENSOR),
        P(None, TENSOR, FSDP),
        P(None, None, TENSOR, FSDP),
        P(None, TENSOR, FSDP),
        P(None, None, FSDP),
        P(None, None, FSDP),
    )
    out_specs = (
        P((DP, FSDP, TENSOR), None),
        P((DP, FSDP, TENSOR), None),
        P(None, None, FSDP, TENSOR),
        P(None, TENSOR, FSDP),
        P(None, FSDP, TENSOR),
        P(None, TENSOR, FSDP),
        P(None, None, TENSOR, FSDP),
        P(None, TENSOR, FSDP),
        P(None, None, FSDP),
        P(None, None, FSDP),
    )
    return jax.shard_map(
        per_device, mesh=mesh, in_specs=in_specs, out_specs=out_specs, check_vma=False
    )
```

```python
import functools

import jax
import jax.numpy as jnp
from jax import lax
from jax.experimental import pallas as pl
from jax.experimental.pallas import tpu as pltpu
from jax.sharding import PartitionSpec as P

HEAD = 64
PAIR = 2 * HEAD
LAYERS = 2
LENGTHS = (512, 256, 128, 128, 128)
STARTS = (0, 512, 768, 896, 1024)
STREAMS = ((0,), (1, 2, 3, 4))
CUT = 2
HALVES = 2
BF = jnp.bfloat16
DP, FSDP, TENSOR = "dp", "fsdp", "tensor"
F32 = jnp.float32
MIB = 1 << 20
CORE_SWAP = [(0, 1), (1, 0), (2, 3), (3, 2)]
CHIP_SWAP = [(0, 2), (2, 0), (1, 3), (3, 1)]


def to_core(value):
    return lax.ppermute(value, TENSOR, CORE_SWAP)


def to_chip(value):
    return lax.ppermute(value, TENSOR, CHIP_SWAP)


def from_fsdp(value, step):
    size = lax.axis_size(FSDP)
    return lax.ppermute(value, FSDP, [((i + step) % size, i) for i in range(size)])


def to_fsdp(value, step):
    size = lax.axis_size(FSDP)
    return lax.ppermute(value, FSDP, [(i, (i + step) % size) for i in range(size)])


def own_first(whole, axis):
    size = lax.axis_size(FSDP)
    here = lax.axis_index(FSDP)
    width = whole.shape[axis] // size
    return jnp.concatenate(
        [lax.dynamic_slice_in_dim(whole, (here + k) % size * width, width, axis) for k in range(size)], axis
    )


def natural(relative, axis):
    size = lax.axis_size(FSDP)
    here = lax.axis_index(FSDP)
    width = relative.shape[axis] // size
    return jnp.concatenate(
        [
            lax.dynamic_slice_in_dim(relative, (k - here + size) % size * width, width, axis)
            for k in range(size)
        ],
        axis,
    )


def dot(left, right):
    return jnp.dot(left, right, preferred_element_type=F32)


def dot_t(left, right):
    return lax.dot_general(left, right, (((1,), (1,)), ((), ())), preferred_element_type=F32)


def dot_rows(left, right):
    return lax.dot_general(left, right, (((0,), (0,)), ((), ())), preferred_element_type=F32)


def share_rows(stream):
    return sum(LENGTHS[page] for page in stream) // HALVES


def page_places(stream):
    places, at = [], 0
    for page in stream:
        places.append((page, LENGTHS[page], at, at // HALVES))
        at += LENGTHS[page]
    return places


SCOPED = 8


class Order:
    def __init__(self):
        self.last = None
        self.pins = []

    def pin(self, arrays):
        self.pins.extend(v for v in arrays)

    def call(
        self,
        body,
        inputs,
        outputs,
        scratch=(),
        grid=(),
        in_specs=None,
        out_specs=None,
        name=None,
        limit=SCOPED,
        alias=None,
    ):
        pins, self.pins = self.pins, []
        count = len(inputs)
        in_specs = in_specs or [None] * count
        out_specs = out_specs or [None] * len(outputs)
        in_specs = [whole_of(v.shape, grid) if s is None else s for s, v in zip(in_specs, inputs)]
        out_specs = [whole_of(v.shape, grid) if s is None else s for s, v in zip(out_specs, outputs)]
        token = shape_of((8, 128), F32)
        inputs = list(inputs) + pins + ([] if self.last is None else [self.last])
        in_specs += [ANY] * (len(inputs) - count)
        extra = len(inputs) - count

        def kernel(*refs):
            given, refs = refs[:count], refs[count + extra :]
            outs, mark, own = refs[: len(outputs)], refs[len(outputs)], refs[len(outputs) + 1 :]
            mark[...] = jnp.zeros(mark.shape, F32)
            body(*given, *outs, *own)

        *result, self.last = pl.pallas_call(
            kernel,
            grid=grid,
            in_specs=in_specs,
            out_specs=[*out_specs, whole_of(token.shape, grid)],
            out_shape=[*outputs, token],
            scratch_shapes=list(scratch),
            input_output_aliases=alias or {},
            name=name,
            cost_estimate=pl.CostEstimate(flops=0, bytes_accessed=0, transcendentals=0),
            compiler_params=pltpu.CompilerParams(vmem_limit_bytes=limit * MIB),
        )(*inputs)
        return result


def whole_of(shape, grid):
    if not grid:
        return pl.BlockSpec(memory_space=pltpu.VMEM)
    return pl.BlockSpec(shape, lambda *at: (0,) * len(shape))


def shape_of(shape, dtype):
    return jax.ShapeDtypeStruct(tuple(shape), dtype)


SMEM = pl.BlockSpec(memory_space=pltpu.SMEM)
ANY = pl.BlockSpec(memory_space=pl.ANY)
HELD = pl.BlockSpec(memory_space=pltpu.HBM)


def core_index():
    return lax.rem(lax.axis_index(TENSOR), 2)


class Weight:
    def __init__(self, order, whole, layer, axis, direct=False):
        self.order, self.whole, self.layer, self.axis = order, whole, layer, axis
        self.size = lax.axis_size(FSDP)
        shape = whole.shape[1:]
        width = shape[axis]
        self.halved = not direct and self.size == 2 and lax.axis_size(DP) % 2 == 0 and width % 256 == 0
        self.widths = [width] + ([width // 2] * 2 if self.halved else [width] * (self.size - 1))
        self.shape = shape

    def places(self):
        width = self.widths[0]
        if not self.halved:
            return [pl.ds(k * width, width) for k in range(self.size)]
        parity = lax.rem(lax.axis_index(DP), 2)
        half = width // 2
        return [
            pl.ds(0, width),
            pl.ds(pl.multiple_of(width + parity * half, 128), half),
            pl.ds(pl.multiple_of(width + (1 - parity) * half, 128), half),
        ]

    def start(self, own, half):
        if self.halved:
            self.early = [from_fsdp(half, 1)]
            size = lax.axis_size(DP)
            self.late = [lax.ppermute(self.early[0], DP, [(i, i ^ 1) for i in range(size)])]
        else:
            self.early = [from_fsdp(own, step) for step in range(1, self.size)]
            self.late = []
        self.arrays = [own, *self.early, *self.late]

    def specs(self):
        return [None] * len(self.arrays)

    def take(self, refs):
        count = len(self.arrays)
        return list(zip(refs[:count], self.places())), refs[count:]


def fetch(order, weights):
    outputs = []
    for w in weights:
        outputs.append(shape_of(w.shape, BF))
        if w.halved:
            shape = list(w.shape)
            shape[w.axis] //= 2
            outputs.append(shape_of(shape, BF))

    def body(*refs):
        outs, sems = list(refs[len(weights) : -1]), refs[-1]
        parity = lax.rem(lax.axis_index(DP), 2)
        copies = []
        for w, ref in zip(weights, refs):
            sources = [ref.at[w.layer]]
            if w.halved:
                half = w.widths[1]
                place = [slice(None)] * len(w.shape)
                place[w.axis] = pl.ds(pl.multiple_of(parity * half, 128), half)
                sources.append(ref.at[(w.layer, *place)])
            for source in sources:
                copy = pltpu.make_async_copy(source, outs.pop(0), sems.at[len(copies)])
                copy.start()
                copies.append(copy)
        for copy in copies:
            copy.wait()

    found = order.call(
        body,
        [w.whole for w in weights],
        outputs,
        scratch=[pltpu.SemaphoreType.DMA((len(outputs),))],
        in_specs=[HELD] * len(weights),
        name="fetch",
    )
    for w in weights:
        own = found.pop(0)
        w.start(own, found.pop(0) if w.halved else None)


def deal_rows(order, activations):
    features = activations.shape[1]
    size = lax.axis_size(FSDP)
    width = features // size

    def body(whole, *outs):
        here = core_index()
        mine = lax.axis_index(FSDP)
        for at, stream in enumerate(STREAMS):
            for slot in range(HALVES):
                out = outs[at * HALVES + slot]
                for page, length, _, offset in page_places(stream):
                    part = length // HALVES
                    row = pl.multiple_of(STARTS[page] + (here ^ slot) * part, 32)
                    for k in range(size):
                        column = pl.multiple_of(lax.rem(mine + k, size) * width, 128)
                        out[offset : offset + part, k * width : (k + 1) * width] = whole[
                            pl.ds(row, part), pl.ds(column, width)
                        ]

    outs = order.call(
        body,
        [activations],
        [shape_of((share_rows(stream), features), BF) for stream in STREAMS for _ in range(HALVES)],
        name="deal_rows",
    )
    return [outs[at * HALVES : (at + 1) * HALVES] for at in range(len(STREAMS))]


def copy_rows(order, rows):
    def body(a, out):
        out[...] = a[...]

    return order.call(body, [rows], [shape_of(rows.shape, rows.dtype)], name="copy_rows")[0]


def deal_share(order, slots):
    rows, features = slots[0].shape
    size = lax.axis_size(FSDP)
    width = features // size

    def body(a, b, c, d, *outs):
        whole = outs[-1]
        here = lax.axis_index(TENSOR)
        core = core_index()
        mine = lax.axis_index(FSDP)
        for slot, ref in enumerate((a, b, c, d)):
            whole[pl.ds(pl.multiple_of((here ^ slot) * rows, 32), rows), :] = ref[...]
        for at, stream in enumerate(STREAMS):
            for page, length, _, offset in page_places(stream):
                part = length // HALVES
                row = pl.multiple_of(STARTS[page] + core * part, 32)
                for k in range(size):
                    column = pl.multiple_of(lax.rem(mine + k, size) * width, 128)
                    outs[at][offset : offset + part, k * width : (k + 1) * width] = whole[
                        pl.ds(row, part), pl.ds(column, width)
                    ]

    return order.call(
        body,
        slots,
        [shape_of((share_rows(stream), features), BF) for stream in STREAMS],
        scratch=[pltpu.VMEM((rows * 4, features), BF)],
        name="deal_share",
    )


def natural_share(order, slots, dtype):
    rows, features = slots[0].shape
    share = rows // 2
    size = lax.axis_size(FSDP)
    width = features // size

    def body(a, b, out, whole):
        here = lax.axis_index(TENSOR)
        core = core_index()
        mine = lax.axis_index(FSDP)
        for slot, ref in enumerate((a, b)):
            first = 0
            for stream in STREAMS:
                for page, length, _, offset in page_places(stream):
                    part = length // HALVES
                    row = pl.multiple_of(STARTS[page] + (core ^ slot) * part, 32)
                    whole[pl.ds(row, part), :] = ref[first + offset : first + offset + part, :]
                first += share_rows(stream)
        own = pl.multiple_of(here * share, 32)
        for k in range(size):
            column = pl.multiple_of(lax.rem(mine + k, size) * width, 128)
            out[:, pl.ds(column, width)] = whole[pl.ds(own, share), k * width : (k + 1) * width].astype(dtype)

    return order.call(
        body,
        slots,
        [shape_of((share, features), dtype)],
        scratch=[pltpu.VMEM((rows * 2, features), BF)],
        name="natural_share",
    )[0]


def add_send(order, kept, came):
    def body(a, *refs):
        low, at = refs[-1], 0
        for ref in refs[:-1]:
            rows = slice(at, at + ref.shape[0])
            low[rows, :] = (a[rows, :].astype(F32) + ref[...].astype(F32)).astype(BF)
            at += ref.shape[0]

    return order.call(body, [kept, *came], [shape_of(kept.shape, BF)], name="add_send")[0]


def sum_terms(own, *refs):
    *pieces, across = refs
    beside = jnp.concatenate([ref[...] for ref in pieces], 0)
    return own[...].astype(F32) + beside.astype(F32) + across[...].astype(F32)


def row_of(ref, at):
    return ref[at : at + 1, :]


def norm_forward(order, terms, residual, vectors, rows_of_vectors):
    rows, features = terms[0].shape
    bias_at, gain_at, shift_at = rows_of_vectors

    def body(*refs):
        parts, (before, vec, *lows, normed, inverse, kept) = refs[: len(terms)], refs[len(terms) :]
        value = before[...].astype(F32)
        if residual[1] is not None:
            value = value * row_of(vec, residual[1]) + row_of(vec, residual[2])
        value = value + sum_terms(*parts) + row_of(vec, bias_at)
        center = value - jnp.mean(value, -1, keepdims=True)
        scale = lax.rsqrt(jnp.mean(center * center, -1, keepdims=True) + 1e-05)
        unit = center * scale
        normed[...] = unit
        kept[...] = unit.astype(BF)
        inverse[...] = scale
        split_rows(lows, slice(None), unit * row_of(vec, gain_at) + row_of(vec, shift_at))

    outs = order.call(
        body,
        [*terms, residual[0], vectors],
        [
            *[shape_of((rows // CUT, features), BF)] * CUT,
            shape_of((rows, features), F32),
            shape_of((rows, 1), F32),
            shape_of((rows, features), BF),
        ],
        name="norm_forward",
    )
    return [outs[:CUT], *outs[CUT:]]


def norm_backward(order, terms, normed, inverse, vectors, gain_at):
    rows, features = normed.shape
    count = len(terms)

    def body(*refs):
        unit, scale, vec, *lows, sums, wide = refs[count:]
        total = refs[count - 1][...].astype(F32)
        if count > 1:
            total = total + sum_terms(*refs[: count - 1])
        n = unit[...].astype(F32)
        grad = total * row_of(vec, gain_at)
        mean_one = jnp.mean(grad, -1, keepdims=True)
        mean_two = jnp.mean(grad * n, -1, keepdims=True)
        result = scale[...] * (grad - mean_one - n * mean_two)
        wide[...] = result
        split_rows(lows, slice(None), result)
        sums[0:1, :] = jnp.sum(total * n, 0, keepdims=True)
        sums[1:2, :] = jnp.sum(total, 0, keepdims=True)
        sums[2:3, :] = jnp.sum(result, 0, keepdims=True)

    outs = order.call(
        body,
        [*terms, normed, inverse, vectors],
        [
            *[shape_of((rows // CUT, features), BF)] * CUT,
            shape_of((3, features), F32),
            shape_of((rows, features), F32),
        ],
        name="norm_backward",
    )
    return [outs[:CUT], *outs[CUT:]]


def last_sum(order, terms):
    def body(*refs):
        refs[-1][...] = (refs[-2][...] + sum_terms(*refs[:-2])).astype(BF)

    return order.call(body, terms, [shape_of(terms[0].shape, BF)], name="last_sum")[0]


def head_mask(which):
    lane = lax.broadcasted_iota(jnp.int32, (1, PAIR), 1)
    return (lane < HEAD) if which == 0 else (lane >= HEAD)


def key_bias(length, limit):
    part = length // HALVES
    place = lax.broadcasted_iota(jnp.int32, (1, length), 1)
    half = (place // part) ^ core_index()
    return jnp.where(half * part + place % part < limit, 0.0, -1000000000.0).astype(F32)


def put_rows(ref, lanes, value, row, part, share, offset):
    done = 0
    while done < value.shape[0]:
        at = row + done
        count = min(part - at % part, value.shape[0] - done)
        first = (at // part) * share + offset + at % part
        ref[first : first + count, lanes] = value[done : done + count]
        done += count


def attention_forward(order, stream, slots, weights, lengths):
    w_proj, w_mix, bias_rows = weights
    share, features = slots_shape(slots)
    span = w_mix.shape[0]
    heads = span // HEAD
    places = page_places(stream)

    def body(*refs):
        xs, refs = refs[: len(slots)], refs[len(slots) :]
        wp, refs = w_proj.take(refs)
        wm, refs = w_mix.take(refs)
        bias, limits, refs = refs[0], refs[1], refs[2:]
        others, (part_own, qkv, ctx), probs = refs[:CUT], refs[CUT : CUT + 3], refs[CUT + 3 :]
        for kind in range(3):
            value = None
            for w, at in wp:
                rows = jnp.concatenate([x[:, at] for x in xs], 0)
                term = dot(rows, w[kind])
                value = term if value is None else value + term
            if kind == 0:
                value = value + bias[0:1, :]
            elif kind == 2:
                value = value + bias[1:2, :]
            value = value.astype(BF)
            if kind == 0:
                value = value * jnp.asarray(HEAD ** (-0.5), BF)
            for _, length, base, offset in places:
                part = length // HALVES
                for slot in range(HALVES):
                    qkv[base + slot * part : base + (slot + 1) * part, kind * span : (kind + 1) * span] = value[
                        slot * share + offset : slot * share + offset + part, :
                    ]
        for index, (page, length, base, offset) in enumerate(places):
            part = length // HALVES
            shut = key_bias(length, limits[page])
            step = min(length, 256)
            for pair in range(heads // 2):
                lanes = slice(pair * PAIR, (pair + 1) * PAIR)
                keys = qkv[base : base + length, span + pair * PAIR : span + (pair + 1) * PAIR]
                values = qkv[base : base + length, 2 * span + pair * PAIR : 2 * span + (pair + 1) * PAIR]
                for row in range(0, length, step):
                    queries = qkv[base + row : base + row + step, lanes]
                    found = []
                    for which in range(2):
                        masked = queries * head_mask(which).astype(BF)
                        scores = dot_t(masked, keys) + shut
                        peak = jnp.max(scores, -1, keepdims=True)
                        raised = jnp.exp(scores - peak)
                        chance = raised * (1.0 / jnp.sum(raised, -1, keepdims=True))
                        chance = chance.astype(BF)
                        probs[index][2 * pair + which, row : row + step, :] = chance
                        found.append(dot(chance, values))
                    both = jnp.where(head_mask(0), found[0], found[1]).astype(BF)
                    put_rows(ctx, lanes, both, row, part, share, offset)
        for w, at in wm:
            value = dot(ctx[...], w[...])
            part_own[:, at] = value[:share].astype(BF)
            split_rows(others, at, value[share:])

    outs = order.call(
        body,
        [*slots, *w_proj.arrays, *w_mix.arrays, bias_rows, lengths],
        [
            *[shape_of((share // CUT, features), BF)] * CUT,
            shape_of((share, features), BF),
            shape_of((2 * share, 3 * span), BF),
            shape_of((2 * share, span), BF),
        ]
        + [shape_of((heads, length, length), BF) for _, length, _, _ in places],
        in_specs=[None] * len(slots) + w_proj.specs() + w_mix.specs() + [None, SMEM],
        name="attention_forward",
    )
    return {"other": outs[:CUT], "own": outs[CUT], "qkv": outs[CUT + 1], "ctx": outs[CUT + 2], "probs": outs[CUT + 3 :]}


def attention_backward(order, stream, slots, weights, state):
    w_proj, w_mix = weights
    probs, qkv = state["probs"], state["qkv"]
    share, features = slots_shape(slots)
    span = w_mix.shape[0]
    heads = span // HEAD
    places = page_places(stream)

    def body(*refs):
        ds, refs = refs[: len(slots)], refs[len(slots) :]
        wp, refs = w_proj.take(refs)
        wm, refs = w_mix.take(refs)
        chances, refs = refs[: len(places)], refs[len(places) :]
        qkv_ref, *others, part_own, grad, sums, low = refs
        value = None
        for w, at in wm:
            rows = jnp.concatenate([d[:, at] for d in ds], 0)
            term = dot_t(rows, w[...])
            value = term if value is None else value + term
        value = value.astype(BF)
        for _, length, base, offset in places:
            part = length // HALVES
            for slot in range(HALVES):
                low[base + slot * part : base + (slot + 1) * part, :] = value[
                    slot * share + offset : slot * share + offset + part, :
                ]
        for index, (page, length, base, offset) in enumerate(places):
            part = length // HALVES
            step = min(length, 256)
            for pair in range(heads // 2):
                lanes = slice(pair * PAIR, (pair + 1) * PAIR)
                keys = qkv_ref[base : base + length, span + pair * PAIR : span + (pair + 1) * PAIR]
                values = qkv_ref[base : base + length, 2 * span + pair * PAIR : 2 * span + (pair + 1) * PAIR]
                grad_keys, grad_values = [None, None], [None, None]
                for row in range(0, length, step):
                    queries = qkv_ref[base + row : base + row + step, lanes]
                    grad_rows = low[base + row : base + row + step, lanes]
                    found = []
                    for which in range(2):
                        chance = chances[index][2 * pair + which, row : row + step, :]
                        wide = chance.astype(F32)
                        back = dot_t(grad_rows * head_mask(which).astype(BF), values)
                        inner = jnp.sum(wide * back, -1, keepdims=True)
                        grad_scores = (wide * (back - inner)).astype(BF)
                        found.append(dot(grad_scores, keys))
                        of_keys = dot_rows(grad_scores, queries)
                        of_values = dot_rows(chance, grad_rows)
                        first = grad_keys[which] is None
                        grad_keys[which] = of_keys if first else grad_keys[which] + of_keys
                        grad_values[which] = of_values if first else grad_values[which] + of_values
                    both = (jnp.where(head_mask(0), found[0], found[1]) * HEAD ** (-0.5)).astype(BF)
                    put_rows(grad, lanes, both, row, part, share, offset)
                for kind, parts in ((1, grad_keys), (2, grad_values)):
                    both = jnp.where(head_mask(0), parts[0], parts[1]).astype(BF)
                    for slot in range(HALVES):
                        grad[
                            slot * share + offset : slot * share + offset + part,
                            kind * span + pair * PAIR : kind * span + (pair + 1) * PAIR,
                        ] = both[slot * part : (slot + 1) * part, :]
        for w, at in wp:
            value = None
            for kind in range(3):
                term = dot_t(grad[:, kind * span : (kind + 1) * span], w[kind])
                value = term if value is None else value + term
            part_own[:, at] = value[:share].astype(BF)
            split_rows(others, at, value[share:])
        sums[...] = jnp.sum(grad[...].astype(F32), 0, keepdims=True)

    outs = order.call(
        body,
        [*slots, *w_proj.arrays, *w_mix.arrays, *probs, qkv],
        [
            *[shape_of((share // CUT, features), BF)] * CUT,
            shape_of((share, features), BF),
            shape_of((2 * share, 3 * span), BF),
            shape_of((1, 3 * span), F32),
        ],
        scratch=[pltpu.VMEM((2 * share, span), BF)],
        in_specs=[None] * len(slots) + w_proj.specs() + w_mix.specs() + [None] * (len(places) + 1),
        name="attention_backward",
    )
    return {"other": outs[:CUT], "own": outs[CUT], "grad": outs[CUT + 1], "sums": outs[CUT + 2]}


def slots_shape(slots):
    return sum(v.shape[0] for v in slots) // 2, slots[0].shape[1]


def split_rows(refs, at, value):
    count = value.shape[0] // CUT
    for i, ref in enumerate(refs):
        ref[:, at] = value[i * count : (i + 1) * count].astype(BF)


def leave_terms(low, weight, product, share, others, part_own):
    for w, at in weight:
        done = product(low, w[...])
        part_own[:, at] = done[:share, :].astype(BF)
        split_rows(others, at, done[share:, :])


def feed_forward(order, slots, weights):
    w_grow, w_shrink, bias = weights
    share, features = slots_shape(slots)
    hidden = w_shrink.shape[0]

    def body(*refs):
        xs, refs = refs[: len(slots)], refs[len(slots) :]
        wg, refs = w_grow.take(refs)
        ws, refs = w_shrink.take(refs)
        b, *others, act, slope, part_own = refs
        value = None
        for w, at in wg:
            rows = jnp.concatenate([x[:, at] for x in xs], 0)
            term = dot(rows, w[...])
            value = term if value is None else value + term
        up = value + b[...]
        cdf = 0.5 * (1.0 + lax.erf(up * 0.7071067811865476))
        density = jnp.exp(-0.5 * up * up) * 0.3989422804014327
        low = (up * cdf).astype(BF)
        act[...] = low
        slope[...] = (cdf + up * density).astype(BF)
        leave_terms(low, ws, dot, share, others, part_own)

    outs = order.call(
        body,
        [*slots, *w_grow.arrays, *w_shrink.arrays, bias],
        [
            *[shape_of((share // CUT, features), BF)] * CUT,
            shape_of((2 * share, hidden), BF),
            shape_of((2 * share, hidden), BF),
            shape_of((share, features), BF),
        ],
        name="feed_forward",
        limit=FEED_LIMIT,
    )
    return {"other": outs[:CUT], "act": outs[CUT], "slope": outs[CUT + 1], "own": outs[CUT + 2]}


def feed_backward(order, slots, slope, weights):
    w_grow, w_shrink = weights
    share, features = slots_shape(slots)
    hidden = w_shrink.shape[0]

    def body(*refs):
        ds, refs = refs[: len(slots)], refs[len(slots) :]
        wg, refs = w_grow.take(refs)
        ws, refs = w_shrink.take(refs)
        tilt, *others, grad, sums, part_own = refs
        value = None
        for w, at in ws:
            rows = jnp.concatenate([d[:, at] for d in ds], 0)
            term = dot_t(rows, w[...])
            value = term if value is None else value + term
        low = (value * tilt[...].astype(F32)).astype(BF)
        grad[...] = low
        sums[...] = jnp.sum(low.astype(F32), 0, keepdims=True)
        leave_terms(low, wg, dot_t, share, others, part_own)

    outs = order.call(
        body,
        [*slots, *w_grow.arrays, *w_shrink.arrays, slope],
        [
            *[shape_of((share // CUT, features), BF)] * CUT,
            shape_of((2 * share, hidden), BF),
            shape_of((1, hidden), F32),
            shape_of((share, features), BF),
        ],
        name="feed_backward",
        limit=FEED_LIMIT,
    )
    return {"other": outs[:CUT], "grad": outs[CUT], "sums": outs[CUT + 1], "own": outs[CUT + 2]}


def weight_grad(order, pairs, part, parts, extra=None):
    features = pairs[0][0][0].shape[1]
    width = features // parts
    start, shards = (0, 1) if part == 0 else (1, parts - 1)
    flat, specs, total = [], [], 0
    for left, right, first, count in pairs:
        flat += [*left, *right]
        specs += [pl.BlockSpec((v.shape[0], width), lambda i: (0, start + i)) for v in left]
        specs += [pl.BlockSpec((v.shape[0], count), lambda i, at=first // count: (0, at)) for v in right]
        total += count
    more = 0 if extra is None else extra.shape[1]
    if more:
        flat.append(extra)
        specs.append(pl.BlockSpec((1, *extra.shape[1:]), lambda i: (start + i, 0, 0)))

    def body(*refs):
        out, at, column = refs[-1], 0, 0
        if more:
            out[0, width:, :] = refs[len(flat) - 1][0].astype(BF)
        for left, right, _, count in pairs:
            a = jnp.concatenate([r[...] for r in refs[at : at + len(left)]], 0)
            at += len(left)
            b = jnp.concatenate([r[...] for r in refs[at : at + len(right)]], 0)
            at += len(right)
            out[0, :width, column : column + count] = dot_rows(a, b).astype(BF)
            column += count

    return order.call(
        body,
        flat,
        [shape_of((shards, width + more, total), BF)],
        grid=(shards,),
        in_specs=specs,
        out_specs=[pl.BlockSpec((1, width + more, total), lambda i: (i, 0, 0))],
        name="weight_grad",
        limit=GRAD_LIMIT,
    )[0]


class Pipeline:
    def __init__(self, order):
        self.order = order
        self.line = lax.axis_size(DP) == 4
        self.waiting, self.pieces, self.at = [], [], 0

    def offer(self, others, own, finish):
        self.waiting.append({"others": others, "own": own, "finish": finish})

    def piece(self, at):
        return self.pieces[at] if 0 <= at < len(self.pieces) else None

    def step(self, last=False):
        size = lax.axis_size(FSDP)
        now = self.at
        self.at += 1
        oldest, older, old, new = (self.piece(now - 1 - back) for back in (3, 2, 1, 0))
        if last and self.line and oldest is not None:
            oldest["finish"](oldest["total"], oldest["back"])
            oldest = None
        sums = []
        if new is not None:
            sums.append(("sum", new, [new["own"], *new["came"]]))
        if self.line and old is not None:
            sums.append(("inner", old, [old["sum"], old["swapped"]]))
        if self.line and older is not None:
            sums.append(("total", older, [older["inner"], older["met"]]))
        if sums:
            send = [piece[0] for piece in sums] if self.line else []
            found = combine(self.order, [terms for *_, terms in sums], send)
            for (name, piece, _), value in zip(sums, found):
                piece[name] = value
        if not self.line and new is not None:
            total = lax.psum(new["sum"], DP)
            new["finish"](total, total)
        elif self.line:
            if old is not None:
                old["met"] = lax.ppermute(old["inner"], DP, [(1, 2), (2, 1)])
            if new is not None and older is not None:
                new["swapped"] = older["back"] = lax.ppermute(found[-1], DP, [(0, 1), (1, 0), (2, 3), (3, 2)])
            elif new is not None:
                new["swapped"] = lax.ppermute(new["sum"], DP, [(0, 1), (3, 2)])
            elif older is not None:
                older["back"] = lax.ppermute(older["total"], DP, [(1, 0), (2, 3)])
        if self.waiting:
            piece = self.waiting.pop(0)
            piece["came"] = [to_fsdp(piece["others"][k], k + 1) for k in range(size - 1)]
            self.pieces.append(piece)
        else:
            self.pieces.append(None)
        if self.line and oldest is not None:
            oldest["finish"](oldest["total"], oldest["back"])

    def drain(self):
        while self.waiting or any(p is not None for p in self.pieces[max(self.at - 4, 0) :]):
            self.step(True)


def at_end():
    here = lax.axis_index(DP)
    return (here == 0) | (here == lax.axis_size(DP) - 1)


def combine(order, groups, names):
    width = groups[0][0].shape[1]
    rows = [terms[0].shape[0] for terms in groups]
    both = "sum" in names and "total" in names
    given = [v for terms in groups for v in terms]
    outputs = [shape_of((count, width), BF) for count in rows]
    if both:
        ends, inside = names.index("sum"), names.index("total")
        outputs.append(shape_of((max(rows[ends], rows[inside]), width), BF))

    def body(*refs):
        at, sums = 0, []
        for index, (terms, count) in enumerate(zip(groups, rows)):
            total = refs[at][...].astype(F32)
            for ref in refs[at + 1 : at + len(terms)]:
                total = total + ref[:count, :].astype(F32)
            at += len(terms)
            sums.append(total)
            refs[len(given) + index][...] = total.astype(BF)
        if both:
            a, b, send = sums[ends], sums[inside], refs[-1]
            short = min(rows[ends], rows[inside])
            send[:short, :] = jnp.where(at_end(), a[:short], b[:short]).astype(BF)
            if send.shape[0] > short:
                send[short:, :] = (a if rows[ends] > short else b)[short:].astype(BF)

    return order.call(body, given, outputs, name="combine")


def finish_piece(order, total, back, layer, rows, held, parts, name):
    more = total.shape[0] - rows
    width = total.shape[1]
    given = [v for v in held if v is not None]
    both = [total, back]
    scratch = []
    for shape, form, _, _, count in parts:
        if form == "kinds":
            scratch.append(pltpu.VMEM((shape[1], rows, count // shape[1]), F32))
        else:
            scratch.append(pltpu.VMEM((rows, count) if form == "columns" else (count, rows), F32))

    def body(*refs):
        outs = refs[len(both) + len(given) : len(both) + len(given) + len(parts)]
        rest = refs[len(both) + len(given) + len(parts) :]
        if more:
            extra, rest = rest[0], rest[1:]
        blocks, sems = rest[:-1], rest[-1]
        value = jnp.where(at_end(), refs[1][: total.shape[0], :].astype(F32), refs[0][...].astype(F32))
        if more:
            extra[...] = value[rows:]
            value = value[:rows]
        copies = []
        for at, (out, block, (shape, form, place, first, count)) in enumerate(zip(outs, blocks, parts)):
            if form == "kinds":
                span = count // shape[1]
                for g in range(shape[1]):
                    block[g] = value[:, first + g * span : first + (g + 1) * span]
                there = out.at[layer]
            elif form == "turned":
                block[...] = value[:, first : first + count].T
                there = out.at[layer, pl.ds(place, count), :]
            else:
                block[...] = value[:, first : first + count]
                there = out.at[layer, :, pl.ds(place, count)]
            copy = pltpu.make_async_copy(block, there, sems.at[at])
            copy.start()
            copies.append(copy)
        for copy in copies:
            copy.wait()

    alias, at = {}, 0
    for index, v in enumerate(held):
        if v is not None:
            alias[len(both) + at] = index
            at += 1
    return order.call(
        body,
        [*both, *given],
        [shape_of(shape, F32) for shape, *_ in parts] + ([shape_of((more, width), F32)] if more else []),
        scratch=[*scratch, pltpu.SemaphoreType.DMA((len(parts),))],
        in_specs=[None] * len(both) + [HELD] * len(given),
        out_specs=[HELD] * len(parts) + ([None] if more else []),
        alias=alias,
        name=name,
        limit=12,
    )


def sum_norm_rows(order, sums):
    streams = len(sums[0])
    features = sums[0][0].shape[1]

    def body(*refs):
        out = refs[-1]
        found = []
        for at in range(len(sums)):
            total = refs[at * streams][...]
            for ref in refs[at * streams + 1 : (at + 1) * streams]:
                total = total + ref[...]
            found.append(total)
        rows = [found[at][0:1] for at in range(2 * LAYERS)]
        for layer in range(LAYERS):
            one, two = found[2 * layer], found[2 * layer + 1]
            rows += [one[2:3], two[2:3], one[1:2], two[1:2]]
        for at, row in enumerate(rows):
            out[at : at + 1, :] = row

    return order.call(
        body,
        [v for group in sums for v in group],
        [shape_of((6 * LAYERS, features), F32)],
        name="sum_norm_rows",
    )[0]


def little_gradients(order, norms, grow, heads, span):
    size = lax.axis_size(FSDP)
    features = norms[0].shape[1]
    width = features // size
    columns = 3 * span
    hidden = grow[0][0].shape[1]
    streams = len(grow[0])

    def body(a, b, *refs):
        out = refs[-1]
        out[...] = jnp.zeros(out.shape, F32)
        total = a[...] + b[...]
        rows = 6 * LAYERS
        for k in range(size):
            out[k, :rows, :width] = total[:, k * width : (k + 1) * width]
        for layer in range(LAYERS):
            at = layer * streams
            up = sum(ref[...] for ref in refs[at : at + streams])
            at += LAYERS * streams
            qkv = sum(ref[...] for ref in refs[at : at + streams])
            for k in range(size):
                row = rows + 2 * layer
                rest = hidden - columns
                out[k, row : row + 1, :] = up[:, :columns]
                out[k, row + 1 : row + 2, :rest] = up[:, columns:]
                out[k, row + 1 : row + 2, rest : rest + span] = qkv[:, :span]
                out[k, row + 1 : row + 2, rest + span : rest + 2 * span] = qkv[:, 2 * span :]

    return order.call(
        body,
        [*norms, *[v for group in grow for v in group], *[v for group in heads for v in group]],
        [shape_of((size, 8 * LAYERS, columns), F32)],
        name="little_gradients",
    )[0]


FILLS = (0, 2, 2, 2, 2, 2, 2, 2)
STEPS = (0, 1, 1, 1, 1, 1, 1, 1)
MORE_STEPS = (0, 0, 0, 0, 0, 0, 0, 0)
GRAD_LIMIT = 12
ADD_FIRST = (1,) * 16
FEED_LIMIT = 12


def gather_halves(pieces):
    return [*pieces, *[to_core(piece) for piece in pieces]]


def per_device(
    activations, cotangent, lengths, w_qkv, w_out, w_up, w_down, b_qv, b_up, norm_gains, layer_biases
):
    size = lax.axis_size(FSDP)
    order = Order()
    kinds = range(len(STREAMS))

    smalls = (b_qv, b_up, norm_gains, layer_biases)
    flat = jnp.concatenate([value.reshape(-1) for value in smalls])
    pieces = [flat] + [from_fsdp(flat, step) for step in range(1, size)]

    def unpack(at):
        found, start = [], 0
        for value in smalls:
            found.append(pieces[at][start : start + value.size].reshape(value.shape))
            start += value.size
        return found

    unpacked = [unpack(at) for at in range(size)]
    bias_heads, bias_grow, gains, biases = (
        jnp.concatenate([u[i] for u in unpacked], -1).astype(F32) for i in range(4)
    )
    bias_heads, bias_grow = natural(bias_heads, 3), natural(bias_grow, 2)
    features = gains.shape[-1]
    vectors = jnp.concatenate([gains.reshape(-1, features), biases.reshape(-1, features)], 0)
    head_rows = [bias_heads[layer].reshape(2, -1) for layer in range(LAYERS)]
    grow_rows = [bias_grow[layer].reshape(1, -1) for layer in range(LAYERS)]

    weights = [
        [
            Weight(order, w_qkv, layer, 1),
            Weight(order, w_out, layer, 1, layer > 0),
            Weight(order, w_up, layer, 0),
            Weight(order, w_down, layer, 1),
        ]
        for layer in range(LAYERS)
    ]
    fetch(order, weights[0][:2])

    slots = deal_rows(order, activations)
    order.pin([*weights[0][0].early, *weights[0][1].early])
    fetch(order, weights[1])
    residual = [(slots[s][0], None, None) for s in kinds]
    cotangent = copy_rows(order, cotangent)
    across = to_chip(cotangent)
    cotangents = [cotangent, to_core(cotangent), across, to_core(across)]

    order.pin([*weights[0][0].early, *weights[0][0].late, *weights[0][1].early, *weights[0][1].late])
    fetch(order, weights[0][2:3])

    def ahead(at):
        zero, one = weights
        waits = {
            1: lambda: zero[2].early,
            2: lambda: [*zero[3].early, *zero[2].late, *one[0].early],
            3: lambda: [*one[1].early, *one[0].late],
            4: lambda: [*one[1].late, *one[2].early],
            5: lambda: [*one[2].late, *one[3].early],
            6: lambda: one[3].late,
        }
        return waits[at]() if at in waits else []

    streams = len(STREAMS)
    kept = [{k: [None] * streams for k in ("x", "attended", "grown", "one", "two", "middle")} for _ in range(LAYERS)]
    terms = [None] * streams
    back_two, slots_two, fed = ([[None] * streams for _ in range(LAYERS)] for _ in range(3))
    back_one, slots_one, went = ([[None] * streams for _ in range(LAYERS)] for _ in range(3))

    def gain_at(layer, which):
        return 2 * layer + which

    def bias_at(layer, which):
        return 2 * LAYERS + 4 * layer + which

    def second_norm(layer, s):
        one = kept[layer]["one"][s]
        kept[layer]["two"][s] = norm_forward(
            order,
            terms[s],
            (one[1], gain_at(layer, 0), bias_at(layer, 2)),
            vectors,
            (bias_at(layer, 1), gain_at(layer, 1), bias_at(layer, 3)),
        )

    def attend(layer, s):
        def before():
            if layer > 0:
                second_norm(layer - 1, s)
                two = kept[layer - 1]["two"][s]
                slots[s] = gather_halves(two[0])
                residual[s] = (two[1], gain_at(layer - 1, 1), bias_at(layer - 1, 3))
            kept[layer]["x"][s] = slots[s]

        def products():
            w_proj, w_mix = weights[layer][:2]
            found = attention_forward(order, STREAMS[s], slots[s], (w_proj, w_mix, head_rows[layer]), lengths)
            kept[layer]["attended"][s] = found
            return found, []

        return before, products

    def feed(layer, s):
        def before():
            one = norm_forward(
                order, terms[s], residual[s], vectors, (bias_at(layer, 0), gain_at(layer, 0), bias_at(layer, 2))
            )
            kept[layer]["one"][s] = one
            kept[layer]["middle"][s] = gather_halves(one[0])

        def products():
            w_grow, w_shrink = weights[layer][2:]
            found = feed_forward(order, kept[layer]["middle"][s], (w_grow, w_shrink, grow_rows[layer]))
            kept[layer]["grown"][s] = found
            return found, []

        return before, products

    def feed_back(layer, s):
        def before():
            if layer + 1 == LAYERS:
                second_norm(layer, s)
                terms[s] = [shares[s]]
            two = kept[layer]["two"][s]
            back_two[layer][s] = norm_backward(order, terms[s], two[3], two[2], vectors, gain_at(layer, 1))
            slots_two[layer][s] = gather_halves(back_two[layer][s][0])

        def products():
            w_grow, w_shrink = weights[layer][2:]
            found = feed_backward(order, slots_two[layer][s], kept[layer]["grown"][s]["slope"], (w_grow, w_shrink))
            fed[layer][s] = found
            if s + 1 == streams:
                queue_feed(layer)
            return found, [back_two[layer][s][2]]

        return before, products

    def attend_back(layer, s):
        def before():
            one = kept[layer]["one"][s]
            back_one[layer][s] = norm_backward(order, terms[s], one[3], one[2], vectors, gain_at(layer, 0))
            slots_one[layer][s] = gather_halves(back_one[layer][s][0])

        def products():
            w_proj, w_mix = weights[layer][:2]
            state = kept[layer]
            found = attention_backward(order, STREAMS[s], slots_one[layer][s], (w_proj, w_mix), state["attended"][s])
            went[layer][s] = found
            if s + 1 == streams:
                queue_attend(layer)
            return found, [back_one[layer][s][2]]

        return before, products

    pipeline = Pipeline(order)
    fillers = []
    outputs = {}
    span, hidden = w_out.shape[1], w_down.shape[1]
    width = features // size
    shapes = {
        "proj": (LAYERS, 3, width, span),
        "mix": (LAYERS, span, width),
        "up": (LAYERS, width, hidden),
        "down": (LAYERS, hidden, width),
    }
    forms = {"proj": "kinds", "mix": "turned", "up": "columns", "down": "turned"}

    def queue(layer, sources, extra=None):
        pairs = [source[1:] for source in sources]
        starts = [sum(source[4] for source in sources[:i]) for i in range(len(sources))]
        parts = [
            (shapes[name], forms[name], first, start, count)
            for (name, _, _, first, count), start in zip(sources, starts)
        ]

        def finish(total, back):
            names = [source[0] for source in sources]
            found = finish_piece(
                order, total, back, layer, width, [outputs.get(n) for n in names], parts, "finish_" + names[0]
            )
            outputs.update(zip(names, found))
            if extra is not None:
                outputs["little"] = found[-1]

        found = {}

        def others():
            found["rows"] = None if extra is None else extra()
            rows = found["rows"]
            found["others"] = weight_grad(order, pairs, 1, size, rows)

        def own():
            rows = found["rows"]
            found["own"] = weight_grad(order, pairs, 0, size, rows)[0]
            pipeline.offer(found["others"], found["own"], finish)

        fillers.extend([others, own])

    def queue_feed(layer):
        state = kept[layer]
        down = [v for t in kinds for v in slots_two[layer][t]], [state["grown"][t]["act"] for t in kinds]
        up = [v for t in kinds for v in state["middle"][t]], [fed[layer][t]["grad"] for t in kinds]
        most, half = 3 * hidden // 4, hidden // 2
        queue(layer, [("down", *down, 0, most)])
        queue(layer, [("down", *down, most, hidden - most), ("up", *up, 0, half)])

    def queue_attend(layer):
        state = kept[layer]
        up = [v for t in kinds for v in state["middle"][t]], [fed[layer][t]["grad"] for t in kinds]
        mix = [v for t in kinds for v in slots_one[layer][t]], [state["attended"][t]["ctx"] for t in kinds]
        proj = [v for t in kinds for v in state["x"][t]], [went[layer][t]["grad"] for t in kinds]
        half = hidden // 2
        queue(layer, [("up", *up, half, half), ("mix", *mix, 0, span)])
        queue(layer, [("proj", *proj, 0, 3 * span)], None if layer > 0 else little_rows)

    def fill(count):
        for _ in range(count):
            if fillers:
                fillers.pop(0)()

    norm_sums = []

    def sum_norms():
        found = sum_norm_rows(
            order, [[back[layer][s][1] for s in kinds] for layer in range(LAYERS) for back in (back_one, back_two)]
        )
        norm_sums.extend([found, to_core(found)])

    def little_rows():
        return little_gradients(
            order,
            norm_sums,
            [[fed[layer][s]["sums"] for s in kinds] for layer in range(LAYERS)],
            [[went[layer][s]["sums"] for s in kinds] for layer in range(LAYERS)],
            span,
        )

    items = []
    for layer in range(LAYERS):
        items += [attend(layer, s) for s in kinds] + [feed(layer, s) for s in kinds]
    forward_items = len(items)
    for layer in reversed(range(LAYERS)):
        items += [feed_back(layer, s) for s in kinds] + [attend_back(layer, s) for s in kinds]
    items[0][0]()
    for at, (_, products) in enumerate(items):
        s = at % streams
        found, more = products()
        beside = [to_core(part) for part in found["other"]]
        if at >= forward_items:
            fill(FILLS[at - forward_items])
            for _ in range(STEPS[at - forward_items]):
                pipeline.step()
        early = ADD_FIRST[at]
        if early:
            low = add_send(order, found["own"], beside)
        order.pin(ahead(at + 1))
        if at == 0:
            fetch(order, weights[0][3:])
            shares = deal_share(order, cotangents)
        if at + 1 < len(items):
            items[at + 1][0]()
        if at == forward_items + 1:
            out_rows = gather_halves([jnp.concatenate([v for t in kinds for v in kept[-1]["two"][t][0]], 0)])
        if at + 2 == len(items):
            sum_norms()
        if not early:
            low = add_send(order, found["own"], beside)
        terms[s] = [found["own"], *beside, to_chip(low), *more]
        for _ in range(MORE_STEPS[at - forward_items] if at >= forward_items else 0):
            pipeline.step()
    while fillers:
        fill(2)
        pipeline.step(True)
    layer_out = natural_share(order, out_rows, BF)
    pipeline.step(True)
    ends = [last_sum(order, terms[s]) for s in kinds]
    end_rows = gather_halves([jnp.concatenate(ends, 0)])
    pipeline.step(True)
    input_grad = natural_share(order, end_rows, F32)
    pipeline.drain()

    little = outputs["little"]
    grad_gains = little[: 2 * LAYERS, :width].reshape(LAYERS, 2, width)
    grad_biases = little[2 * LAYERS : 6 * LAYERS, :width].reshape(LAYERS, 4, width)
    rest = little[6 * LAYERS : 8 * LAYERS].reshape(LAYERS, -1)
    here = lax.axis_index(FSDP)
    grow = rest[:, :hidden].reshape(bias_grow.shape)
    heads = rest[:, hidden : hidden + 2 * span].reshape(bias_heads.shape)
    part = grow.shape[-1] // size
    grow = lax.dynamic_slice_in_dim(grow, here * part, part, grow.ndim - 1)
    part = heads.shape[-1] // size
    heads = lax.dynamic_slice_in_dim(heads, here * part, part, heads.ndim - 1)
    return (
        layer_out,
        input_grad,
        outputs["proj"],
        outputs["mix"],
        outputs["up"],
        outputs["down"],
        heads,
        grow,
        grad_gains,
        grad_biases,
    )


def solution(mesh):
    in_specs = (
        P((DP, FSDP), None),
        P((DP, FSDP, TENSOR), None),
        P((DP, FSDP)),
        P(None, None, FSDP, TENSOR),
        P(None, TENSOR, FSDP),
        P(None, FSDP, TENSOR),
        P(None, TENSOR, FSDP),
        P(None, None, TENSOR, FSDP),
        P(None, TENSOR, FSDP),
        P(None, None, FSDP),
        P(None, None, FSDP),
    )
    out_specs = (
        P((DP, FSDP, TENSOR), None),
        P((DP, FSDP, TENSOR), None),
        P(None, None, FSDP, TENSOR),
        P(None, TENSOR, FSDP),
        P(None, FSDP, TENSOR),
        P(None, TENSOR, FSDP),
        P(None, None, TENSOR, FSDP),
        P(None, TENSOR, FSDP),
        P(None, None, FSDP),
        P(None, None, FSDP),
    )
    return jax.shard_map(
        per_device, mesh=mesh, in_specs=in_specs, out_specs=out_specs, check_vma=False
    )
```
